32 devices in a mesh: seq: 8 (over y, x, core), wt: 4 (over z).
Axes of the slice: x: 2, y: 2, z: 4, core: 2. Of those that a mesh axis runs over, the one named last changes fastest.
Arguments:
- tokens: bfloat16 [2048, 2048], P('seq'), may hold values from -6 to 6
- cotangent: bfloat16 [2048, 2048], P('seq'), may hold values from -6 to 6
- doc_start: int32 [2048], P('seq'), may hold values from 0 to 1, as said below
- premix_gain: float32 [2048], replicated, may hold values from 0.5 to 1.5
- inner_proj: bfloat16 [2048, 4096], P('seq', 'wt'), may hold values from -0.125 to 0.125
- switch_proj: bfloat16 [2048, 4096], P('seq', 'wt'), may hold values from -0.125 to 0.125
- conv_taps: float32 [4, 4096], P(None, 'wt'), may hold values from -3 to 3
- conv_bias: float32 [4096], P('wt'), may hold values from -3 to 3
- select_proj: bfloat16 [160, 4096], P('seq', 'wt'), may hold values from -0.09375 to 0.09375
- step_proj: bfloat16 [128, 4096], P('seq', 'wt'), may hold values from -0.5 to 0.5
- step_bias: float32 [4096], P('wt'), may hold values from -6 to -2
- decay_log: float32 [16, 4096], P(None, 'wt'), may hold values from -8 to 1
- skip_gain: float32 [4096], P('wt'), may hold values from 0.5 to 1.5
- mixer_out: bfloat16 [2048, 4096], P('seq', 'wt'), may hold values from -0.09375 to 0.09375
- preffn_gain: float32 [2048], replicated, may hold values from 0.5 to 1.5
- ffn_gate: bfloat16 [2048, 8192], P('seq', 'wt'), may hold values from -0.125 to 0.125
- ffn_up: bfloat16 [2048, 8192], P('seq', 'wt'), may hold values from -0.125 to 0.125
- ffn_down: bfloat16 [2048, 8192], P('seq', 'wt'), may hold values from -0.0625 to 0.0625
Outputs:
- block_out: bfloat16 [2048, 2048], P('seq')
- tokens_grad: bfloat16 [2048, 2048], P('seq')
- premix_gain_grad: float32 [2048], replicated
- inner_proj_grad: float32 [2048, 4096], P('seq', 'wt')
- switch_proj_grad: float32 [2048, 4096], P('seq', 'wt')
- conv_taps_grad: float32 [4, 4096], P(None, 'wt')
- conv_bias_grad: float32 [4096], P('wt')
- select_proj_grad: float32 [160, 4096], P('seq', 'wt')
- step_proj_grad: float32 [128, 4096], P('seq', 'wt')
- step_bias_grad: float32 [4096], P('wt')
- decay_log_grad: float32 [16, 4096], P(None, 'wt')
- skip_gain_grad: float32 [4096], P('wt')
- mixer_out_grad: float32 [2048, 4096], P('seq', 'wt')
- preffn_gain_grad: float32 [2048], replicated
- ffn_gate_grad: float32 [2048, 8192], P('seq', 'wt')
- ffn_up_grad: float32 [2048, 8192], P('seq', 'wt')
- ffn_down_grad: float32 [2048, 8192], P('seq', 'wt')
The draws below stay inside these ranges and needn't reach their ends.
Inputs may be any that keep to these rules, and one draw needn't show every extreme that they name: `doc_start`: 1 marks the first token of a document; token 0 holds 0 and opens the first document. One document begins among the first 256/2 tokens and ends among the last 256/2, and no other begins in between.
All inputs are finite; a program needn't handle non-finite values.
Results may differ from the reference program's by a relative error of at most 0.012.
The reference program's roundings to bfloat16 on the way count: a program that leaves them out, or rounds other values in their place, can miss the bound.
Values may be sent and summed in bfloat16 or wider, within the bound.
A program may use at most 256 MiB of HBM per device.

```python
import math
import jax
import jax.numpy as jnp
from jax import lax

D = 2048
DI = 4096
NS = 16
R = 128
FF = 8192
KC = 4
TOK_DEV = 256
TOKENS = 2048


def draw_doc_start(key, part):
    key_open = jax.random.fold_in(key, 11)
    key_close = jax.random.fold_in(key, 12)
    key_coin = jax.random.fold_in(key, 13)
    opening = jax.random.randint(key_open, (), 1, max(TOK_DEV // 2, 2))
    closing = jax.random.randint(key_close, (), TOKENS - TOK_DEV // 2, TOKENS)
    places = jnp.arange(TOKENS)
    coins = jax.random.randint(key_coin, (TOKENS,), 0, 6)
    outside = ((places < opening) | (places > closing)) & (places > 0) & (coins == 0)
    marks = (places == opening) | (places == closing) | outside
    return marks.astype(jnp.int32)


def level_of(rng, dims, pieces, low, largest):
    factor_of, own = 1.0, jax.random.fold_in(rng, 6)
    for dim, parts in pieces:
        heights = jnp.exp(jax.random.uniform(jax.random.fold_in(own, dim), (parts,), jnp.float32, low / len(pieces), largest / len(pieces)))
        factor_of = factor_of * jnp.repeat(heights, dims[dim] // parts).reshape([-1 if axis == dim else 1 for axis in range(len(dims))])
    return factor_of


def scatter_about(rng, extent, deviation, bound, shards=(), kind=jnp.bfloat16):
    array = deviation * jax.random.normal(rng, extent, jnp.float32)
    if shards:
        array = array * level_of(rng, extent, shards, -0.22, 0.18)
    return jnp.clip(array, -bound, bound).astype(kind)


def setup_inputs(seed: int = 0) -> dict:
    splits = jax.random.split(jax.random.key(seed), 19)
    tokens = scatter_about(splits[0], (TOKENS, D), 1.0, 6.0, ((0, 8),))
    cotangent = scatter_about(splits[1], (TOKENS, D), 1.0, 6.0, ((0, 8),))
    doc_start = draw_doc_start(jax.random.fold_in(splits[18], 71), 0)
    premix_gain = jnp.clip(1.0 + 0.1 * jax.random.normal(splits[3], (D,), jnp.float32), 0.5, 1.5)
    inner_proj = scatter_about(splits[4], (D, DI), D ** -0.5, 0.125, ((0, 8), (1, 4)))
    switch_proj = scatter_about(splits[5], (D, DI), D ** -0.5, 0.125, ((0, 8), (1, 4)))
    conv_taps = scatter_about(splits[6], (KC, DI), KC ** -0.5, 3.0, ((1, 4),), jnp.float32)
    conv_bias = scatter_about(splits[7], (DI,), 0.5, 3.0, ((0, 4),), jnp.float32)
    select_proj = scatter_about(splits[8], (R + 2 * NS, DI), DI ** -0.5, 0.09375, ((0, 8), (1, 4)))
    step_proj = scatter_about(splits[9], (R, DI), R ** -0.5, 0.5, ((0, 8), (1, 4)))
    step_bias = jnp.clip(-6.0 + 4.0 * jax.random.uniform(splits[10], (DI,), jnp.float32) ** level_of(splits[10], (DI,), ((0, 4),), -0.2, 0.2), -6.0, -2.0)
    decay_log = jnp.clip(-8.0 + 9.0 * jax.random.uniform(splits[11], (NS, DI), jnp.float32) ** level_of(splits[11], (NS, DI), ((1, 4),), -0.2, 0.2), -8.0, 1.0)
    skip_gain = jnp.clip(0.5 + 1.0 * jax.random.uniform(splits[12], (DI,), jnp.float32) ** level_of(splits[12], (DI,), ((0, 4),), -0.2, 0.2), 0.5, 1.5)
    mixer_out = scatter_about(splits[13], (D, DI), DI ** -0.5, 0.09375, ((0, 8), (1, 4)))
    preffn_gain = jnp.clip(1.0 + 0.1 * jax.random.normal(splits[14], (D,), jnp.float32), 0.5, 1.5)
    ffn_gate = scatter_about(splits[15], (D, FF), D ** -0.5, 0.125, ((0, 8), (1, 4)))
    ffn_up = scatter_about(splits[16], (D, FF), D ** -0.5, 0.125, ((0, 8), (1, 4)))
    ffn_down = scatter_about(splits[17], (D, FF), FF ** -0.5, 0.0625, ((0, 8), (1, 4)))
    return dict(tokens=tokens, cotangent=cotangent, doc_start=doc_start, premix_gain=premix_gain, inner_proj=inner_proj, switch_proj=switch_proj, conv_taps=conv_taps, conv_bias=conv_bias, select_proj=select_proj, step_proj=step_proj, step_bias=step_bias, decay_log=decay_log, skip_gain=skip_gain, mixer_out=mixer_out, preffn_gain=preffn_gain, ffn_gate=ffn_gate, ffn_up=ffn_up, ffn_down=ffn_down)


@jax.custom_vjp
def low(v):
    return lax.optimization_barrier(v.astype(jnp.bfloat16)).astype(jnp.float32)

@jax.custom_vjp
def low_back(v):
    return v

def low_keep(v):
    return (low(v), None)

def low_pass(kept, grad):
    return (grad,)

def back_keep(v):
    return (v, None)

def back_low(kept, grad):
    return (low(grad),)
low.defvjp(low_keep, low_pass)
low_back.defvjp(back_keep, back_low)
EPS = 1e-05

def matmul(first_op, second_op):
    return jnp.dot(first_op, second_op, precision=lax.Precision.HIGHEST, preferred_element_type=jnp.float32)

def rms_scale(values, gain_vec):
    mean_sq = lax.optimization_barrier(jnp.mean(values * values, axis=-1, keepdims=True))
    return values * lax.rsqrt(mean_sq + EPS) * gain_vec

def conv_mix(inner_act, conv_taps, conv_bias, counts):
    summed = conv_bias[None, :] + conv_taps[0][None, :] * inner_act
    for offset in range(1, conv_taps.shape[0]):
        shifted = jnp.concatenate([jnp.zeros((offset, inner_act.shape[1]), inner_act.dtype), inner_act[:-offset]], axis=0)
        before = jnp.concatenate([jnp.zeros((offset,), counts.dtype), counts[:-offset]])
        same_doc = (counts == before).astype(inner_act.dtype)
        summed = summed + conv_taps[offset][None, :] * shifted * same_doc[:, None]
    return summed

def scan_rows(carried, blocked, decay):

    def step(running, per_token):
        step_t, input_t, write_t, read_t, flag_t = per_token
        factor = jnp.exp(step_t[None, :] * decay) * (1.0 - flag_t)
        running = factor * running + write_t[:, None] * (step_t * input_t)[None, :]
        return (running, lax.optimization_barrier(jnp.sum(read_t[:, None] * running, axis=0)))
    return lax.scan(step, carried, blocked)

def selective(step_size, mixed_in, write_vec, read_vec, start_flags, decay):
    block_len = math.gcd(step_size.shape[0], 256)
    block_count = step_size.shape[0] // block_len
    blocked = tuple((v.reshape((block_count, block_len) + v.shape[1:]) for v in (step_size, mixed_in, write_vec, read_vec, start_flags)))

    def run_block(carried, segment):
        return scan_rows(carried, segment, decay)
    zero_state = jnp.zeros((write_vec.shape[1], step_size.shape[1]), step_size.dtype)
    last_state, outputs = lax.scan(jax.checkpoint(run_block), zero_state, blocked)
    return outputs.reshape(step_size.shape)

def reference(tokens, cotangent, doc_start, premix_gain, inner_proj, switch_proj, conv_taps, conv_bias, select_proj, step_proj, step_bias, decay_log, skip_gain, mixer_out, preffn_gain, ffn_gate, ffn_up, ffn_down):
    counts = jnp.cumsum(doc_start).astype(jnp.int32)
    start_flags = doc_start.astype(jnp.float32)

    def forward(tokens, premix_gain, inner_proj, switch_proj, conv_taps, conv_bias, select_proj, step_proj, step_bias, decay_log, skip_gain, mixer_out, preffn_gain, ffn_gate, ffn_up, ffn_down):
        first_in = low(rms_scale(tokens, premix_gain))
        inner_act = low_back(low(matmul(first_in, inner_proj)))
        switch = low_back(matmul(first_in, switch_proj))
        conv_out = low_back(conv_mix(inner_act, conv_taps, conv_bias, counts))
        mixed_in = low(jax.nn.silu(conv_out))
        select = low_back(matmul(mixed_in, select_proj.T))
        low_rank = low(select[:, :R])
        write_vec = select[:, R:R + NS]
        read_vec = select[:, R + NS:]
        step_size = jax.nn.softplus(low_back(matmul(low_rank, step_proj)) + step_bias)
        decay = -jnp.exp(decay_log)
        scanned = selective(step_size, mixed_in, write_vec, read_vec, start_flags, decay) + skip_gain * mixed_in
        gated = low(scanned * jax.nn.silu(switch))
        residual = tokens + low_back(matmul(gated, mixer_out.T))
        second_in = low(rms_scale(residual, preffn_gain))
        gate_pre = low_back(matmul(second_in, ffn_gate))
        up_pre = low_back(matmul(second_in, ffn_up))
        hidden = low(jax.nn.silu(gate_pre) * up_pre)
        return residual + matmul(hidden, ffn_down.T)
    result, pullback = jax.vjp(forward, tokens.astype(jnp.float32), premix_gain, inner_proj.astype(jnp.float32), switch_proj.astype(jnp.float32), conv_taps, conv_bias, select_proj.astype(jnp.float32), step_proj.astype(jnp.float32), step_bias, decay_log, skip_gain, mixer_out.astype(jnp.float32), preffn_gain, ffn_gate.astype(jnp.float32), ffn_up.astype(jnp.float32), ffn_down.astype(jnp.float32))
    grads = pullback(cotangent.astype(jnp.float32))
    return (result.astype(jnp.bfloat16), grads[0].astype(jnp.bfloat16), grads[1], grads[2], grads[3], grads[4], grads[5], grads[6], grads[7], grads[8], grads[9], grads[10], grads[11], grads[12], grads[13], grads[14], grads[15])
```

```python
import functools

import jax
import jax.numpy as jnp
from jax import lax
from jax.experimental import pallas as pl
from jax.experimental.pallas import tpu as pltpu
from jax.sharding import PartitionSpec as P

NS = 16
R = 128
KC = 4
EPS = 1e-05
F32 = jnp.float32
BF16 = jnp.bfloat16
LOG2E = 1.4426950408889634
FAR = 1e30
MESH = pl.DeviceIdType.MESH
VMEM = pl.BlockSpec(memory_space=pltpu.VMEM)
SMEM = pl.BlockSpec(memory_space=pltpu.SMEM)
MIB = 2**20


def greet(axes):
    barrier = pltpu.get_barrier_semaphore()
    total = 0
    for axis in axes:
        n, me = lax.axis_size(axis), lax.axis_index(axis)
        for k in range(1, n):
            pl.semaphore_signal(
                barrier, inc=1, device_id={axis: lax.rem(me + k, n)}, device_id_type=MESH
            )
        total += n - 1
    pl.semaphore_wait(barrier, total)


def remote(src, dst, sems, slot, axis, peer):
    return pltpu.make_async_remote_copy(
        src_ref=src,
        dst_ref=dst,
        send_sem=sems.at[0, slot],
        recv_sem=sems.at[1, slot],
        device_id={axis: peer},
        device_id_type=MESH,
    )


def send(src, dst, sems, slot, axis, peer):
    copy = remote(src, dst, sems, slot, axis, peer)
    copy.start()
    return copy


def scatter_start(part, recv, sems, axis):
    n, me = lax.axis_size(axis), lax.axis_index(axis)
    rows = recv.shape[1]
    copies = []
    for k in range(1, n):
        peer = lax.rem(me + k, n)
        copies.append(
            send(part.at[pl.ds(peer * rows, rows)], recv.at[k - 1], sems, k - 1, axis, peer)
        )
    return copies


def gather_start(whole, rows, sems, axis):
    n, me = lax.axis_size(axis), lax.axis_index(axis)
    mine = whole.at[pl.ds(me * rows, rows)]
    return [send(mine, mine, sems, k - 1, axis, lax.rem(me + k, n)) for k in range(1, n)]


def arrived(copies):
    for copy in copies:
        copy.wait_recv()


def left(copies):
    for copy in copies:
        copy.wait_send()


def pair_sems(n):
    return pltpu.SemaphoreType.DMA((2, n - 1))


def summed(part, recv, at, step, row0):
    total = part[pl.ds(row0 + at, step)].astype(F32)
    for k in range(recv.shape[0]):
        total = total + recv[k, pl.ds(at, step)].astype(F32)
    return total


def step_rows(rows, step, body):
    def run(i, carry):
        body(pl.multiple_of(i * step, step))
        return carry

    lax.fori_loop(0, rows // step, run, 0)


def wt_sum_kernel(part, out, recv, s_scatter, s_gather):
    me = lax.axis_index("wt")
    rows = recv.shape[1]
    greet(("wt",))
    first = scatter_start(part, recv, s_scatter, "wt")
    arrived(first)
    out[pl.ds(me * rows, rows)] = summed(part, recv, 0, rows, me * rows)
    second = gather_start(out, rows, s_gather, "wt")
    arrived(second)
    left(first)
    left(second)


def wt_sum(part, n_wt, ident):
    rows, cols = part.shape
    return pl.pallas_call(
        wt_sum_kernel,
        out_shape=jax.ShapeDtypeStruct((rows, cols), F32),
        in_specs=[VMEM],
        out_specs=VMEM,
        scratch_shapes=[
            pltpu.VMEM((n_wt - 1, rows // n_wt, cols), F32),
            pair_sems(n_wt),
            pair_sems(n_wt),
        ],
        compiler_params=pltpu.CompilerParams(collective_id=ident, has_side_effects=True),
        cost_estimate=pl.CostEstimate(flops=10**5, bytes_accessed=10**6, transcendentals=0),
    )(part)


def second_norm_kernel(part, tok, gain, out, res, recv, s_scatter, s_gather):
    me = lax.axis_index("wt")
    rows = recv.shape[1]
    greet(("wt",))
    first = scatter_start(part, recv, s_scatter, "wt")
    arrived(first)
    row0 = me * rows

    def body(at):
        r = tok[pl.ds(at, 16)] + summed(part, recv, at, 16, row0)
        res[pl.ds(at, 16)] = r
        inverse = lax.rsqrt(jnp.mean(r * r, axis=-1, keepdims=True) + EPS)
        out[pl.ds(pl.multiple_of(row0 + at, 16), 16)] = (r * inverse * gain[...]).astype(BF16)

    step_rows(rows, 16, body)
    second = gather_start(out, rows, s_gather, "wt")
    arrived(second)
    left(first)
    left(second)


def second_norm(part, tok_own, gain, n_wt, ident):
    rows, cols = part.shape
    own = rows // n_wt
    return pl.pallas_call(
        second_norm_kernel,
        out_shape=[
            jax.ShapeDtypeStruct((rows, cols), BF16),
            jax.ShapeDtypeStruct((own, cols), F32),
        ],
        in_specs=[VMEM] * 3,
        out_specs=[VMEM] * 2,
        scratch_shapes=[
            pltpu.VMEM((n_wt - 1, own, cols), BF16),
            pair_sems(n_wt),
            pair_sems(n_wt),
        ],
        compiler_params=pltpu.CompilerParams(collective_id=ident, has_side_effects=True),
        cost_estimate=pl.CostEstimate(flops=10**6, bytes_accessed=10**8, transcendentals=0),
    )(part, tok_own, gain[None])


def norm_back_rows(grad, vals, gain):
    inverse = lax.rsqrt(jnp.mean(vals * vals, axis=-1, keepdims=True) + EPS)
    normed = vals * inverse
    scaled = grad * gain
    mean = jnp.mean(scaled * normed, axis=-1, keepdims=True)
    return inverse * (scaled - normed * mean), grad * normed


def second_back_kernel(part, res, cot, gain, out, d_res, gain_grad, recv, s_scatter, s_gather):
    me = lax.axis_index("wt")
    rows = recv.shape[1]
    greet(("wt",))
    first = scatter_start(part, recv, s_scatter, "wt")
    gain_grad[...] = jnp.zeros_like(gain_grad)
    arrived(first)
    row0 = me * rows

    def body(at):
        grad = summed(part, recv, at, 16, row0)
        back, prod = norm_back_rows(grad, res[pl.ds(at, 16)], gain[...])
        gain_grad[...] += prod[:8] + prod[8:]
        d = cot[pl.ds(at, 16)] + back
        d_res[pl.ds(at, 16)] = d
        out[pl.ds(pl.multiple_of(row0 + at, 16), 16)] = d.astype(BF16)

    step_rows(rows, 16, body)
    second = gather_start(out, rows, s_gather, "wt")
    arrived(second)
    left(first)
    left(second)


def second_back(part, res, cot_own, gain, n_wt, ident):
    rows, cols = part.shape
    own = rows // n_wt
    return pl.pallas_call(
        second_back_kernel,
        out_shape=[
            jax.ShapeDtypeStruct((rows, cols), BF16),
            jax.ShapeDtypeStruct((own, cols), F32),
            jax.ShapeDtypeStruct((8, cols), F32),
        ],
        in_specs=[VMEM] * 4,
        out_specs=[VMEM] * 3,
        scratch_shapes=[
            pltpu.VMEM((n_wt - 1, own, cols), BF16),
            pair_sems(n_wt),
            pair_sems(n_wt),
        ],
        compiler_params=pltpu.CompilerParams(collective_id=ident, has_side_effects=True),
        cost_estimate=pl.CostEstimate(flops=10**6, bytes_accessed=10**8, transcendentals=0),
    )(part, res, cot_own, gain[None])


def last_kernel(
    part, tok, d_res, gain, rows_small, by_chan, gain_grad2,
    out, small_out, chan_out, gains_out,
    recv, recv_small, recv_chan, gain_buf, recv_gz, recv_gs,
    s_scatter, s_gather, s_small, s_chan, s_gz, s_gs,
):
    me = lax.axis_index("wt")
    seq, n_seq = lax.axis_index("seq"), lax.axis_size("seq")
    rows = recv.shape[1]
    greet(("wt", "seq"))
    first = scatter_start(part, recv, s_scatter, "wt")
    smalls, chans = [], []
    for k in range(1, n_seq):
        peer = lax.rem(seq + k, n_seq)
        smalls.append(
            send(rows_small.at[peer], recv_small.at[k - 1], s_small, k - 1, "seq", peer)
        )
        chans.append(send(by_chan, recv_chan.at[k - 1], s_chan, k - 1, "seq", peer))
    gain_buf[1] = gain_grad2[...]
    gain_buf[0] = jnp.zeros_like(gain_grad2)
    arrived(smalls)
    total = rows_small[seq]
    for k in range(n_seq - 1):
        total = total + recv_small[k]
    small_out[...] = total
    arrived(chans)
    total = jnp.zeros_like(chan_out)
    for pos in range(n_seq):
        slot = lax.rem(seq - pos + n_seq, n_seq)
        other = recv_chan[jnp.maximum(slot - 1, 0)]
        total = total + jnp.where(slot == 0, by_chan[...], other)
    chan_out[...] = total
    arrived(first)
    row0 = me * rows

    def body(at):
        grad = summed(part, recv, at, 16, row0)
        back, prod = norm_back_rows(grad, tok[pl.ds(at, 16)], gain[...])
        gain_buf[0] += prod[:8] + prod[8:]
        out[pl.ds(pl.multiple_of(row0 + at, 16), 16)] = (d_res[pl.ds(at, 16)] + back).astype(BF16)

    step_rows(rows, 16, body)
    second = gather_start(out, rows, s_gather, "wt")
    n_wt = lax.axis_size("wt")
    zs = [
        send(gain_buf, recv_gz.at[me], s_gz, k - 1, "wt", lax.rem(me + k, n_wt))
        for k in range(1, n_wt)
    ]
    recv_gz[me] = gain_buf[...]
    arrived(zs)
    total = recv_gz[0]
    for pos in range(1, n_wt):
        total = total + recv_gz[pos]
    recv_gs[seq] = total
    mine = recv_gs.at[seq]
    ss = [
        send(mine, mine, s_gs, k - 1, "seq", lax.rem(seq + k, n_seq)) for k in range(1, n_seq)
    ]
    arrived(ss)
    total = recv_gs[0]
    for pos in range(1, n_seq):
        total = total + recv_gs[pos]
    gains_out[...] = jnp.sum(total, axis=1, keepdims=True)
    arrived(second)
    for group in (first, second, smalls, chans, zs, ss):
        left(group)


def last(part, tok_own, d_res, gain, rows_small, by_chan, gain_grad2, n_wt, n_seq, ident):
    rows, cols = part.shape
    own = rows // n_wt
    return pl.pallas_call(
        last_kernel,
        out_shape=[
            jax.ShapeDtypeStruct((rows, cols), BF16),
            jax.ShapeDtypeStruct(rows_small.shape[1:], F32),
            jax.ShapeDtypeStruct(by_chan.shape, F32),
            jax.ShapeDtypeStruct((2, 1, cols), F32),
        ],
        in_specs=[VMEM] * 7,
        out_specs=[VMEM] * 4,
        scratch_shapes=[
            pltpu.VMEM((n_wt - 1, own, cols), BF16),
            pltpu.VMEM((n_seq - 1,) + rows_small.shape[1:], F32),
            pltpu.VMEM((n_seq - 1,) + by_chan.shape, F32),
            pltpu.VMEM((2, 8, cols), F32),
            pltpu.VMEM((n_wt, 2, 8, cols), F32),
            pltpu.VMEM((n_seq, 2, 8, cols), F32),
            pair_sems(n_wt),
            pair_sems(n_wt),
            pair_sems(n_seq),
            pair_sems(n_seq),
            pair_sems(n_wt),
            pair_sems(n_seq),
        ],
        compiler_params=pltpu.CompilerParams(
            collective_id=ident, has_side_effects=True, vmem_limit_bytes=40 * MIB
        ),
        cost_estimate=pl.CostEstimate(flops=10**6, bytes_accessed=10**8, transcendentals=0),
    )(part, tok_own, d_res, gain[None], rows_small, by_chan, gain_grad2)


def load(ref):
    return tuple(ref[n] for n in range(NS))


def store(ref, values):
    for n in range(NS):
        ref[n] = values[n]


def fold(mine, box, recv, a2, carried, backward):
    n, me = lax.axis_size("seq"), lax.axis_index("seq")
    carried[...] = jnp.zeros_like(carried)
    for k in range(n - 1, 0, -1):

        @pl.when((me + k < n) if backward else (me >= k))
        def _():
            giver = me + k if backward else me - k
            remote(mine, recv.at[k - 1], box, k - 1, "seq", giver).wait_recv()
            through = recv[k - 1, NS]
            for s in range(NS):
                carried[s] = (
                    jnp.exp2(a2[s] * through) * carried[s] + recv[k - 1, s]
                )


def hand_on(mine, recv, box, backward):
    n, me = lax.axis_size("seq"), lax.axis_index("seq")
    for k in range(1, n):

        @pl.when((me >= k) if backward else (me + k < n))
        def _():
            peer = me - k if backward else me + k
            send(mine, recv.at[k - 1], box, k - 1, "seq", peer)


def handed(mine, recv, box, backward):
    n, me = lax.axis_size("seq"), lax.axis_index("seq")
    for k in range(1, n):

        @pl.when((me >= k) if backward else (me + k < n))
        def _():
            peer = me - k if backward else me + k
            remote(mine, recv.at[k - 1], box, k - 1, "seq", peer).wait_send()


def fwd_kernel(sa, dx, w, r, a2, y, h0, mine, recv, box):
    tok = sa.shape[0]
    greet(("seq",))

    def end(t, carry):
        s, d = sa[t], dx[t]
        h, total = carry
        return (
            tuple(jnp.exp2(s * a2[n]) * h[n] + w[t, n] * d for n in range(NS)),
            total + s,
        )

    zero = jnp.zeros(sa.shape[1:], F32)
    ends, total = lax.fori_loop(0, tok, end, ((zero,) * NS, zero), unroll=4)
    store(mine, ends)
    mine[NS] = total
    hand_on(mine, recv, box, False)
    fold(mine, box, recv, a2, h0, False)

    def body(t, h):
        s, d = sa[t], dx[t]
        new, sums = [], [None] * 4
        for n in range(NS):
            hn = jnp.exp2(s * a2[n]) * h[n] + w[t, n] * d
            new.append(hn)
            c = r[t, n] * hn
            sums[n % 4] = c if sums[n % 4] is None else sums[n % 4] + c
        y[t] = (sums[0] + sums[1]) + (sums[2] + sums[3])
        return tuple(new)

    lax.fori_loop(0, tok, body, load(h0), unroll=4)
    handed(mine, recv, box, False)


def fwd_scan(sa, dx, w, r, a2, n_seq, ident):
    tok, high = sa.shape[:2]
    return pl.pallas_call(
        fwd_kernel,
        out_shape=[
            jax.ShapeDtypeStruct((tok, high, 128), F32),
            jax.ShapeDtypeStruct((NS, high, 128), F32),
        ],
        in_specs=[VMEM, VMEM, SMEM, SMEM, VMEM],
        out_specs=[VMEM] * 2,
        scratch_shapes=[
            pltpu.VMEM((NS + 1, high, 128), F32),
            pltpu.VMEM((n_seq - 1, NS + 1, high, 128), F32),
            pair_sems(n_seq),
        ],
        compiler_params=pltpu.CompilerParams(
            collective_id=ident, has_side_effects=True, vmem_limit_bytes=32 * MIB
        ),
        cost_estimate=pl.CostEstimate(
            flops=10**8, bytes_accessed=8 * 10**7, transcendentals=2 * tok * NS * 1024
        ),
    )(sa, dx, w, r, a2)


def bwd_kernel(
    sa, dx, w, r, do, a2, h0, part, res,
    along, ds2, grad_a, pw, pr, out,
    hs, qw, qr, g0, mine, recv, recv_z, box, s_scatter, s_gather,
):
    tok = sa.shape[0]
    chunk = qw.shape[0] // (NS * 8)
    greet(("wt", "seq"))
    first = scatter_start(part, recv_z, s_scatter, "wt")

    def end(i, carry):
        t = tok - 1 - i
        s, d = sa[t], do[t]
        g, total = carry
        return (
            tuple(jnp.exp2(s * a2[n]) * (g[n] + r[t, n] * d) for n in range(NS)),
            total + s,
        )

    zero = jnp.zeros(sa.shape[1:], F32)
    ends, total = lax.fori_loop(0, tok, end, ((zero,) * NS, zero), unroll=4)
    store(mine, ends)
    mine[NS] = total
    hand_on(mine, recv, box, True)

    def again(t, h):
        s, d = sa[t], dx[t]
        new = []
        for n in range(NS):
            hs[t, n] = h[n]
            new.append(jnp.exp2(s * a2[n]) * h[n] + w[t, n] * d)
        return tuple(new)

    lax.fori_loop(0, tok, again, load(h0), unroll=2)

    arrived(first)
    me = lax.axis_index("wt")
    rows = recv_z.shape[1]
    row0 = me * rows

    def block_rows(at):
        total = res[pl.ds(at, 16)] + summed(part, recv_z, at, 16, row0)
        out[pl.ds(pl.multiple_of(row0 + at, 16), 16)] = total.astype(BF16)

    step_rows(rows, 16, block_rows)
    second = gather_start(out, rows, s_gather, "wt")

    fold(mine, box, recv, a2, g0, True)
    grad_a[...] = jnp.zeros_like(grad_a)

    def one_chunk(j, g):
        base = (tok // chunk - 1 - j) * chunk

        def body(i, g):
            at = chunk - 1 - i
            t = base + at
            s, d, o = sa[t], dx[t], do[t]
            al = d2 = None
            new = []
            for n in range(NS):
                hp = hs[t, n]
                f = jnp.exp2(s * a2[n])
                hn = f * hp + w[t, n] * d
                gn = r[t, n] * o + g[n]
                adj = f * gn
                new.append(adj)
                th = adj * hp
                grad_a[n] += th * s
                x = w[t, n] * gn
                al = x if al is None else al + x
                x = a2[n] * th
                d2 = x if d2 is None else d2 + x
                row = pl.multiple_of((at * NS + n) * 8, 8)
                qw[pl.ds(row, 8), :] = gn * d
                qr[pl.ds(row, 8), :] = hn * o
            along[t] = al
            ds2[t] = d2
            return tuple(new)

        g = lax.fori_loop(0, chunk, body, g)

        def lanes(i, carry):
            for q, p in ((qw, pw), (qr, pr)):
                acc = q[pl.ds(i * NS * 8, NS, stride=8), :]
                for s in range(1, 8):
                    acc = acc + q[pl.ds(i * NS * 8 + s, NS, stride=8), :]
                p[base + i] = acc
            return carry

        lax.fori_loop(0, chunk, lanes, 0, unroll=4)
        return g

    lax.fori_loop(0, tok // chunk, one_chunk, load(g0))
    handed(mine, recv, box, True)
    arrived(second)
    left(first)
    left(second)


def bwd_scan(sa, dx, w, r, do, a2, h0, part, res, n_wt, n_seq, ident):
    tok, high = sa.shape[:2]
    rows, cols = part.shape
    chunk = 32
    return pl.pallas_call(
        bwd_kernel,
        out_shape=[
            jax.ShapeDtypeStruct((tok, high, 128), F32),
            jax.ShapeDtypeStruct((tok, high, 128), F32),
            jax.ShapeDtypeStruct((NS, high, 128), F32),
            jax.ShapeDtypeStruct((tok, NS, 128), F32),
            jax.ShapeDtypeStruct((tok, NS, 128), F32),
            jax.ShapeDtypeStruct((rows, cols), BF16),
        ],
        in_specs=[VMEM, VMEM, SMEM, SMEM] + [VMEM] * 5,
        out_specs=[VMEM] * 6,
        scratch_shapes=[
            pltpu.VMEM((tok, NS, high, 128), F32),
            pltpu.VMEM((chunk * NS * 8, 128), F32),
            pltpu.VMEM((chunk * NS * 8, 128), F32),
            pltpu.VMEM((NS, high, 128), F32),
            pltpu.VMEM((NS + 1, high, 128), F32),
            pltpu.VMEM((n_seq - 1, NS + 1, high, 128), F32),
            pltpu.VMEM((n_wt - 1, rows // n_wt, cols), BF16),
            pair_sems(n_seq),
            pair_sems(n_wt),
            pair_sems(n_wt),
        ],
        compiler_params=pltpu.CompilerParams(
            collective_id=ident, has_side_effects=True, vmem_limit_bytes=56 * MIB
        ),
        cost_estimate=pl.CostEstimate(
            flops=10**8, bytes_accessed=15 * 10**7, transcendentals=3 * tok * NS * 1024
        ),
    )(sa, dx, w, r, do, a2, h0, part, res)


def gather(block):
    return lax.all_gather(block, "seq", axis=0, tiled=True)


def from_behind(block, axis, distance):
    devices = range(lax.axis_size(axis))
    route = [(i - distance, i) for i in devices if i - distance in devices]
    return lax.ppermute(block, axis, route)


def contract(left_op, right_op, pattern):
    return jnp.einsum(pattern, left_op, right_op, preferred_element_type=F32)


def silu_slope(values):
    sigma = jax.nn.sigmoid(values)
    return sigma * (1.0 + values * (1.0 - sigma))


def tiles(rows):
    return rows.reshape(rows.shape[0], rows.shape[1] // 128, 128)


def flat(rows):
    return rows.reshape(rows.shape[0], rows.shape[1] * rows.shape[2])


def local(
    tokens,
    cotangent,
    doc_start,
    premix_gain,
    inner_proj,
    switch_proj,
    conv_taps,
    conv_bias,
    select_proj,
    step_proj,
    step_bias,
    decay_log,
    skip_gain,
    mixer_out,
    preffn_gain,
    ffn_gate,
    ffn_up,
    ffn_down,
):
    tok_count, width = tokens.shape
    chan = inner_proj.shape[1]
    units = ffn_gate.shape[1]
    edge = KC - 1
    n_seq, n_wt = lax.axis_size("seq"), lax.axis_size("wt")
    z = lax.axis_index("wt")
    own = tok_count // n_wt
    gather_acts = n_seq * tok_count <= width

    w_mixer = gather(jnp.concatenate([inner_proj, switch_proj, mixer_out], axis=1))
    w_first, w_mix = w_mixer[:, : 2 * chan], w_mixer[:, 2 * chan :]
    w_small = lax.all_gather(jnp.concatenate([select_proj, step_proj], axis=0), "seq", axis=0)
    w_select = w_small[:, : select_proj.shape[0]].reshape(-1, chan)
    w_step = w_small[:, select_proj.shape[0] :].reshape(-1, chan)
    w_all = gather(jnp.concatenate([ffn_gate, ffn_up, ffn_down], axis=1))
    w_ffn, w_down = w_all[:, : 2 * units], w_all[:, 2 * units :]

    token_vals = tokens.astype(F32)
    first_inv = lax.rsqrt(jnp.mean(token_vals * token_vals, axis=-1, keepdims=True) + EPS)
    first_in = (token_vals * first_inv * premix_gain).astype(BF16)
    both = contract(first_in, w_first, "td,dc->tc")
    inner_act = both[:, :chan].astype(BF16)
    switch = both[:, chan:]

    counts = jnp.cumsum(doc_start)
    last_count = counts[-1]
    head_keep = (counts == 0).astype(F32)
    tail_keep = (counts == last_count).astype(F32)
    tail_rows = jnp.where(
        tail_keep[-edge:, None] > 0, inner_act[-edge:], jnp.zeros_like(inner_act[-edge:])
    )
    prev_rows = from_behind(tail_rows, "seq", 1)
    extended = jnp.concatenate([prev_rows, inner_act], axis=0).astype(F32)
    ext_counts = jnp.concatenate([jnp.zeros((edge,), jnp.int32), counts])
    conv_out = jnp.zeros((tok_count, chan), F32) + conv_bias[None, :]
    for offset in range(KC):
        same_doc = (counts == ext_counts[edge - offset : edge - offset + tok_count]).astype(F32)
        conv_out = (
            conv_out
            + conv_taps[offset][None, :]
            * extended[edge - offset : edge - offset + tok_count]
            * same_doc[:, None]
        )
    mixed_in = jax.nn.silu(conv_out).astype(BF16)
    mixed_f = mixed_in.astype(F32)
    select = wt_sum(contract(w_select, mixed_in, "jc,tc->jt"), n_wt, 0)
    low_rank = select[:R].astype(BF16)
    write_vec = select[R : R + NS].T
    read_vec = select[R + NS :].T
    step_pre = contract(low_rank, w_step, "rt,rc->tc") + step_bias[None, :]
    step_size = jax.nn.softplus(step_pre)
    decay = -jnp.exp(decay_log)
    decay2 = tiles(decay * LOG2E)
    step_a = tiles(jnp.where(doc_start[:, None] > 0, FAR, step_size))
    drive = tiles(step_size * mixed_f)
    scan_out, carried_in = fwd_scan(step_a, drive, write_vec, read_vec, decay2, n_seq, 1)

    scanned = flat(scan_out) + skip_gain[None, :] * mixed_f
    switch_act = jax.nn.silu(switch)
    gated = (scanned * switch_act).astype(BF16)
    mix_part = contract(gated, w_mix, "tc,dc->td").astype(BF16)
    tokens_own = lax.dynamic_slice_in_dim(tokens, z * own, own, 0).astype(F32)
    cot_own = lax.dynamic_slice_in_dim(cotangent, z * own, own, 0).astype(F32)
    second_in, residual = second_norm(mix_part, tokens_own, preffn_gain, n_wt, 2)
    gate_up = contract(second_in, w_ffn, "td,df->tf")
    gate_pre, up_pre = gate_up[:, :units], gate_up[:, units:]
    gate_act = jax.nn.silu(gate_pre)
    hidden = (gate_act * up_pre).astype(BF16)

    d_hidden = contract(cotangent, w_down, "td,df->tf")
    d_gate = (d_hidden * up_pre * silu_slope(gate_pre)).astype(BF16)
    d_up = (d_hidden * gate_act).astype(BF16)
    d_ffn = jnp.concatenate([d_gate, d_up], axis=1)
    d_second = contract(d_ffn, w_ffn, "tf,df->td").astype(BF16)
    d_branch, d_residual, grad_preffn = second_back(d_second, residual, cot_own, preffn_gain, n_wt, 3)
    down_part = contract(hidden, w_down, "tf,df->td").astype(BF16)
    d_gated = contract(d_branch, w_mix, "td,dc->tc")
    d_scanned = d_gated * switch_act
    d_switch = (d_gated * scanned * silu_slope(switch)).astype(BF16)
    grad_skip = jnp.sum(d_scanned * mixed_f, axis=0)
    along, through_sum, grad_decay, write_lanes, read_lanes, block_out = bwd_scan(
        step_a, drive, write_vec, read_vec, tiles(d_scanned), decay2, carried_in,
        down_part, residual, n_wt, n_seq, 4,
    )
    along = flat(along)
    d_step = along * mixed_f + flat(through_sum) * (1.0 / LOG2E)
    grad_decay_log = flat(grad_decay) * decay
    d_pre = d_step * jax.nn.sigmoid(step_pre)
    grad_step_bias = jnp.sum(d_pre, axis=0)
    d_pre_low = d_pre.astype(BF16)
    grad_step = contract(low_rank, d_pre_low, "rt,tc->rc")
    d_select = wt_sum(
        jnp.concatenate(
            [
                contract(w_step, d_pre_low, "rc,tc->rt"),
                jnp.sum(write_lanes, axis=-1).T,
                jnp.sum(read_lanes, axis=-1).T,
            ],
            axis=0,
        ),
        n_wt,
        5,
    ).astype(BF16)
    grad_select = contract(d_select, mixed_in, "jt,tc->jc")
    d_mixed = (
        along * step_size
        + skip_gain[None, :] * d_scanned
        + contract(d_select, w_select, "jt,jc->tc")
    )
    d_conv = (d_mixed * silu_slope(conv_out)).astype(BF16)
    d_conv_f = d_conv.astype(F32)
    grad_conv_bias = jnp.sum(d_conv_f, axis=0)
    head_rows = jnp.where(head_keep[:edge, None] > 0, d_conv[:edge], jnp.zeros_like(d_conv[:edge]))
    next_rows = from_behind(head_rows, "seq", -1)
    ext_grad = jnp.concatenate([d_conv, next_rows], axis=0).astype(F32)
    ext_after = jnp.concatenate([counts, jnp.zeros((edge,), jnp.int32) + last_count])
    d_inner = jnp.zeros_like(d_conv_f)
    taps_rows = []
    for offset in range(KC):
        same_doc = (counts == ext_counts[edge - offset : edge - offset + tok_count]).astype(F32)
        taps_rows.append(
            jnp.sum(
                d_conv_f * extended[edge - offset : edge - offset + tok_count] * same_doc[:, None],
                axis=0,
            )
        )
        later_same = (ext_after[offset : offset + tok_count] == counts).astype(F32)
        d_inner = (
            d_inner
            + conv_taps[offset][None, :]
            * ext_grad[offset : offset + tok_count]
            * later_same[:, None]
        )
    d_inner_low = d_inner.astype(BF16)
    d_first = contract(
        jnp.concatenate([d_inner_low, d_switch], axis=1), w_first, "tc,dc->td"
    ).astype(BF16)
    small = jnp.concatenate(
        [grad_select.reshape(n_seq, -1, chan), grad_step.reshape(n_seq, -1, chan)], axis=1
    )
    by_chan = jnp.concatenate(
        [
            jnp.stack(taps_rows, axis=0),
            grad_decay_log,
            grad_conv_bias[None],
            grad_step_bias[None],
            grad_skip[None],
            jnp.zeros((1, chan), F32),
        ],
        axis=0,
    )
    tokens_grad, small, by_chan, gains = last(
        d_first, tokens_own, d_residual, premix_gain, small, by_chan, grad_preffn, n_wt, n_seq, 6
    )

    if gather_acts:
        ffn_all = gather(jnp.concatenate([hidden, d_ffn], axis=1))
        mix_all = gather(jnp.concatenate([gated, d_switch, d_inner_low], axis=1))
        blocks = lambda v: v.reshape(tok_count, n_seq, 1, width // n_seq)
        early = jnp.concatenate([blocks(cotangent), blocks(first_in)], axis=2)
        late = jnp.concatenate([blocks(second_in), blocks(d_branch)], axis=2)
        early = lax.all_to_all(early, "seq", 1, 0, tiled=True).reshape(n_seq * tok_count, -1)
        late = lax.all_to_all(late, "seq", 1, 0, tiled=True).reshape(n_seq * tok_count, -1)
        piece = width // n_seq
        cot_f, first_f = early[:, :piece], early[:, piece:]
        second_f, branch_f = late[:, :piece], late[:, piece:]
        out_down = contract(cot_f, ffn_all[:, :units], "td,tf->df")
        out_gate = contract(second_f, ffn_all[:, units : 2 * units], "td,tf->df")
        out_up = contract(second_f, ffn_all[:, 2 * units :], "td,tf->df")
        out_mix = contract(branch_f, mix_all[:, :chan], "td,tc->dc")
        out_switch = contract(first_f, mix_all[:, chan : 2 * chan], "td,tc->dc")
        out_inner = contract(first_f, mix_all[:, 2 * chan :], "td,tc->dc")
    else:
        scatter = lambda v: lax.psum_scatter(v, "seq", scatter_dimension=0, tiled=True)
        out_down = scatter(contract(cotangent, hidden, "td,tf->df"))
        out_gate = scatter(contract(second_in, d_gate, "td,tf->df"))
        out_up = scatter(contract(second_in, d_up, "td,tf->df"))
        out_mix = scatter(contract(d_branch, gated, "td,tc->dc"))
        out_switch = scatter(contract(first_in, d_switch, "td,tc->dc"))
        out_inner = scatter(contract(first_in, d_inner_low, "td,tc->dc"))
    rows_sel = select_proj.shape[0]
    return (
        block_out,
        tokens_grad,
        gains[0, 0],
        out_inner,
        out_switch,
        by_chan[:KC],
        by_chan[KC + NS],
        small[:rows_sel],
        small[rows_sel:],
        by_chan[KC + NS + 1],
        by_chan[KC : KC + NS],
        by_chan[KC + NS + 2],
        out_mix,
        gains[1, 0],
        out_gate,
        out_up,
        out_down,
    )


def solution(mesh):
    placed = (
        P("seq", None),
        P("seq", None),
        P("seq"),
        P(),
        P("seq", "wt"),
        P("seq", "wt"),
        P(None, "wt"),
        P("wt"),
        P("seq", "wt"),
        P("seq", "wt"),
        P("wt"),
        P(None, "wt"),
        P("wt"),
        P("seq", "wt"),
        P(),
        P("seq", "wt"),
        P("seq", "wt"),
        P("seq", "wt"),
    )
    return jax.shard_map(
        local,
        mesh=mesh,
        in_specs=placed,
        out_specs=(
            P("seq", None),
            P("seq", None),
            P(),
            P("seq", "wt"),
            P("seq", "wt"),
            P(None, "wt"),
            P("wt"),
            P("seq", "wt"),
            P("seq", "wt"),
            P("wt"),
            P(None, "wt"),
            P("wt"),
            P("seq", "wt"),
            P(),
            P("seq", "wt"),
            P("seq", "wt"),
            P("seq", "wt"),
        ),
        check_vma=False,
    )
```

```python
import functools

import jax
import jax.numpy as jnp
from jax import lax
from jax.experimental import pallas as pl
from jax.experimental.pallas import tpu as pltpu
from jax.sharding import PartitionSpec as P

NS = 16
R = 128
KC = 4
EPS = 1e-05
F32 = jnp.float32
BF16 = jnp.bfloat16
LOG2E = 1.4426950408889634
FAR = 1e30
MESH = pl.DeviceIdType.MESH
VMEM = pl.BlockSpec(memory_space=pltpu.VMEM)
SMEM = pl.BlockSpec(memory_space=pltpu.SMEM)
ANY = pl.BlockSpec(memory_space=pl.ANY)
MIB = 2**20


def greet(axes):
    barrier = pltpu.get_barrier_semaphore()
    total = 0
    for axis in axes:
        n, me = lax.axis_size(axis), lax.axis_index(axis)
        for k in range(1, n):
            pl.semaphore_signal(
                barrier, inc=1, device_id={axis: lax.rem(me + k, n)}, device_id_type=MESH
            )
        total += n - 1
    pl.semaphore_wait(barrier, total)


def remote(src, dst, sems, slot, axis, peer):
    return pltpu.make_async_remote_copy(
        src_ref=src,
        dst_ref=dst,
        send_sem=sems.at[0, slot],
        recv_sem=sems.at[1, slot],
        device_id={axis: peer},
        device_id_type=MESH,
    )


def send(src, dst, sems, slot, axis, peer):
    copy = remote(src, dst, sems, slot, axis, peer)
    copy.start()
    return copy


def scatter_start(part, recv, sems, axis):
    n, me = lax.axis_size(axis), lax.axis_index(axis)
    rows = recv.shape[1]
    copies = []
    for k in range(1, n):
        peer = lax.rem(me + k, n)
        copies.append(
            send(part.at[pl.ds(peer * rows, rows)], recv.at[k - 1], sems, k - 1, axis, peer)
        )
    return copies


def gather_start(whole, rows, sems, axis):
    n, me = lax.axis_size(axis), lax.axis_index(axis)
    mine = whole.at[pl.ds(me * rows, rows)]
    return [send(mine, mine, sems, k - 1, axis, lax.rem(me + k, n)) for k in range(1, n)]


def arrived(copies):
    for copy in copies:
        copy.wait_recv()


def left(copies):
    for copy in copies:
        copy.wait_send()


def pair_sems(n):
    return pltpu.SemaphoreType.DMA((2, n - 1))


def summed(part, recv, at, step, row0):
    total = part[pl.ds(row0 + at, step)].astype(F32)
    for k in range(recv.shape[0]):
        total = total + recv[k, pl.ds(at, step)].astype(F32)
    return total


def step_rows(rows, step, body):
    def run(i, carry):
        body(pl.multiple_of(i * step, step))
        return carry

    lax.fori_loop(0, rows // step, run, 0)


def flips():
    seq = lax.axis_index("seq")
    core, x, y = lax.rem(seq, 2), lax.rem(seq // 2, 2), seq // 4

    def at(fy, fx, fc):
        return (
            (1 - y if fy else y) * 4 + (1 - x if fx else x) * 2 + (1 - core if fc else core)
        )

    return at


def cube_sems():
    return pltpu.SemaphoreType.DMA((2, 9))


def cube_first(block, whole, sems):
    at = flips()
    mine = whole.at[at(0, 0, 0)]
    return [
        send(block, mine, sems, 0, "seq", at(0, 1, 0)),
        send(block, mine, sems, 1, "seq", at(1, 0, 0)),
        send(block, mine, sems, 2, "seq", at(0, 0, 1)),
    ]


def keep(block, whole, sem):
    copy = pltpu.make_async_copy(block, whole.at[lax.axis_index("seq")], sem)
    copy.start()
    return copy


def spread(src, dst, sems, own_sem):
    seq, n_seq = lax.axis_index("seq"), lax.axis_size("seq")
    piece = dst.shape[2]

    def columns(peer):
        return src.at[:, pl.ds(pl.multiple_of(peer * piece, piece), piece)]

    out = []
    for k in range(1, n_seq):
        peer = lax.rem(seq + k, n_seq)
        out.append(send(columns(peer), dst.at[seq], sems, k - 1, "seq", peer))
    return out, keep(columns(seq), dst, own_sem)


def cube_second(whole, sems, first):
    at = flips()
    half = whole.shape[1] // 2
    first[0].wait_recv()
    block = whole.at[at(0, 1, 0)]
    top = block.at[pl.ds(0, half)]
    sent = [
        send(top, top, sems, 3, "seq", at(1, 0, 0)),
        send(block, block, sems, 5, "seq", at(0, 0, 1)),
    ]
    first[1].wait_recv()
    block = whole.at[at(1, 0, 0)]
    low = block.at[pl.ds(half, half)]
    sent += [
        send(low, low, sems, 4, "seq", at(0, 1, 0)),
        send(block, block, sems, 6, "seq", at(0, 0, 1)),
    ]
    return sent


def cube_third(whole, sems, second):
    at = flips()
    half = whole.shape[1] // 2
    block = whole.at[at(1, 1, 0)]
    sent = []
    for slot, came in ((0, second[0]), (1, second[2])):
        came.wait_recv()
        piece = block.at[pl.ds(slot * half, half)]
        sent.append(send(piece, piece, sems, 7 + slot, "seq", at(0, 0, 1)))
    return sent


def cube_end(first, second, third):
    first[2].wait_recv()
    second[1].wait_recv()
    second[3].wait_recv()
    arrived(third)
    for group in (first, second, third):
        left(group)


def first_kernel(
    mixer, small, cot, act, w_mixer, w_small, cot_f, act_f,
    s_big, s_small, s_own, s_cot, s_act, s_cz, s_az,
):
    seq, n_seq = lax.axis_index("seq"), lax.axis_size("seq")
    z, n_wt = lax.axis_index("wt"), lax.axis_size("wt")
    own, piece = cot_f.shape[2:]
    kept = [keep(mixer, w_mixer, s_own.at[0]), keep(small, w_small, s_own.at[1])]
    greet(("seq", "wt"))
    little = cube_first(small, w_small, s_small)
    sent, mine = [], []
    for i, (src, dst, sems) in enumerate(((cot, cot_f, s_cot), (act, act_f, s_act))):
        rows = src.at[pl.ds(pl.multiple_of(z * own, own), own)]

        def columns(peer, rows=rows):
            return rows.at[:, pl.ds(pl.multiple_of(peer * piece, piece), piece)]

        for k in range(1, n_seq):
            peer = lax.rem(seq + k, n_seq)
            sent.append(send(columns(peer), dst.at[seq, z], sems, k - 1, "seq", peer))
        mine.append(pltpu.make_async_copy(columns(seq), dst.at[seq, z], s_own.at[2 + i]))
        mine[-1].start()
    big = cube_first(mixer, w_mixer, s_big)
    arrived(sent)
    for copy in mine:
        copy.wait()
    along = []
    for dst, sems in ((cot_f, s_cz), (act_f, s_az)):
        lines = dst.at[:, z]
        along += [
            send(lines, lines, sems, k - 1, "wt", lax.rem(z + k, n_wt)) for k in range(1, n_wt)
        ]
    little2 = cube_second(w_small, s_small, little)
    little3 = cube_third(w_small, s_small, little2)
    big2 = cube_second(w_mixer, s_big, big)
    big3 = cube_third(w_mixer, s_big, big2)
    cube_end(little, little2, little3)
    cube_end(big, big2, big3)
    arrived(along)
    left(along)
    left(sent)
    for copy in kept:
        copy.wait()


def first_gather(mixer, small, cot, act, n_wt, n_seq, ident):
    tok, width = cot.shape
    far = jax.ShapeDtypeStruct((n_seq, n_wt, tok // n_wt, width // n_seq), BF16)
    return pl.pallas_call(
        first_kernel,
        out_shape=[
            jax.ShapeDtypeStruct((n_seq,) + mixer.shape, BF16),
            jax.ShapeDtypeStruct((n_seq,) + small.shape, BF16),
            far,
            far,
        ],
        in_specs=[ANY, ANY, VMEM, VMEM],
        out_specs=[ANY] * 4,
        scratch_shapes=[
            cube_sems(),
            cube_sems(),
            pltpu.SemaphoreType.DMA((4,)),
            pair_sems(n_seq),
            pair_sems(n_seq),
            pair_sems(n_wt),
            pair_sems(n_wt),
        ],
        compiler_params=pltpu.CompilerParams(collective_id=ident, has_side_effects=True),
        cost_estimate=pl.CostEstimate(flops=10**6, bytes_accessed=10**8, transcendentals=0),
    )(mixer, small, cot, act)


UNITS = 256


def nt(left_op, right_op):
    return lax.dot_general(
        left_op, right_op, (((1,), (1,)), ((), ())), preferred_element_type=F32
    )


def ffn_kernel(x, c, wg, wu, wd, acts, down, d_second, acc_down, acc_second):
    step = pl.program_id(0)

    @pl.when(step == 0)
    def _():
        acc_down[...] = jnp.zeros_like(acc_down)
        acc_second[...] = jnp.zeros_like(acc_second)

    gate = jnp.dot(x[...], wg[...], preferred_element_type=F32)
    up = jnp.dot(x[...], wu[...], preferred_element_type=F32)
    d_hidden = jnp.dot(c[...], wd[...], preferred_element_type=F32)
    sigma = jax.nn.sigmoid(gate)
    act = gate * sigma
    hidden = (act * up).astype(BF16)
    d_gate = (d_hidden * up * (sigma * (1.0 + gate * (1.0 - sigma)))).astype(BF16)
    d_up = (d_hidden * act).astype(BF16)
    acts[:, :UNITS] = hidden
    acts[:, UNITS : 2 * UNITS] = d_gate
    acts[:, 2 * UNITS :] = d_up
    acc_down[...] += nt(hidden, wd[...])
    acc_second[...] += nt(d_gate, wg[...]) + nt(d_up, wu[...])

    @pl.when(step == pl.num_programs(0) - 1)
    def _():
        down[...] = acc_down[...].astype(BF16)
        d_second[...] = acc_second[...].astype(BF16)


def ffn(x, c, w_all):
    tok, width = x.shape
    units = w_all.shape[1] // 3
    steps = units // UNITS
    whole = pl.BlockSpec((tok, width), lambda i: (0, 0))
    tile = lambda part: pl.BlockSpec((width, UNITS), lambda i: (0, part * steps + i))
    return pl.pallas_call(
        ffn_kernel,
        grid=(steps,),
        in_specs=[whole, whole, tile(0), tile(1), tile(2)],
        out_specs=[pl.BlockSpec((tok, 3 * UNITS), lambda i: (0, i)), whole, whole],
        out_shape=[
            jax.ShapeDtypeStruct((tok, 3 * units), BF16),
            jax.ShapeDtypeStruct((tok, width), BF16),
            jax.ShapeDtypeStruct((tok, width), BF16),
        ],
        scratch_shapes=[pltpu.VMEM((tok, width), F32)] * 2,
        compiler_params=pltpu.CompilerParams(vmem_limit_bytes=40 * MIB),
        cost_estimate=pl.CostEstimate(
            flops=12 * tok * width * units, bytes_accessed=6 * width * units, transcendentals=0
        ),
    )(x, c, w_all, w_all, w_all)


def grads_kernel(lefts, *refs):
    n, m = max(lefts) + 1, len(lefts)
    for which, act, out in zip(lefts, refs[n : n + m], refs[n + m :]):
        out[...] = jnp.dot(refs[which][...], act[...], preferred_element_type=F32)


def grads(left_ops, lefts, acts):
    rows, tok = left_ops[0].shape
    cols = acts[0].shape[1]
    n = len(acts)
    return pl.pallas_call(
        functools.partial(grads_kernel, lefts),
        grid=(cols // UNITS,),
        in_specs=[pl.BlockSpec((rows, tok), lambda i: (0, 0))] * len(left_ops)
        + [pl.BlockSpec((tok, UNITS), lambda i: (0, i))] * n,
        out_specs=[pl.BlockSpec((rows, UNITS), lambda i: (0, i))] * n,
        out_shape=[jax.ShapeDtypeStruct((rows, cols), F32)] * n,
        compiler_params=pltpu.CompilerParams(vmem_limit_bytes=60 * MIB),
        cost_estimate=pl.CostEstimate(
            flops=2 * n * tok * rows * cols, bytes_accessed=2 * n * tok * cols, transcendentals=0
        ),
    )(*left_ops, *acts)


def wt_sum_kernel(n_cube, n_spread, part, *refs):
    n = n_cube + n_spread
    srcs, out, dsts, refs = refs[:n], refs[n], refs[n + 1 : 2 * n + 1], refs[2 * n + 1 :]
    recv, s_scatter, s_gather = refs[:3]
    me = lax.axis_index("wt")
    rows = recv.shape[1]
    greet(("wt", "seq") if n else ("wt",))
    first = scatter_start(part, recv, s_scatter, "wt")
    sems = refs[3:]
    cubes, sent, kept = [], [], []
    for i in range(n):
        if i < n_cube:
            cubes.append(cube_first(srcs[i], dsts[i], sems[2 * i]))
            kept.append(keep(srcs[i], dsts[i], sems[2 * i + 1]))
        else:
            new, own = spread(srcs[i], dsts[i], sems[2 * i], sems[2 * i + 1])
            sent += new
            kept.append(own)
    arrived(first)
    out[pl.ds(me * rows, rows)] = summed(part, recv, 0, rows, me * rows)
    second = gather_start(out, rows, s_gather, "wt")
    cubes2 = [cube_second(dsts[i], sems[2 * i], cubes[i]) for i in range(n_cube)]
    cubes3 = [cube_third(dsts[i], sems[2 * i], cubes2[i]) for i in range(n_cube)]
    for one, two, three in zip(cubes, cubes2, cubes3):
        cube_end(one, two, three)
    for copy in kept:
        copy.wait()
    arrived(second)
    arrived(sent)
    left(first)
    left(second)
    left(sent)


def wt_sum(part, blocks, srcs, n_wt, n_seq, ident):
    rows, cols = part.shape
    return pl.pallas_call(
        functools.partial(wt_sum_kernel, len(blocks), len(srcs)),
        out_shape=[jax.ShapeDtypeStruct((rows, cols), F32)]
        + [jax.ShapeDtypeStruct((n_seq,) + a.shape, BF16) for a in blocks]
        + [jax.ShapeDtypeStruct((n_seq, a.shape[0], a.shape[1] // n_seq), BF16) for a in srcs],
        in_specs=[VMEM] + [ANY] * len(blocks) + [VMEM] * len(srcs),
        out_specs=[VMEM] + [ANY] * len(blocks + srcs),
        scratch_shapes=[
            pltpu.VMEM((n_wt - 1, rows // n_wt, cols), F32),
            pair_sems(n_wt),
            pair_sems(n_wt),
        ]
        + [cube_sems(), pltpu.SemaphoreType.DMA] * len(blocks)
        + [pair_sems(n_seq), pltpu.SemaphoreType.DMA] * len(srcs),
        compiler_params=pltpu.CompilerParams(collective_id=ident, has_side_effects=True),
        cost_estimate=pl.CostEstimate(flops=10**5, bytes_accessed=10**6, transcendentals=0),
    )(part, *blocks, *srcs)


def second_norm_kernel(part, tok, gain, out, res, recv, s_scatter, s_gather):
    me = lax.axis_index("wt")
    rows = recv.shape[1]
    greet(("wt",))
    first = scatter_start(part, recv, s_scatter, "wt")
    arrived(first)
    row0 = me * rows

    def body(at):
        r = tok[pl.ds(at, 16)] + summed(part, recv, at, 16, row0)
        res[pl.ds(at, 16)] = r
        inverse = lax.rsqrt(jnp.mean(r * r, axis=-1, keepdims=True) + EPS)
        out[pl.ds(pl.multiple_of(row0 + at, 16), 16)] = (r * inverse * gain[...]).astype(BF16)

    step_rows(rows, 16, body)
    second = gather_start(out, rows, s_gather, "wt")
    arrived(second)
    left(first)
    left(second)


def second_norm(part, tok_own, gain, n_wt, ident):
    rows, cols = part.shape
    own = rows // n_wt
    return pl.pallas_call(
        second_norm_kernel,
        out_shape=[
            jax.ShapeDtypeStruct((rows, cols), BF16),
            jax.ShapeDtypeStruct((own, cols), F32),
        ],
        in_specs=[VMEM] * 3,
        out_specs=[VMEM] * 2,
        scratch_shapes=[
            pltpu.VMEM((n_wt - 1, own, cols), BF16),
            pair_sems(n_wt),
            pair_sems(n_wt),
        ],
        compiler_params=pltpu.CompilerParams(collective_id=ident, has_side_effects=True),
        cost_estimate=pl.CostEstimate(flops=10**6, bytes_accessed=10**8, transcendentals=0),
    )(part, tok_own, gain[None])


def norm_back_rows(grad, vals, gain):
    inverse = lax.rsqrt(jnp.mean(vals * vals, axis=-1, keepdims=True) + EPS)
    normed = vals * inverse
    scaled = grad * gain
    mean = jnp.mean(scaled * normed, axis=-1, keepdims=True)
    return inverse * (scaled - normed * mean), grad * normed


def second_back_kernel(part, res, cot, gain, out, d_res, gain_grad, recv, s_scatter, s_gather):
    me = lax.axis_index("wt")
    rows = recv.shape[1]
    greet(("wt",))
    first = scatter_start(part, recv, s_scatter, "wt")
    gain_grad[...] = jnp.zeros_like(gain_grad)
    arrived(first)
    row0 = me * rows

    def body(at):
        grad = summed(part, recv, at, 16, row0)
        back, prod = norm_back_rows(grad, res[pl.ds(at, 16)], gain[...])
        gain_grad[...] += prod[:8] + prod[8:]
        d = cot[pl.ds(at, 16)] + back
        d_res[pl.ds(at, 16)] = d
        out[pl.ds(pl.multiple_of(row0 + at, 16), 16)] = d.astype(BF16)

    step_rows(rows, 16, body)
    second = gather_start(out, rows, s_gather, "wt")
    arrived(second)
    left(first)
    left(second)


def second_back(part, res, cot_own, gain, n_wt, ident):
    rows, cols = part.shape
    own = rows // n_wt
    return pl.pallas_call(
        second_back_kernel,
        out_shape=[
            jax.ShapeDtypeStruct((rows, cols), BF16),
            jax.ShapeDtypeStruct((own, cols), F32),
            jax.ShapeDtypeStruct((8, cols), F32),
        ],
        in_specs=[VMEM] * 4,
        out_specs=[VMEM] * 3,
        scratch_shapes=[
            pltpu.VMEM((n_wt - 1, own, cols), BF16),
            pair_sems(n_wt),
            pair_sems(n_wt),
        ],
        compiler_params=pltpu.CompilerParams(collective_id=ident, has_side_effects=True),
        cost_estimate=pl.CostEstimate(flops=10**6, bytes_accessed=10**8, transcendentals=0),
    )(part, res, cot_own, gain[None])


def last_kernel(cube, part, tok, d_res, gain, gain_grad2, sel, stp, taps, decays, bias3, *refs):
    blocks, refs = refs[:cube], refs[cube:]
    if cube:
        cot_t, second_t, acts, refs = refs[0], refs[1], refs[2], refs[3:]
    out, sel_out, stp_out, chan_out, gains_out = refs[:5]
    wholes, refs = refs[5 : 5 + cube], refs[5 + cube :]
    if cube:
        grad_outs, refs = refs[:3], refs[3:]
        tile, s_tile, refs = refs[0], refs[1], refs[2:]
        width = tile.shape[2]
        tiles = acts.shape[1] // width

        def fetch(j, slot):
            columns = acts.at[:, pl.ds(pl.multiple_of(j * width, width), width)]
            return pltpu.make_async_copy(columns, tile.at[slot], s_tile.at[slot])

        def one_tile(j, carry):
            slot = lax.rem(j, 2)

            @pl.when(j + 1 < tiles)
            def _():
                fetch(j + 1, 1 - slot).start()

            fetch(j, slot).wait()
            columns = pl.ds(pl.multiple_of(j * UNITS, UNITS), UNITS)
            for i, left_op in enumerate((cot_t, second_t, second_t)):
                grad_outs[i][:, columns] = jnp.dot(
                    left_op[...],
                    tile[slot, :, i * UNITS : (i + 1) * UNITS],
                    preferred_element_type=F32,
                )
            return carry

        fetch(0, 0).start()
    recv, recv_sel, recv_stp, recv_chan, pack, gain_buf, recv_gz, recv_gs = refs[:8]
    s_scatter, s_gather, s_sel, s_stp, s_chan, s_cg, s_gz, s_gs = refs[8:16]
    me, n_wt = lax.axis_index("wt"), lax.axis_size("wt")
    seq, n_seq = lax.axis_index("seq"), lax.axis_size("seq")
    rows = recv.shape[1]
    greet(("wt", "seq"))
    first = scatter_start(part, recv, s_scatter, "wt")
    share = -(-(KC + NS + 3) // n_seq)
    lines = [(taps, i) for i in range(KC)] + [(decays, i) for i in range(NS)]
    lines += [(bias3, i) for i in range(3)]
    for at, (ref, i) in enumerate(lines):
        pack[at // share, at % share : at % share + 1] = ref[i : i + 1]
    smalls = []
    for src, dst, sems in ((sel, recv_sel, s_sel), (stp, recv_stp, s_stp), (pack, recv_chan, s_chan)):
        for k in range(1, n_seq):
            peer = lax.rem(seq + k, n_seq)
            smalls.append(send(src.at[peer], dst.at[k - 1], sems, k - 1, "seq", peer))
    cubes = []
    for i in range(cube):
        s_cube, s_own = refs[16 + 2 * i : 18 + 2 * i]
        cubes.append([cube_first(blocks[i], wholes[i], s_cube), s_cube, wholes[i]])
        cubes[-1].append(keep(blocks[i], wholes[i], s_own))
    if cube:
        lax.fori_loop(0, tiles // 2, one_tile, 0)
    arrived(smalls)
    for src, recv_one, one_out in ((sel, recv_sel, sel_out), (stp, recv_stp, stp_out)):
        total = src[seq].astype(F32)
        for k in range(n_seq - 1):
            total = total + recv_one[k].astype(F32)
        one_out[...] = total
    total = pack[seq]
    for k in range(n_seq - 1):
        total = total + recv_chan[k]
    chan_out[seq] = total
    mine = chan_out.at[seq]
    chans = [
        send(mine, mine, s_cg, k - 1, "seq", lax.rem(seq + k, n_seq)) for k in range(1, n_seq)
    ]
    arrived(first)
    row0 = me * rows
    gain_buf[...] = jnp.zeros_like(gain_buf)

    def body(at):
        grad = summed(part, recv, at, 16, row0)
        back, prod = norm_back_rows(grad, tok[pl.ds(at, 16)], gain[...])
        gain_buf[...] += prod[:8] + prod[8:]
        out[pl.ds(pl.multiple_of(row0 + at, 16), 16)] = (d_res[pl.ds(at, 16)] + back).astype(BF16)

    step_rows(rows, 16, body)
    second = gather_start(out, rows, s_gather, "wt")
    high = recv_gz.shape[1] // 2
    for i, grad in enumerate((gain_buf, gain_grad2)):
        line = jnp.sum(grad[...], axis=0, keepdims=True)
        for t in range(high):
            recv_gz[me, i * high + t : i * high + t + 1] = line[:, t * 128 : (t + 1) * 128]
    mine_z = recv_gz.at[me]
    zs = [send(mine_z, mine_z, s_gz, k - 1, "wt", lax.rem(me + k, n_wt)) for k in range(1, n_wt)]
    cubes2 = [cube_second(whole, sems, one) for one, sems, whole, _ in cubes]
    if cube:
        lax.fori_loop(tiles // 2, tiles, one_tile, 0)
    arrived(zs)
    total = recv_gz[0]
    for pos in range(1, n_wt):
        total = total + recv_gz[pos]
    recv_gs[seq] = total
    mine_s = recv_gs.at[seq]
    ss = [
        send(mine_s, mine_s, s_gs, k - 1, "seq", lax.rem(seq + k, n_seq)) for k in range(1, n_seq)
    ]
    cubes3 = [cube_third(whole, sems, two) for (_, sems, whole, _), two in zip(cubes, cubes2)]
    arrived(ss)
    total = recv_gs[0]
    for pos in range(1, n_seq):
        total = total + recv_gs[pos]
    gains_out[...] = total
    arrived(chans)
    for (one, _, _, kept), two, three in zip(cubes, cubes2, cubes3):
        cube_end(one, two, three)
        kept.wait()
    arrived(second)
    for group in (first, second, smalls, chans, zs, ss):
        left(group)


def last(part, tok_own, d_res, gain, gain_grad2, sel, stp, taps, decays, bias3, blocks, more, n_wt, n_seq, ident):
    rows, cols = part.shape
    own = rows // n_wt
    chan = taps.shape[1]
    if more:
        deep, tok_all = more[0].shape
        units = more[2].shape[1] // 3
    return pl.pallas_call(
        functools.partial(last_kernel, len(blocks)),
        out_shape=[
            jax.ShapeDtypeStruct((rows, cols), BF16),
            jax.ShapeDtypeStruct(sel.shape[1:], F32),
            jax.ShapeDtypeStruct(stp.shape[1:], F32),
            jax.ShapeDtypeStruct((n_seq, 8, chan), F32),
            jax.ShapeDtypeStruct((2 * cols // 128, 128), F32),
        ]
        + [jax.ShapeDtypeStruct((n_seq,) + a.shape, BF16) for a in blocks]
        + ([jax.ShapeDtypeStruct((deep, units), F32)] * 3 if more else []),
        in_specs=[VMEM] * 10 + [ANY] * len(blocks) + ([VMEM, VMEM, ANY] if more else []),
        out_specs=[VMEM] * 5 + [ANY] * len(blocks) + ([VMEM] * 3 if more else []),
        scratch_shapes=(
            [pltpu.VMEM((2, tok_all, 3 * UNITS), BF16), pltpu.SemaphoreType.DMA((2,))]
            if more
            else []
        )
        + [
            pltpu.VMEM((n_wt - 1, own, cols), BF16),
            pltpu.VMEM((n_seq - 1,) + sel.shape[1:], BF16),
            pltpu.VMEM((n_seq - 1,) + stp.shape[1:], BF16),
            pltpu.VMEM((n_seq - 1, 8, chan), F32),
            pltpu.VMEM((n_seq, 8, chan), F32),
            pltpu.VMEM((8, cols), F32),
            pltpu.VMEM((n_wt, 2 * cols // 128, 128), F32),
            pltpu.VMEM((n_seq, 2 * cols // 128, 128), F32),
            pair_sems(n_wt),
            pair_sems(n_wt),
            pair_sems(n_seq),
            pair_sems(n_seq),
            pair_sems(n_seq),
            pair_sems(n_seq),
            pair_sems(n_wt),
            pair_sems(n_seq),
        ]
        + [cube_sems(), pltpu.SemaphoreType.DMA] * len(blocks),
        compiler_params=pltpu.CompilerParams(
            collective_id=ident, has_side_effects=True, vmem_limit_bytes=40 * MIB
        ),
        cost_estimate=pl.CostEstimate(flops=10**6, bytes_accessed=10**8, transcendentals=0),
    )(part, tok_own, d_res, gain[None], gain_grad2, sel, stp, taps, decays, bias3, *blocks, *more)


def load(ref):
    return tuple(ref[n] for n in range(NS))


def store(ref, values):
    for n in range(NS):
        ref[n] = values[n]


def fold(mine, box, recv, a2, carried, backward):
    n, me = lax.axis_size("seq"), lax.axis_index("seq")
    carried[...] = jnp.zeros_like(carried)
    for k in range(n - 1, 0, -1):

        @pl.when((me + k < n) if backward else (me >= k))
        def _():
            giver = me + k if backward else me - k
            remote(mine, recv.at[k - 1], box, k - 1, "seq", giver).wait_recv()
            through = recv[k - 1, NS]
            for s in range(NS):
                carried[s] = (
                    jnp.exp2(a2[s] * through) * carried[s] + recv[k - 1, s]
                )


def hand_on(mine, recv, box, backward):
    n, me = lax.axis_size("seq"), lax.axis_index("seq")
    for k in range(1, n):

        @pl.when((me >= k) if backward else (me + k < n))
        def _():
            peer = me - k if backward else me + k
            send(mine, recv.at[k - 1], box, k - 1, "seq", peer)


def handed(mine, recv, box, backward):
    n, me = lax.axis_size("seq"), lax.axis_index("seq")
    for k in range(1, n):

        @pl.when((me >= k) if backward else (me + k < n))
        def _():
            peer = me - k if backward else me + k
            remote(mine, recv.at[k - 1], box, k - 1, "seq", peer).wait_send()


def fwd_kernel(sa, dx, w, r, a2, y, h0, mine, recv, box):
    tok = sa.shape[0]
    greet(("seq",))

    def end(t, carry):
        s, d = sa[t], dx[t]
        h, total = carry
        return (
            tuple(jnp.exp2(s * a2[n]) * h[n] + w[t, n] * d for n in range(NS)),
            total + s,
        )

    zero = jnp.zeros(sa.shape[1:], F32)
    ends, total = lax.fori_loop(0, tok, end, ((zero,) * NS, zero), unroll=4)
    store(mine, ends)
    mine[NS] = total
    hand_on(mine, recv, box, False)
    fold(mine, box, recv, a2, h0, False)

    def body(t, h):
        s, d = sa[t], dx[t]
        new, sums = [], [None] * 4
        for n in range(NS):
            hn = jnp.exp2(s * a2[n]) * h[n] + w[t, n] * d
            new.append(hn)
            c = r[t, n] * hn
            sums[n % 4] = c if sums[n % 4] is None else sums[n % 4] + c
        y[t] = (sums[0] + sums[1]) + (sums[2] + sums[3])
        return tuple(new)

    lax.fori_loop(0, tok, body, load(h0), unroll=4)
    handed(mine, recv, box, False)


def fwd_scan(sa, dx, w, r, a2, n_seq, ident):
    tok, high = sa.shape[:2]
    return pl.pallas_call(
        fwd_kernel,
        out_shape=[
            jax.ShapeDtypeStruct((tok, high, 128), F32),
            jax.ShapeDtypeStruct((NS, high, 128), F32),
        ],
        in_specs=[VMEM, VMEM, SMEM, SMEM, VMEM],
        out_specs=[VMEM] * 2,
        scratch_shapes=[
            pltpu.VMEM((NS + 1, high, 128), F32),
            pltpu.VMEM((n_seq - 1, NS + 1, high, 128), F32),
            pair_sems(n_seq),
        ],
        compiler_params=pltpu.CompilerParams(
            collective_id=ident, has_side_effects=True, vmem_limit_bytes=32 * MIB
        ),
        cost_estimate=pl.CostEstimate(
            flops=10**8, bytes_accessed=8 * 10**7, transcendentals=2 * tok * NS * 1024
        ),
    )(sa, dx, w, r, a2)


def bwd_kernel(
    sa, dx, w, r, do, a2, h0, part, res,
    along, ds2, grad_a, pw, pr, out,
    hs, qw, qr, g0, mine, recv, recv_z, box, s_scatter, s_gather,
):
    tok = sa.shape[0]
    chunk = qw.shape[0] // (NS * 8)
    greet(("wt", "seq"))
    first = scatter_start(part, recv_z, s_scatter, "wt")

    def end(i, carry):
        t = tok - 1 - i
        s, d = sa[t], do[t]
        g, total = carry
        return (
            tuple(jnp.exp2(s * a2[n]) * (g[n] + r[t, n] * d) for n in range(NS)),
            total + s,
        )

    zero = jnp.zeros(sa.shape[1:], F32)
    ends, total = lax.fori_loop(0, tok, end, ((zero,) * NS, zero), unroll=4)
    store(mine, ends)
    mine[NS] = total
    hand_on(mine, recv, box, True)

    def again(t, h):
        s, d = sa[t], dx[t]
        new = []
        for n in range(NS):
            hs[t, n] = h[n]
            new.append(jnp.exp2(s * a2[n]) * h[n] + w[t, n] * d)
        return tuple(new)

    lax.fori_loop(0, tok, again, load(h0), unroll=2)

    arrived(first)
    me = lax.axis_index("wt")
    rows = recv_z.shape[1]
    row0 = me * rows

    def block_rows(at):
        total = res[pl.ds(at, 16)] + summed(part, recv_z, at, 16, row0)
        out[pl.ds(pl.multiple_of(row0 + at, 16), 16)] = total.astype(BF16)

    step_rows(rows, 16, block_rows)
    second = gather_start(out, rows, s_gather, "wt")

    fold(mine, box, recv, a2, g0, True)
    grad_a[...] = jnp.zeros_like(grad_a)

    def one_chunk(j, g):
        base = (tok // chunk - 1 - j) * chunk

        def body(i, g):
            at = chunk - 1 - i
            t = base + at
            s, d, o = sa[t], dx[t], do[t]
            al = d2 = None
            new = []
            for n in range(NS):
                hp = hs[t, n]
                f = jnp.exp2(s * a2[n])
                hn = f * hp + w[t, n] * d
                gn = r[t, n] * o + g[n]
                adj = f * gn
                new.append(adj)
                th = adj * hp
                grad_a[n] += th * s
                x = w[t, n] * gn
                al = x if al is None else al + x
                x = a2[n] * th
                d2 = x if d2 is None else d2 + x
                row = pl.multiple_of((at * NS + n) * 8, 8)
                qw[pl.ds(row, 8), :] = gn * d
                qr[pl.ds(row, 8), :] = hn * o
            along[t] = al
            ds2[t] = d2
            return tuple(new)

        g = lax.fori_loop(0, chunk, body, g)

        def lanes(i, carry):
            for q, p in ((qw, pw), (qr, pr)):
                acc = q[pl.ds(i * NS * 8, NS, stride=8), :]
                for s in range(1, 8):
                    acc = acc + q[pl.ds(i * NS * 8 + s, NS, stride=8), :]
                p[base + i] = acc
            return carry

        lax.fori_loop(0, chunk, lanes, 0, unroll=4)
        return g

    lax.fori_loop(0, tok // chunk, one_chunk, load(g0))
    handed(mine, recv, box, True)
    arrived(second)
    left(first)
    left(second)


def bwd_scan(sa, dx, w, r, do, a2, h0, part, res, n_wt, n_seq, ident):
    tok, high = sa.shape[:2]
    rows, cols = part.shape
    chunk = 32
    return pl.pallas_call(
        bwd_kernel,
        out_shape=[
            jax.ShapeDtypeStruct((tok, high, 128), F32),
            jax.ShapeDtypeStruct((tok, high, 128), F32),
            jax.ShapeDtypeStruct((NS, high, 128), F32),
            jax.ShapeDtypeStruct((tok, NS, 128), F32),
            jax.ShapeDtypeStruct((tok, NS, 128), F32),
            jax.ShapeDtypeStruct((rows, cols), BF16),
        ],
        in_specs=[VMEM, VMEM, SMEM, SMEM] + [VMEM] * 5,
        out_specs=[VMEM] * 6,
        scratch_shapes=[
            pltpu.VMEM((tok, NS, high, 128), F32),
            pltpu.VMEM((chunk * NS * 8, 128), F32),
            pltpu.VMEM((chunk * NS * 8, 128), F32),
            pltpu.VMEM((NS, high, 128), F32),
            pltpu.VMEM((NS + 1, high, 128), F32),
            pltpu.VMEM((n_seq - 1, NS + 1, high, 128), F32),
            pltpu.VMEM((n_wt - 1, rows // n_wt, cols), BF16),
            pair_sems(n_seq),
            pair_sems(n_wt),
            pair_sems(n_wt),
        ],
        compiler_params=pltpu.CompilerParams(
            collective_id=ident, has_side_effects=True, vmem_limit_bytes=56 * MIB
        ),
        cost_estimate=pl.CostEstimate(
            flops=10**8, bytes_accessed=15 * 10**7, transcendentals=3 * tok * NS * 1024
        ),
    )(sa, dx, w, r, do, a2, h0, part, res)


def gather(block):
    return lax.all_gather(block, "seq", axis=0, tiled=True)


def from_behind(block, axis, distance):
    devices = range(lax.axis_size(axis))
    route = [(i - distance, i) for i in devices if i - distance in devices]
    return lax.ppermute(block, axis, route)


def contract(left_op, right_op, pattern):
    return jnp.einsum(pattern, left_op, right_op, preferred_element_type=F32)


def silu_slope(values):
    sigma = jax.nn.sigmoid(values)
    return sigma * (1.0 + values * (1.0 - sigma))


def tiles(rows):
    return rows.reshape(rows.shape[0], rows.shape[1] // 128, 128)


def flat(rows):
    return rows.reshape(rows.shape[0], rows.shape[1] * rows.shape[2])


def local(
    tokens,
    cotangent,
    doc_start,
    premix_gain,
    inner_proj,
    switch_proj,
    conv_taps,
    conv_bias,
    select_proj,
    step_proj,
    step_bias,
    decay_log,
    skip_gain,
    mixer_out,
    preffn_gain,
    ffn_gate,
    ffn_up,
    ffn_down,
):
    tok_count, width = tokens.shape
    chan = inner_proj.shape[1]
    units = ffn_gate.shape[1]
    edge = KC - 1
    n_seq, n_wt = lax.axis_size("seq"), lax.axis_size("wt")
    z = lax.axis_index("wt")
    own = tok_count // n_wt
    cube = n_seq == 8 and n_seq * tok_count <= width

    token_vals = tokens.astype(F32)
    first_inv = lax.rsqrt(jnp.mean(token_vals * token_vals, axis=-1, keepdims=True) + EPS)
    first_in = (token_vals * first_inv * premix_gain).astype(BF16)
    rows_sel, rows_step = select_proj.shape[0], step_proj.shape[0]
    if cube:
        fill = jnp.zeros((-(rows_sel + rows_step) % 32, chan), BF16)
        small = jnp.concatenate([select_proj, step_proj, fill], axis=0)
        w_mixer, w_small, cot_f, first_f = first_gather(
            jnp.concatenate([inner_proj, switch_proj, mixer_out], axis=1),
            small, cotangent, first_in, n_wt, n_seq, 7,
        )
        w_mixer = w_mixer.reshape(width, 3 * chan)
    else:
        w_mixer = gather(jnp.concatenate([inner_proj, switch_proj, mixer_out], axis=1))
        w_small = lax.all_gather(jnp.concatenate([select_proj, step_proj], axis=0), "seq", axis=0)
    w_first, w_mix = w_mixer[:, : 2 * chan], w_mixer[:, 2 * chan :]
    w_select = w_small[:, :rows_sel].reshape(-1, chan)
    w_step = w_small[:, rows_sel : rows_sel + rows_step].reshape(-1, chan)
    ffn_own = jnp.concatenate([ffn_gate, ffn_up, ffn_down], axis=1)
    ffn_own, w_small = lax.optimization_barrier((ffn_own, w_small))
    w_all = gather(ffn_own)
    both = contract(first_in, w_first, "td,dc->tc")
    inner_act = both[:, :chan].astype(BF16)
    switch = both[:, chan:]

    counts = jnp.cumsum(doc_start)
    last_count = counts[-1]
    head_keep = (counts == 0).astype(F32)
    tail_keep = (counts == last_count).astype(F32)
    tail_rows = jnp.where(
        tail_keep[-edge:, None] > 0, inner_act[-edge:], jnp.zeros_like(inner_act[-edge:])
    )
    prev_rows = from_behind(tail_rows, "seq", 1)
    extended = jnp.concatenate([prev_rows, inner_act], axis=0).astype(F32)
    ext_counts = jnp.concatenate([jnp.zeros((edge,), jnp.int32), counts])
    conv_out = jnp.zeros((tok_count, chan), F32) + conv_bias[None, :]
    for offset in range(KC):
        same_doc = (counts == ext_counts[edge - offset : edge - offset + tok_count]).astype(F32)
        conv_out = (
            conv_out
            + conv_taps[offset][None, :]
            * extended[edge - offset : edge - offset + tok_count]
            * same_doc[:, None]
        )
    mixed_in = jax.nn.silu(conv_out).astype(BF16)
    mixed_f = mixed_in.astype(F32)
    (select,) = wt_sum(contract(w_select, mixed_in, "jc,tc->jt"), (), (), n_wt, n_seq, 0)
    low_rank = select[:R].astype(BF16)
    write_vec = select[R : R + NS].T
    read_vec = select[R + NS :].T
    step_pre = contract(low_rank, w_step, "rt,rc->tc") + step_bias[None, :]
    step_size = jax.nn.softplus(step_pre)
    decay = -jnp.exp(decay_log)
    decay2 = tiles(decay * LOG2E)
    step_a = tiles(jnp.where(doc_start[:, None] > 0, FAR, step_size))
    drive = tiles(step_size * mixed_f)
    scan_out, carried_in = fwd_scan(step_a, drive, write_vec, read_vec, decay2, n_seq, 1)

    scanned = flat(scan_out) + skip_gain[None, :] * mixed_f
    switch_act = jax.nn.silu(switch)
    gated = (scanned * switch_act).astype(BF16)
    mix_part = contract(gated, w_mix, "tc,dc->td").astype(BF16)
    tokens_own = lax.dynamic_slice_in_dim(tokens, z * own, own, 0).astype(F32)
    cot_own = lax.dynamic_slice_in_dim(cotangent, z * own, own, 0).astype(F32)
    second_in, residual = second_norm(mix_part, tokens_own, preffn_gain, n_wt, 2)
    acts, down_part, d_second = ffn(second_in, cotangent, w_all)
    d_branch, d_residual, grad_preffn = second_back(
        d_second, residual, cot_own, preffn_gain, n_wt, 3
    )
    d_gated = contract(d_branch, w_mix, "td,dc->tc")
    d_scanned = d_gated * switch_act
    d_switch = (d_gated * scanned * silu_slope(switch)).astype(BF16)
    grad_skip = jnp.sum(d_scanned * mixed_f, axis=0)
    along, through_sum, grad_decay, write_lanes, read_lanes, block_out = bwd_scan(
        step_a, drive, write_vec, read_vec, tiles(d_scanned), decay2, carried_in,
        down_part, residual, n_wt, n_seq, 4,
    )
    along = flat(along)
    d_step = along * mixed_f + flat(through_sum) * (1.0 / LOG2E)
    grad_decay_log = flat(grad_decay) * decay
    d_pre = d_step * jax.nn.sigmoid(step_pre)
    grad_step_bias = jnp.sum(d_pre, axis=0)
    d_pre_low = d_pre.astype(BF16)
    pad_rows = lambda v: jnp.pad(
        v.reshape(n_seq, -1, tok_count), ((0, 0), (0, -(v.shape[0] // n_seq) % 16), (0, 0))
    ).reshape(-1, tok_count)
    grad_step = contract(pad_rows(low_rank), d_pre_low, "rt,tc->rc").astype(BF16)
    d_select, *gathered = wt_sum(
        jnp.concatenate(
            [
                contract(w_step, d_pre_low, "rc,tc->rt"),
                jnp.sum(write_lanes, axis=-1).T,
                jnp.sum(read_lanes, axis=-1).T,
            ],
            axis=0,
        ),
        (gated,) if cube else (),
        (second_in, d_branch) if cube else (),
        n_wt,
        n_seq,
        5,
    )
    d_select = d_select.astype(BF16)
    grad_select = contract(pad_rows(d_select), mixed_in, "jt,tc->jc").astype(BF16)
    d_mixed = (
        along * step_size
        + skip_gain[None, :] * d_scanned
        + contract(d_select, w_select, "jt,jc->tc")
    )
    d_conv = (d_mixed * silu_slope(conv_out)).astype(BF16)
    d_conv_f = d_conv.astype(F32)
    grad_conv_bias = jnp.sum(d_conv_f, axis=0)
    head_rows = jnp.where(head_keep[:edge, None] > 0, d_conv[:edge], jnp.zeros_like(d_conv[:edge]))
    next_rows = from_behind(head_rows, "seq", -1)
    ext_grad = jnp.concatenate([d_conv, next_rows], axis=0).astype(F32)
    ext_after = jnp.concatenate([counts, jnp.zeros((edge,), jnp.int32) + last_count])
    d_inner = jnp.zeros_like(d_conv_f)
    taps_rows = []
    for offset in range(KC):
        same_doc = (counts == ext_counts[edge - offset : edge - offset + tok_count]).astype(F32)
        taps_rows.append(
            jnp.sum(
                d_conv_f * extended[edge - offset : edge - offset + tok_count] * same_doc[:, None],
                axis=0,
            )
        )
        later_same = (ext_after[offset : offset + tok_count] == counts).astype(F32)
        d_inner = (
            d_inner
            + conv_taps[offset][None, :]
            * ext_grad[offset : offset + tok_count]
            * later_same[:, None]
        )
    d_inner_low = d_inner.astype(BF16)
    d_first = contract(
        jnp.concatenate([d_inner_low, d_switch], axis=1), w_first, "tc,dc->td"
    ).astype(BF16)
    more = ()
    if cube:
        line_up = lambda v: v.reshape(n_seq * tok_count, v.shape[-1])
        gated_all, second_f, branch_f = map(line_up, gathered)
        more = (line_up(cot_f).T, second_f.T, gather(acts))
    tokens_grad, out_select, out_step, by_chan, gains, *others = last(
        d_first, tokens_own, d_residual, premix_gain, grad_preffn,
        grad_select.reshape(n_seq, -1, chan), grad_step.reshape(n_seq, -1, chan),
        jnp.stack(taps_rows, axis=0), grad_decay_log,
        jnp.stack([grad_conv_bias, grad_step_bias, grad_skip]),
        (d_switch, d_inner_low) if cube else (), more, n_wt, n_seq, 6,
    )
    share = -(-(KC + NS + 3) // n_seq)
    by_chan = by_chan[:, :share].reshape(n_seq * share, chan)
    gains = gains.reshape(2, width)
    if cube:
        out_down, out_gate, out_up = others[2:]
        out_mix, out_switch, out_inner = grads(
            (branch_f.T, line_up(first_f).T),
            (0, 1, 1),
            (gated_all, line_up(others[0]), line_up(others[1])),
        )
    else:
        scatter = lambda v: lax.psum_scatter(v, "seq", scatter_dimension=0, tiled=True)
        by_unit = acts.reshape(tok_count, -1, 3, UNITS)
        hidden, d_gate, d_up = [by_unit[:, :, i].reshape(tok_count, units) for i in range(3)]
        out_down = scatter(contract(cotangent, hidden, "td,tf->df"))
        out_gate = scatter(contract(second_in, d_gate, "td,tf->df"))
        out_up = scatter(contract(second_in, d_up, "td,tf->df"))
        out_mix = scatter(contract(d_branch, gated, "td,tc->dc"))
        out_switch = scatter(contract(first_in, d_switch, "td,tc->dc"))
        out_inner = scatter(contract(first_in, d_inner_low, "td,tc->dc"))
    return (
        block_out,
        tokens_grad,
        gains[0],
        out_inner,
        out_switch,
        by_chan[:KC],
        by_chan[KC + NS],
        out_select[:rows_sel],
        out_step[:rows_step],
        by_chan[KC + NS + 1],
        by_chan[KC : KC + NS],
        by_chan[KC + NS + 2],
        out_mix,
        gains[1],
        out_gate,
        out_up,
        out_down,
    )


def solution(mesh):
    placed = (
        P("seq", None),
        P("seq", None),
        P("seq"),
        P(),
        P("seq", "wt"),
        P("seq", "wt"),
        P(None, "wt"),
        P("wt"),
        P("seq", "wt"),
        P("seq", "wt"),
        P("wt"),
        P(None, "wt"),
        P("wt"),
        P("seq", "wt"),
        P(),
        P("seq", "wt"),
        P("seq", "wt"),
        P("seq", "wt"),
    )
    return jax.shard_map(
        local,
        mesh=mesh,
        in_specs=placed,
        out_specs=(
            P("seq", None),
            P("seq", None),
            P(),
            P("seq", "wt"),
            P("seq", "wt"),
            P(None, "wt"),
            P("wt"),
            P("seq", "wt"),
            P("seq", "wt"),
            P("wt"),
            P(None, "wt"),
            P("wt"),
            P("seq", "wt"),
            P(),
            P("seq", "wt"),
            P("seq", "wt"),
            P("seq", "wt"),
        ),
        check_vma=False,
    )
```

```python
import functools

import jax
import jax.numpy as jnp
from jax import lax
from jax.experimental import pallas as pl
from jax.experimental.pallas import tpu as pltpu
from jax.sharding import PartitionSpec as P

NS = 16
R = 128
KC = 4
EPS = 1e-05
F32 = jnp.float32
BF16 = jnp.bfloat16
LOG2E = 1.4426950408889634
FAR = 1e30
MESH = pl.DeviceIdType.MESH
VMEM = pl.BlockSpec(memory_space=pltpu.VMEM)
SMEM = pl.BlockSpec(memory_space=pltpu.SMEM)
ANY = pl.BlockSpec(memory_space=pl.ANY)
VMEM_BYTES = 60 * 2**20


def greet(axes):
    barrier = pltpu.get_barrier_semaphore()
    total = 0
    for axis in axes:
        n, me = lax.axis_size(axis), lax.axis_index(axis)
        for k in range(1, n):
            pl.semaphore_signal(
                barrier, inc=1, device_id={axis: lax.rem(me + k, n)}, device_id_type=MESH
            )
        total += n - 1
    pl.semaphore_wait(barrier, total)


def remote(src, dst, sems, slot, axis, peer):
    return pltpu.make_async_remote_copy(
        src_ref=src,
        dst_ref=dst,
        send_sem=sems.at[0, slot],
        recv_sem=sems.at[1, slot],
        device_id={axis: peer},
        device_id_type=MESH,
    )


def send(src, dst, sems, slot, axis, peer):
    copy = remote(src, dst, sems, slot, axis, peer)
    copy.start()
    return copy


def scatter_start(part, recv, sems, axis):
    n, me = lax.axis_size(axis), lax.axis_index(axis)
    rows = recv.shape[1]
    copies = []
    for k in range(1, n):
        peer = lax.rem(me + k, n)
        copies.append(
            send(part.at[pl.ds(peer * rows, rows)], recv.at[k - 1], sems, k - 1, axis, peer)
        )
    return copies


def gather_start(whole, rows, sems, axis):
    n, me = lax.axis_size(axis), lax.axis_index(axis)
    mine = whole.at[pl.ds(me * rows, rows)]
    return [send(mine, mine, sems, k - 1, axis, lax.rem(me + k, n)) for k in range(1, n)]


def arrived(copies):
    for copy in copies:
        copy.wait_recv()


def left(copies):
    for copy in copies:
        copy.wait_send()


def pair_sems(n):
    return pltpu.SemaphoreType.DMA((2, n - 1))


def summed(part, recv, at, step, row0):
    total = part[pl.ds(row0 + at, step)].astype(F32)
    for k in range(recv.shape[0]):
        total = total + recv[k, pl.ds(at, step)].astype(F32)
    return total


def step_rows(rows, step, body):
    def run(i, carry):
        body(pl.multiple_of(i * step, step))
        return carry

    lax.fori_loop(0, rows // step, run, 0)


def mates():
    z = lax.axis_index("wt")
    mate = z + 1 - 2 * lax.rem(z, 2)
    return z, mate, lax.rem(z + 2, 4), lax.rem(mate + 2, 4)


def line_scatter_start(part, recv, sems):
    if lax.axis_size("wt") != 4:
        return scatter_start(part, recv, sems, "wt")
    rows = recv.shape[1]
    _, mate, _, far_mate = mates()
    return [
        send(part.at[pl.ds(far_mate * rows, rows)], recv.at[0], sems, 0, "wt", mate),
        send(part.at[pl.ds(mate * rows, rows)], recv.at[1], sems, 1, "wt", mate),
    ]


def line_scatter_mid(part, recv, pend, sems, copies):
    if lax.axis_size("wt") != 4:
        return copies
    rows = recv.shape[1]
    _, _, far, _ = mates()
    copies[0].wait_recv()

    def body(at):
        mine = part[pl.ds(pl.multiple_of(far * rows + at, 16), 16)].astype(F32)
        pend[pl.ds(at, 16)] = (mine + recv[0, pl.ds(at, 16)].astype(F32)).astype(BF16)

    step_rows(rows, 16, body)
    return copies + [send(pend, recv.at[2], sems, 2, "wt", far)]


def line_scatter_end(copies):
    if lax.axis_size("wt") != 4:
        arrived(copies)
    else:
        arrived(copies[1:])


def line_summed(part, recv, at, step, row0):
    if lax.axis_size("wt") != 4:
        return summed(part, recv, at, step, row0)
    total = part[pl.ds(row0 + at, step)].astype(F32)
    return total + recv[1, pl.ds(at, step)].astype(F32) + recv[2, pl.ds(at, step)].astype(F32)


def line_gather_start(whole, rows, sems):
    if lax.axis_size("wt") != 4:
        return gather_start(whole, rows, sems, "wt")
    z, mate, far, _ = mates()
    mine = whole.at[pl.ds(z * rows, rows)]
    return [send(mine, mine, sems, 0, "wt", far), send(mine, mine, sems, 1, "wt", mate)]


def line_gather_mid(whole, rows, sems, copies):
    if lax.axis_size("wt") != 4:
        return copies
    _, mate, far, _ = mates()
    copies[0].wait_recv()
    piece = whole.at[pl.ds(far * rows, rows)]
    return copies + [send(piece, piece, sems, 2, "wt", mate)]


def line_gather_end(copies):
    if lax.axis_size("wt") != 4:
        arrived(copies)
    else:
        arrived(copies[1:])


def flips():
    seq = lax.axis_index("seq")
    core, x, y = lax.rem(seq, 2), lax.rem(seq // 2, 2), seq // 4

    def at(fy, fx, fc):
        return (
            (1 - y if fy else y) * 4 + (1 - x if fx else x) * 2 + (1 - core if fc else core)
        )

    return at


def cube_sems():
    return pltpu.SemaphoreType.DMA((2, 9))


def cube_first(block, whole, sems):
    at = flips()
    mine = whole.at[at(0, 0, 0)]
    return [
        send(block, mine, sems, 0, "seq", at(0, 1, 0)),
        send(block, mine, sems, 1, "seq", at(1, 0, 0)),
        send(block, mine, sems, 2, "seq", at(0, 0, 1)),
    ]


def keep(block, whole, sem):
    copy = pltpu.make_async_copy(block, whole.at[lax.axis_index("seq")], sem)
    copy.start()
    return copy


def spread(src, dst, sems, own_sem):
    seq, n_seq = lax.axis_index("seq"), lax.axis_size("seq")
    piece = dst.shape[2]

    def columns(peer):
        return src.at[:, pl.ds(pl.multiple_of(peer * piece, piece), piece)]

    out = []
    for k in range(1, n_seq):
        peer = lax.rem(seq + k, n_seq)
        out.append(send(columns(peer), dst.at[seq], sems, k - 1, "seq", peer))
    return out, keep(columns(seq), dst, own_sem)


def cube_second(whole, sems, first):
    at = flips()
    half = whole.shape[1] // 2
    first[0].wait_recv()
    block = whole.at[at(0, 1, 0)]
    top = block.at[pl.ds(0, half)]
    sent = [
        send(top, top, sems, 3, "seq", at(1, 0, 0)),
        send(block, block, sems, 5, "seq", at(0, 0, 1)),
    ]
    first[1].wait_recv()
    block = whole.at[at(1, 0, 0)]
    low = block.at[pl.ds(half, half)]
    sent += [
        send(low, low, sems, 4, "seq", at(0, 1, 0)),
        send(block, block, sems, 6, "seq", at(0, 0, 1)),
    ]
    return sent


def cube_third(whole, sems, second):
    at = flips()
    half = whole.shape[1] // 2
    block = whole.at[at(1, 1, 0)]
    sent = []
    for slot, came in ((0, second[0]), (1, second[2])):
        came.wait_recv()
        piece = block.at[pl.ds(slot * half, half)]
        sent.append(send(piece, piece, sems, 7 + slot, "seq", at(0, 0, 1)))
    return sent


def cube_end(first, second, third):
    first[2].wait_recv()
    second[1].wait_recv()
    second[3].wait_recv()
    arrived(third)
    for group in (first, second, third):
        left(group)


def share(src, dst, sems, own_sem):
    seq, n_seq, z = lax.axis_index("seq"), lax.axis_size("seq"), lax.axis_index("wt")
    own, piece = dst.shape[2:]
    rows = src.at[pl.ds(pl.multiple_of(z * own, own), own)]

    def columns(peer):
        return rows.at[:, pl.ds(pl.multiple_of(peer * piece, piece), piece)]

    sent = []
    for k in range(1, n_seq):
        peer = lax.rem(seq + k, n_seq)
        sent.append(send(columns(peer), dst.at[seq, z], sems, k - 1, "seq", peer))
    kept = pltpu.make_async_copy(columns(seq), dst.at[seq, z], own_sem)
    kept.start()
    return sent, kept


def pass_along(dst, sems):
    z, n_wt = lax.axis_index("wt"), lax.axis_size("wt")
    lines = dst.at[:, z]
    return [send(lines, lines, sems, k - 1, "wt", lax.rem(z + k, n_wt)) for k in range(1, n_wt)]


def first_kernel(
    mixer, small, cot, tok, gain, w_mixer, w_small, cot_f, act_f, act,
    s_big, s_small, s_own, s_cot, s_act, s_cz, s_az,
):
    kept = [keep(mixer, w_mixer, s_own.at[0]), keep(small, w_small, s_own.at[1])]

    def norm(at):
        v = tok[pl.ds(at, 16)].astype(F32)
        inverse = lax.rsqrt(jnp.mean(v * v, axis=-1, keepdims=True) + EPS)
        act[pl.ds(at, 16)] = (v * inverse * gain[...]).astype(BF16)

    step_rows(tok.shape[0], 16, norm)
    greet(("seq", "wt"))
    little = cube_first(small, w_small, s_small)
    sent1, kept1 = share(cot, cot_f, s_cot, s_own.at[2])
    sent2, kept2 = share(act, act_f, s_act, s_own.at[3])
    big = cube_first(mixer, w_mixer, s_big)
    sent = sent1 + sent2
    arrived(sent)
    kept1.wait()
    kept2.wait()
    along = pass_along(cot_f, s_cz) + pass_along(act_f, s_az)
    little2 = cube_second(w_small, s_small, little)
    little3 = cube_third(w_small, s_small, little2)
    big2 = cube_second(w_mixer, s_big, big)
    big3 = cube_third(w_mixer, s_big, big2)
    cube_end(little, little2, little3)
    cube_end(big, big2, big3)
    arrived(along)
    left(along)
    left(sent)
    for copy in kept:
        copy.wait()


def first_gather(mixer, small, cot, tok, gain, n_wt, n_seq, ident):
    count, width = cot.shape
    far = jax.ShapeDtypeStruct((n_seq, n_wt, count // n_wt, width // n_seq), BF16)
    return pl.pallas_call(
        first_kernel,
        out_shape=[
            jax.ShapeDtypeStruct((n_seq,) + mixer.shape, BF16),
            jax.ShapeDtypeStruct((n_seq,) + small.shape, BF16),
            far,
            far,
            jax.ShapeDtypeStruct((count, width), BF16),
        ],
        in_specs=[ANY, ANY] + [VMEM] * 3,
        out_specs=[ANY] * 4 + [VMEM],
        scratch_shapes=[
            cube_sems(),
            cube_sems(),
            pltpu.SemaphoreType.DMA((4,)),
            pair_sems(n_seq),
            pair_sems(n_seq),
            pair_sems(n_wt),
            pair_sems(n_wt),
        ],
        compiler_params=pltpu.CompilerParams(
            collective_id=ident, has_side_effects=True, vmem_limit_bytes=VMEM_BYTES
        ),
        cost_estimate=pl.CostEstimate(flops=10**6, bytes_accessed=10**8, transcendentals=0),
    )(mixer, small, cot, tok, gain[None])


UNITS = 256


def nt(left_op, right_op):
    return lax.dot_general(
        left_op, right_op, (((1,), (1,)), ((), ())), preferred_element_type=F32
    )


def ffn_kernel(x, c, wg, wu, wd, gated, acts, down, d_second, acc_down, acc_second):
    step = pl.program_id(0)

    @pl.when(step == 0)
    def _():
        acc_down[...] = jnp.zeros_like(acc_down)
        acc_second[...] = jnp.zeros_like(acc_second)

    gate = jnp.dot(x[...], wg[...], preferred_element_type=F32)
    up = jnp.dot(x[...], wu[...], preferred_element_type=F32)
    d_hidden = jnp.dot(c[...], wd[...], preferred_element_type=F32)
    sigma = jax.nn.sigmoid(gate)
    act = gate * sigma
    hidden = (act * up).astype(BF16)
    d_gate = (d_hidden * up * (sigma * (1.0 + gate * (1.0 - sigma)))).astype(BF16)
    d_up = (d_hidden * act).astype(BF16)
    acts[:, :UNITS] = hidden
    acts[:, UNITS : 2 * UNITS] = d_gate
    acts[:, 2 * UNITS : 3 * UNITS] = d_up
    acts[:, 3 * UNITS :] = gated[...]
    acc_down[...] += nt(hidden, wd[...])
    acc_second[...] += nt(d_gate, wg[...]) + nt(d_up, wu[...])

    @pl.when(step == pl.num_programs(0) - 1)
    def _():
        down[...] = acc_down[...].astype(BF16)
        d_second[...] = acc_second[...].astype(BF16)


def ffn(x, c, w_all, gated):
    tok, width = x.shape
    units, chan = w_all.shape[1] // 3, gated.shape[1]
    steps = units // UNITS
    span = 3 * UNITS + chan // steps
    whole = pl.BlockSpec((tok, width), lambda i: (0, 0))
    tile = lambda part: pl.BlockSpec((width, UNITS), lambda i: (0, part * steps + i))
    return pl.pallas_call(
        ffn_kernel,
        grid=(steps,),
        in_specs=[whole, whole, tile(0), tile(1), tile(2)]
        + [pl.BlockSpec((tok, chan // steps), lambda i: (0, i))],
        out_specs=[pl.BlockSpec((tok, span), lambda i: (0, i)), whole, whole],
        out_shape=[
            jax.ShapeDtypeStruct((tok, 3 * units + chan), BF16),
            jax.ShapeDtypeStruct((tok, width), BF16),
            jax.ShapeDtypeStruct((tok, width), BF16),
        ],
        scratch_shapes=[pltpu.VMEM((tok, width), F32)] * 2,
        compiler_params=pltpu.CompilerParams(vmem_limit_bytes=VMEM_BYTES),
        cost_estimate=pl.CostEstimate(
            flops=12 * tok * width * units, bytes_accessed=6 * width * units, transcendentals=0
        ),
    )(x, c, w_all, w_all, w_all, gated)


def grads_kernel(lefts, *refs):
    n, m = max(lefts) + 1, len(lefts)
    for which, act, out in zip(lefts, refs[n : n + m], refs[n + m :]):
        out[...] = jnp.dot(refs[which][...], act[...], preferred_element_type=F32)


def grads(left_ops, lefts, acts):
    rows, tok = left_ops[0].shape
    cols = acts[0].shape[1]
    n = len(acts)
    return pl.pallas_call(
        functools.partial(grads_kernel, lefts),
        grid=(cols // UNITS,),
        in_specs=[pl.BlockSpec((rows, tok), lambda i: (0, 0))] * len(left_ops)
        + [pl.BlockSpec((tok, UNITS), lambda i: (0, i))] * n,
        out_specs=[pl.BlockSpec((rows, UNITS), lambda i: (0, i))] * n,
        out_shape=[jax.ShapeDtypeStruct((rows, cols), F32)] * n,
        compiler_params=pltpu.CompilerParams(vmem_limit_bytes=VMEM_BYTES),
        cost_estimate=pl.CostEstimate(
            flops=2 * n * tok * rows * cols, bytes_accessed=2 * n * tok * cols, transcendentals=0
        ),
    )(*left_ops, *acts)


def wt_sum_kernel(n_cube, n_spread, n_line, part, *refs):
    n = n_cube + n_spread
    srcs, refs = refs[:n], refs[n:]
    lines, out, refs = refs[:n_line], refs[n_line], refs[n_line + 1 :]
    dsts, wholes, refs = refs[:n], refs[n : n + n_line], refs[n + n_line :]
    recv, s_scatter, s_gather = refs[:3]
    sems = refs[3:]
    me = lax.axis_index("wt")
    rows = recv.shape[1]
    for line, whole in zip(lines, wholes):
        whole[pl.ds(pl.multiple_of(me * line.shape[0], 16), line.shape[0])] = line[...]
    greet(("wt", "seq") if n else ("wt",))
    first = scatter_start(part, recv, s_scatter, "wt")
    cubes, sent, kept = [], [], []
    for i in range(n):
        if i < n_cube:
            cubes.append(cube_first(srcs[i], dsts[i], sems[2 * i]))
            kept.append(keep(srcs[i], dsts[i], sems[2 * i + 1]))
        else:
            new, own = spread(srcs[i], dsts[i], sems[2 * i], sems[2 * i + 1])
            sent += new
            kept.append(own)
    arrived(first)
    out[pl.ds(me * rows, rows)] = summed(part, recv, 0, rows, me * rows)
    second = gather_start(out, rows, s_gather, "wt")
    along = [line_gather_start(w, w.shape[0] // lax.axis_size("wt"), sems[-1]) for w in wholes]
    cubes2 = [cube_second(dsts[i], sems[2 * i], cubes[i]) for i in range(n_cube)]
    cubes3 = [cube_third(dsts[i], sems[2 * i], cubes2[i]) for i in range(n_cube)]
    along = [
        line_gather_mid(w, w.shape[0] // lax.axis_size("wt"), sems[-1], a)
        for w, a in zip(wholes, along)
    ]
    for copies in along:
        line_gather_end(copies)
    for one, two, three in zip(cubes, cubes2, cubes3):
        cube_end(one, two, three)
    for copy in kept:
        copy.wait()
    arrived(second)
    arrived(sent)
    for group in (first, second, sent, *along):
        left(group)


def wt_sum(part, blocks, srcs, lines, n_wt, n_seq, ident):
    rows, cols = part.shape
    return pl.pallas_call(
        functools.partial(wt_sum_kernel, len(blocks), len(srcs), len(lines)),
        out_shape=[jax.ShapeDtypeStruct((rows, cols), F32)]
        + [jax.ShapeDtypeStruct((n_seq,) + a.shape, BF16) for a in blocks]
        + [jax.ShapeDtypeStruct((n_seq, a.shape[0], a.shape[1] // n_seq), BF16) for a in srcs]
        + [jax.ShapeDtypeStruct((n_wt * a.shape[0], a.shape[1]), BF16) for a in lines],
        in_specs=[VMEM] + [ANY] * len(blocks) + [VMEM] * len(srcs + lines),
        out_specs=[VMEM] + [ANY] * len(blocks + srcs) + [VMEM] * len(lines),
        scratch_shapes=[
            pltpu.VMEM((n_wt - 1, rows // n_wt, cols), F32),
            pair_sems(n_wt),
            pair_sems(n_wt),
        ]
        + [cube_sems(), pltpu.SemaphoreType.DMA] * len(blocks)
        + [pair_sems(n_seq), pltpu.SemaphoreType.DMA] * len(srcs)
        + [pair_sems(n_wt)] * len(lines),
        compiler_params=pltpu.CompilerParams(
            collective_id=ident, has_side_effects=True, vmem_limit_bytes=VMEM_BYTES
        ),
        cost_estimate=pl.CostEstimate(flops=10**5, bytes_accessed=10**6, transcendentals=0),
    )(part, *blocks, *srcs, *lines)


def second_norm_kernel(part, tok, gain, out, res, recv, pend, s_scatter, s_gather):
    me = lax.axis_index("wt")
    rows = recv.shape[1]
    greet(("wt",))
    first = line_scatter_start(part, recv, s_scatter)
    first = line_scatter_mid(part, recv, pend, s_scatter, first)
    line_scatter_end(first)
    row0 = me * rows

    def body(at):
        r = tok[pl.ds(at, 16)] + line_summed(part, recv, at, 16, row0)
        res[pl.ds(at, 16)] = r
        inverse = lax.rsqrt(jnp.mean(r * r, axis=-1, keepdims=True) + EPS)
        out[pl.ds(pl.multiple_of(row0 + at, 16), 16)] = (r * inverse * gain[...]).astype(BF16)

    step_rows(rows, 16, body)
    second = line_gather_start(out, rows, s_gather)
    second = line_gather_mid(out, rows, s_gather, second)
    line_gather_end(second)
    left(first)
    left(second)


def second_norm(part, tok_own, gain, n_wt, ident):
    rows, cols = part.shape
    own = rows // n_wt
    return pl.pallas_call(
        second_norm_kernel,
        out_shape=[
            jax.ShapeDtypeStruct((rows, cols), BF16),
            jax.ShapeDtypeStruct((own, cols), F32),
        ],
        in_specs=[VMEM] * 3,
        out_specs=[VMEM] * 2,
        scratch_shapes=[
            pltpu.VMEM((n_wt - 1, own, cols), BF16),
            pltpu.VMEM((own, cols), BF16),
            pair_sems(n_wt),
            pair_sems(n_wt),
        ],
        compiler_params=pltpu.CompilerParams(
            collective_id=ident, has_side_effects=True, vmem_limit_bytes=VMEM_BYTES
        ),
        cost_estimate=pl.CostEstimate(flops=10**6, bytes_accessed=10**8, transcendentals=0),
    )(part, tok_own, gain[None])


def norm_back_rows(grad, vals, gain):
    inverse = lax.rsqrt(jnp.mean(vals * vals, axis=-1, keepdims=True) + EPS)
    normed = vals * inverse
    scaled = grad * gain
    mean = jnp.mean(scaled * normed, axis=-1, keepdims=True)
    return inverse * (scaled - normed * mean), grad * normed


def second_back_kernel(n_spread, part, res, cot, gain, *refs):
    srcs, refs = refs[:n_spread], refs[n_spread:]
    out, d_res, gain_grad = refs[:3]
    dsts, refs = refs[3 : 3 + n_spread], refs[3 + n_spread :]
    recv, pend, s_scatter, s_gather = refs[:4]
    me = lax.axis_index("wt")
    rows = recv.shape[1]
    greet(("wt", "seq") if n_spread else ("wt",))
    first = line_scatter_start(part, recv, s_scatter)
    spreads = [
        spread(srcs[i], dsts[i], refs[4 + 2 * i], refs[5 + 2 * i]) for i in range(n_spread)
    ]
    gain_grad[...] = jnp.zeros_like(gain_grad)
    first = line_scatter_mid(part, recv, pend, s_scatter, first)
    line_scatter_end(first)
    row0 = me * rows

    def body(at):
        grad = line_summed(part, recv, at, 16, row0)
        back, prod = norm_back_rows(grad, res[pl.ds(at, 16)], gain[...])
        gain_grad[...] += prod[:8] + prod[8:]
        d = cot[pl.ds(at, 16)] + back
        d_res[pl.ds(at, 16)] = d
        out[pl.ds(pl.multiple_of(row0 + at, 16), 16)] = d.astype(BF16)

    step_rows(rows, 16, body)
    second = line_gather_start(out, rows, s_gather)
    second = line_gather_mid(out, rows, s_gather, second)
    line_gather_end(second)
    for sent, kept in spreads:
        kept.wait()
        arrived(sent)
        left(sent)
    left(first)
    left(second)


def second_back(part, res, cot_own, gain, srcs, n_wt, n_seq, ident):
    rows, cols = part.shape
    own = rows // n_wt
    return pl.pallas_call(
        functools.partial(second_back_kernel, len(srcs)),
        out_shape=[
            jax.ShapeDtypeStruct((rows, cols), BF16),
            jax.ShapeDtypeStruct((own, cols), F32),
            jax.ShapeDtypeStruct((8, cols), F32),
        ]
        + [jax.ShapeDtypeStruct((n_seq, rows, cols // n_seq), BF16)] * len(srcs),
        in_specs=[VMEM] * (4 + len(srcs)),
        out_specs=[VMEM] * 3 + [ANY] * len(srcs),
        scratch_shapes=[
            pltpu.VMEM((n_wt - 1, own, cols), BF16),
            pltpu.VMEM((own, cols), BF16),
            pair_sems(n_wt),
            pair_sems(n_wt),
        ]
        + [pair_sems(n_seq), pltpu.SemaphoreType.DMA] * len(srcs),
        compiler_params=pltpu.CompilerParams(
            collective_id=ident, has_side_effects=True, vmem_limit_bytes=VMEM_BYTES
        ),
        cost_estimate=pl.CostEstimate(flops=10**6, bytes_accessed=10**8, transcendentals=0),
    )(part, res, cot_own, gain[None], *srcs)


def last_kernel(cube, part, tok, d_res, gain, gain_grad2, sel, stp, taps, decays, bias3, *refs):
    blocks, refs = refs[:cube], refs[cube:]
    if cube:
        cot_t, second_t, branch_t, acts, refs = refs[0], refs[1], refs[2], refs[3], refs[4:]
    out, sel_out, stp_out, chan_out, gains_out = refs[:5]
    wholes, refs = refs[5 : 5 + cube], refs[5 + cube :]
    if cube:
        grad_outs, refs = refs[:4], refs[4:]
        tile, s_tile, refs = refs[0], refs[1], refs[2:]
        width = tile.shape[2]
        tiles = acts.shape[1] // width

        def fetch(j, slot):
            columns = acts.at[:, pl.ds(pl.multiple_of(j * width, width), width)]
            return pltpu.make_async_copy(columns, tile.at[slot], s_tile.at[slot])

        def one_tile(j, carry):
            slot = lax.rem(j, 2)

            @pl.when(j + 1 < tiles)
            def _():
                fetch(j + 1, 1 - slot).start()

            fetch(j, slot).wait()
            at = 0
            for left_op, out_ref in zip((cot_t, second_t, second_t, branch_t), grad_outs):
                wide = out_ref.shape[1] // tiles
                out_ref[:, pl.ds(pl.multiple_of(j * wide, wide), wide)] = jnp.dot(
                    left_op[...], tile[slot, :, at : at + wide], preferred_element_type=F32
                )
                at += wide
            return carry

        fetch(0, 0).start()
    recv, pend, recv_sel, recv_stp, recv_chan, pack, gain_buf, recv_gz, recv_gs = refs[:9]
    s_scatter, s_gather, s_sel, s_stp, s_chan, s_cg, s_gz, s_gs = refs[9:17]
    refs = refs[17:]
    me, n_wt = lax.axis_index("wt"), lax.axis_size("wt")
    seq, n_seq = lax.axis_index("seq"), lax.axis_size("seq")
    rows = recv.shape[1]
    greet(("wt", "seq"))
    first = line_scatter_start(part, recv, s_scatter)
    share = -(-(KC + NS + 3) // n_seq)
    lines = [(taps, i) for i in range(KC)] + [(decays, i) for i in range(NS)]
    lines += [(bias3, i) for i in range(3)]
    for at, (ref, i) in enumerate(lines):
        pack[at // share, at % share : at % share + 1] = ref[i : i + 1]
    smalls = []
    for src, dst, sems in ((sel, recv_sel, s_sel), (stp, recv_stp, s_stp), (pack, recv_chan, s_chan)):
        for k in range(1, n_seq):
            peer = lax.rem(seq + k, n_seq)
            smalls.append(send(src.at[peer], dst.at[k - 1], sems, k - 1, "seq", peer))
    cubes = []
    for i in range(cube):
        s_cube, s_own = refs[2 * i : 2 * i + 2]
        cubes.append([cube_first(blocks[i], wholes[i], s_cube), s_cube, wholes[i]])
        cubes[-1].append(keep(blocks[i], wholes[i], s_own))
    if cube:
        lax.fori_loop(0, 3, one_tile, 0)
    first = line_scatter_mid(part, recv, pend, s_scatter, first)
    if cube:
        lax.fori_loop(3, tiles - 2, one_tile, 0)
    arrived(smalls)
    for src, recv_one, one_out in ((sel, recv_sel, sel_out), (stp, recv_stp, stp_out)):
        total = src[seq].astype(F32)
        for k in range(n_seq - 1):
            total = total + recv_one[k].astype(F32)
        one_out[...] = total
    total = pack[seq]
    for k in range(n_seq - 1):
        total = total + recv_chan[k]
    chan_out[seq] = total
    mine = chan_out.at[seq]
    chans = [
        send(mine, mine, s_cg, k - 1, "seq", lax.rem(seq + k, n_seq)) for k in range(1, n_seq)
    ]
    line_scatter_end(first)
    row0 = me * rows
    gain_buf[...] = jnp.zeros_like(gain_buf)

    def body(at):
        grad = line_summed(part, recv, at, 16, row0)
        back, prod = norm_back_rows(grad, tok[pl.ds(at, 16)], gain[...])
        gain_buf[...] += prod[:8] + prod[8:]
        out[pl.ds(pl.multiple_of(row0 + at, 16), 16)] = (d_res[pl.ds(at, 16)] + back).astype(BF16)

    step_rows(rows, 16, body)
    second = line_gather_start(out, rows, s_gather)
    high = recv_gz.shape[1] // 2
    for i, grad in enumerate((gain_buf, gain_grad2)):
        line = jnp.sum(grad[...], axis=0, keepdims=True)
        for t in range(high):
            recv_gz[me, i * high + t : i * high + t + 1] = line[:, t * 128 : (t + 1) * 128]
    mine_z = recv_gz.at[me]
    zs = [send(mine_z, mine_z, s_gz, k - 1, "wt", lax.rem(me + k, n_wt)) for k in range(1, n_wt)]
    cubes2 = [cube_second(whole, sems, one) for one, sems, whole, _ in cubes]
    if cube:
        lax.fori_loop(tiles - 2, tiles, one_tile, 0)
    second = line_gather_mid(out, rows, s_gather, second)
    arrived(zs)
    total = recv_gz[0]
    for pos in range(1, n_wt):
        total = total + recv_gz[pos]
    recv_gs[seq] = total
    mine_s = recv_gs.at[seq]
    ss = [
        send(mine_s, mine_s, s_gs, k - 1, "seq", lax.rem(seq + k, n_seq)) for k in range(1, n_seq)
    ]
    cubes3 = [cube_third(whole, sems, two) for (_, sems, whole, _), two in zip(cubes, cubes2)]
    arrived(ss)
    total = recv_gs[0]
    for pos in range(1, n_seq):
        total = total + recv_gs[pos]
    gains_out[...] = total
    arrived(chans)
    for (one, _, _, kept), two, three in zip(cubes, cubes2, cubes3):
        cube_end(one, two, three)
        kept.wait()
    line_gather_end(second)
    for group in (first, second, smalls, chans, zs, ss):
        left(group)


def last(part, tok_own, d_res, gain, gain_grad2, sel, stp, taps, decays, bias3, blocks, more, n_wt, n_seq, ident):
    rows, cols = part.shape
    own = rows // n_wt
    chan = taps.shape[1]
    if more:
        deep, tok_all = more[0].shape
        units = (more[3].shape[1] - chan) // 3
        span = more[3].shape[1] // (units // UNITS)
    return pl.pallas_call(
        functools.partial(last_kernel, len(blocks)),
        out_shape=[
            jax.ShapeDtypeStruct((rows, cols), BF16),
            jax.ShapeDtypeStruct(sel.shape[1:], F32),
            jax.ShapeDtypeStruct(stp.shape[1:], F32),
            jax.ShapeDtypeStruct((n_seq, 8, chan), F32),
            jax.ShapeDtypeStruct((2 * cols // 128, 128), F32),
        ]
        + [jax.ShapeDtypeStruct((n_seq,) + a.shape, BF16) for a in blocks]
        + ([jax.ShapeDtypeStruct((deep, w), F32) for w in (units, units, units, chan)] if more else []),
        in_specs=[VMEM] * 10 + [ANY] * len(blocks) + ([VMEM, VMEM, VMEM, ANY] if more else []),
        out_specs=[VMEM] * 5 + [ANY] * len(blocks) + ([VMEM] * 4 if more else []),
        scratch_shapes=(
            [pltpu.VMEM((2, tok_all, span), BF16), pltpu.SemaphoreType.DMA((2,))]
            if more
            else []
        )
        + [
            pltpu.VMEM((n_wt - 1, own, cols), BF16),
            pltpu.VMEM((own, cols), BF16),
            pltpu.VMEM((n_seq - 1,) + sel.shape[1:], BF16),
            pltpu.VMEM((n_seq - 1,) + stp.shape[1:], BF16),
            pltpu.VMEM((n_seq - 1, 8, chan), F32),
            pltpu.VMEM((n_seq, 8, chan), F32),
            pltpu.VMEM((8, cols), F32),
            pltpu.VMEM((n_wt, 2 * cols // 128, 128), F32),
            pltpu.VMEM((n_seq, 2 * cols // 128, 128), F32),
            pair_sems(n_wt),
            pair_sems(n_wt),
            pair_sems(n_seq),
            pair_sems(n_seq),
            pair_sems(n_seq),
            pair_sems(n_seq),
            pair_sems(n_wt),
            pair_sems(n_seq),
        ]
        + [cube_sems(), pltpu.SemaphoreType.DMA] * len(blocks),
        compiler_params=pltpu.CompilerParams(
            collective_id=ident, has_side_effects=True, vmem_limit_bytes=VMEM_BYTES
        ),
        cost_estimate=pl.CostEstimate(flops=10**6, bytes_accessed=10**8, transcendentals=0),
    )(part, tok_own, d_res, gain[None], gain_grad2, sel, stp, taps, decays, bias3, *blocks, *more)


def load(ref):
    return tuple(ref[n] for n in range(NS))


def store(ref, values):
    for n in range(NS):
        ref[n] = values[n]


def fold(mine, box, recv, a2, carried, backward):
    n, me = lax.axis_size("seq"), lax.axis_index("seq")
    carried[...] = jnp.zeros_like(carried)
    for k in range(n - 1, 0, -1):

        @pl.when((me + k < n) if backward else (me >= k))
        def _():
            giver = me + k if backward else me - k
            remote(mine, recv.at[k - 1], box, k - 1, "seq", giver).wait_recv()
            through = recv[k - 1, NS]
            for s in range(NS):
                carried[s] = (
                    jnp.exp2(a2[s] * through) * carried[s] + recv[k - 1, s]
                )


def hand_on(mine, recv, box, backward):
    n, me = lax.axis_size("seq"), lax.axis_index("seq")
    for k in range(1, n):

        @pl.when((me >= k) if backward else (me + k < n))
        def _():
            peer = me - k if backward else me + k
            send(mine, recv.at[k - 1], box, k - 1, "seq", peer)


def handed(mine, recv, box, backward):
    n, me = lax.axis_size("seq"), lax.axis_index("seq")
    for k in range(1, n):

        @pl.when((me >= k) if backward else (me + k < n))
        def _():
            peer = me - k if backward else me + k
            remote(mine, recv.at[k - 1], box, k - 1, "seq", peer).wait_send()


def fwd_kernel(sa, dx, wr, a2, y, h0, mine, recv, box):
    tok = sa.shape[0]
    greet(("seq",))

    def end(t, carry):
        s, d = sa[t], dx[t]
        h, total = carry
        return (
            tuple(jnp.exp2(s * a2[n]) * h[n] + wr[n, t] * d for n in range(NS)),
            total + s,
        )

    zero = jnp.zeros(sa.shape[1:], F32)
    ends, total = lax.fori_loop(0, tok, end, ((zero,) * NS, zero), unroll=4)
    store(mine, ends)
    mine[NS] = total
    hand_on(mine, recv, box, False)
    fold(mine, box, recv, a2, h0, False)

    def body(t, h):
        s, d = sa[t], dx[t]
        new, sums = [], [None] * 4
        for n in range(NS):
            hn = jnp.exp2(s * a2[n]) * h[n] + wr[n, t] * d
            new.append(hn)
            c = wr[NS + n, t] * hn
            sums[n % 4] = c if sums[n % 4] is None else sums[n % 4] + c
        y[t] = (sums[0] + sums[1]) + (sums[2] + sums[3])
        return tuple(new)

    lax.fori_loop(0, tok, body, load(h0), unroll=4)
    handed(mine, recv, box, False)


def fwd_scan(sa, dx, wr, a2, n_seq, ident):
    tok, high = sa.shape[:2]
    return pl.pallas_call(
        fwd_kernel,
        out_shape=[
            jax.ShapeDtypeStruct((tok, high, 128), F32),
            jax.ShapeDtypeStruct((NS, high, 128), F32),
        ],
        in_specs=[VMEM, VMEM, SMEM, VMEM],
        out_specs=[VMEM] * 2,
        scratch_shapes=[
            pltpu.VMEM((NS + 1, high, 128), F32),
            pltpu.VMEM((n_seq - 1, NS + 1, high, 128), F32),
            pair_sems(n_seq),
        ],
        compiler_params=pltpu.CompilerParams(
            collective_id=ident, has_side_effects=True, vmem_limit_bytes=VMEM_BYTES
        ),
        cost_estimate=pl.CostEstimate(
            flops=10**8, bytes_accessed=8 * 10**7, transcendentals=2 * tok * NS * 1024
        ),
    )(sa, dx, wr, a2)


def bwd_kernel(
    cube, sa, dx, wr, do, a2, h0, part, res, *refs
):
    src, refs = refs[:cube], refs[cube:]
    along, ds2, grad_a, sums, out = refs[:5]
    dst, refs = refs[5 : 5 + cube], refs[5 + cube :]
    hs, qw, qr, pw, pr, g0, mine, recv, recv_z, box, s_scatter = refs[:11]
    tok = sa.shape[0]
    chunk = qw.shape[0] // (NS * 8)
    greet(("wt", "seq"))
    first = scatter_start(part, recv_z, s_scatter, "wt")

    def end(i, carry):
        t = tok - 1 - i
        s, d = sa[t], do[t]
        g, total = carry
        return (
            tuple(jnp.exp2(s * a2[n]) * (g[n] + wr[NS + n, t] * d) for n in range(NS)),
            total + s,
        )

    zero = jnp.zeros(sa.shape[1:], F32)
    ends, total = lax.fori_loop(0, tok, end, ((zero,) * NS, zero), unroll=4)
    store(mine, ends)
    mine[NS] = total
    hand_on(mine, recv, box, True)
    if cube:
        s_seq, s_wt, s_own = refs[11:]
        sent, kept = share(src[0], dst[0], s_seq, s_own)

    def again(t, h):
        s, d = sa[t], dx[t]
        new = []
        for n in range(NS):
            hs[t, n] = h[n]
            new.append(jnp.exp2(s * a2[n]) * h[n] + wr[n, t] * d)
        return tuple(new)

    lax.fori_loop(0, tok, again, load(h0), unroll=2)

    fold(mine, box, recv, a2, g0, True)
    if cube:
        arrived(sent)
        kept.wait()
        passed = pass_along(dst[0], s_wt)
    grad_a[...] = jnp.zeros_like(grad_a)

    def one_chunk(j, g):
        base = (tok // chunk - 1 - j) * chunk

        def body(i, g):
            at = chunk - 1 - i
            t = base + at
            s, d, o = sa[t], dx[t], do[t]
            al = d2 = None
            new = []
            for n in range(NS):
                hp = hs[t, n]
                f = jnp.exp2(s * a2[n])
                hn = f * hp + wr[n, t] * d
                gn = wr[NS + n, t] * o + g[n]
                adj = f * gn
                new.append(adj)
                th = adj * hp
                grad_a[n] += th * s
                x = wr[n, t] * gn
                al = x if al is None else al + x
                x = a2[n] * th
                d2 = x if d2 is None else d2 + x
                row = pl.multiple_of((at * NS + n) * 8, 8)
                qw[pl.ds(row, 8), :] = gn * d
                qr[pl.ds(row, 8), :] = hn * o
            along[t] = al
            ds2[t] = d2
            return tuple(new)

        g = lax.fori_loop(0, chunk, body, g)

        def lanes(i, carry):
            for q, p in ((qw, pw), (qr, pr)):
                acc = q[pl.ds(i * NS * 8, NS, stride=8), :]
                for s in range(1, 8):
                    acc = acc + q[pl.ds(i * NS * 8 + s, NS, stride=8), :]
                p[pl.ds(pl.multiple_of(i * NS, NS), NS), :] = acc
            return carry

        lax.fori_loop(0, chunk, lanes, 0, unroll=4)
        ones = jnp.ones((8, 128), BF16)
        for which, p in enumerate((pw, pr)):
            high = p[...].astype(BF16)
            low = (p[...] - high.astype(F32)).astype(BF16)
            row = which * (tok // chunk) + base // chunk
            sums[pl.ds(row, 1), :] = (nt(ones, high) + nt(ones, low))[:1]
        return g

    lax.fori_loop(0, tok // chunk, one_chunk, load(g0))
    handed(mine, recv, box, True)
    arrived(first)
    rows = recv_z.shape[1]
    row0 = lax.axis_index("wt") * rows

    def block_rows(at):
        out[pl.ds(at, 16)] = (res[pl.ds(at, 16)] + summed(part, recv_z, at, 16, row0)).astype(BF16)

    step_rows(rows, 16, block_rows)
    left(first)
    if cube:
        arrived(passed)
        left(sent)
        left(passed)


def bwd_scan(sa, dx, wr, do, a2, h0, part, res, src, n_wt, n_seq, ident):
    tok, high = sa.shape[:2]
    rows, cols = part.shape
    chunk = 32
    return pl.pallas_call(
        functools.partial(bwd_kernel, len(src)),
        out_shape=[
            jax.ShapeDtypeStruct((tok, high, 128), F32),
            jax.ShapeDtypeStruct((tok, high, 128), F32),
            jax.ShapeDtypeStruct((NS, high, 128), F32),
            jax.ShapeDtypeStruct((2 * tok // chunk, chunk * NS), F32),
            jax.ShapeDtypeStruct((rows // n_wt, cols), BF16),
        ]
        + [jax.ShapeDtypeStruct((n_seq, n_wt, rows // n_wt, cols // n_seq), BF16)] * len(src),
        in_specs=[VMEM, VMEM, SMEM] + [VMEM] * (5 + len(src)),
        out_specs=[VMEM] * 5 + [ANY] * len(src),
        scratch_shapes=[
            pltpu.VMEM((tok, NS, high, 128), F32),
            pltpu.VMEM((chunk * NS * 8, 128), F32),
            pltpu.VMEM((chunk * NS * 8, 128), F32),
            pltpu.VMEM((chunk * NS, 128), F32),
            pltpu.VMEM((chunk * NS, 128), F32),
            pltpu.VMEM((NS, high, 128), F32),
            pltpu.VMEM((NS + 1, high, 128), F32),
            pltpu.VMEM((n_seq - 1, NS + 1, high, 128), F32),
            pltpu.VMEM((n_wt - 1, rows // n_wt, cols), BF16),
            pair_sems(n_seq),
            pair_sems(n_wt),
        ]
        + [pair_sems(n_seq), pair_sems(n_wt), pltpu.SemaphoreType.DMA] * len(src),
        compiler_params=pltpu.CompilerParams(
            collective_id=ident, has_side_effects=True, vmem_limit_bytes=VMEM_BYTES
        ),
        cost_estimate=pl.CostEstimate(
            flops=10**8, bytes_accessed=15 * 10**7, transcendentals=3 * tok * NS * 1024
        ),
    )(sa, dx, wr, do, a2, h0, part, res, *src)


def gather(block):
    return lax.all_gather(block, "seq", axis=0, tiled=True)


def from_behind(block, axis, distance):
    devices = range(lax.axis_size(axis))
    route = [(i - distance, i) for i in devices if i - distance in devices]
    return lax.ppermute(block, axis, route)


def contract(left_op, right_op, pattern):
    return jnp.einsum(pattern, left_op, right_op, preferred_element_type=F32)


def silu_slope(values):
    sigma = jax.nn.sigmoid(values)
    return sigma * (1.0 + values * (1.0 - sigma))


def tiles(rows):
    return rows.reshape(rows.shape[0], rows.shape[1] // 128, 128)


def flat(rows):
    return rows.reshape(rows.shape[0], rows.shape[1] * rows.shape[2])


def local(
    tokens,
    cotangent,
    doc_start,
    premix_gain,
    inner_proj,
    switch_proj,
    conv_taps,
    conv_bias,
    select_proj,
    step_proj,
    step_bias,
    decay_log,
    skip_gain,
    mixer_out,
    preffn_gain,
    ffn_gate,
    ffn_up,
    ffn_down,
):
    tok_count, width = tokens.shape
    chan = inner_proj.shape[1]
    units = ffn_gate.shape[1]
    edge = KC - 1
    n_seq, n_wt = lax.axis_size("seq"), lax.axis_size("wt")
    z = lax.axis_index("wt")
    own = tok_count // n_wt
    cube = n_seq == 8 and n_seq * tok_count <= width

    rows_sel, rows_step = select_proj.shape[0], step_proj.shape[0]
    if cube:
        fill = jnp.zeros((-(rows_sel + rows_step) % 32, chan), BF16)
        small = jnp.concatenate([select_proj, step_proj, fill], axis=0)
        w_mixer, w_small, cot_f, first_f, first_in = first_gather(
            jnp.concatenate([inner_proj, switch_proj, mixer_out], axis=1),
            small, cotangent, tokens, premix_gain, n_wt, n_seq, 7,
        )
        w_mixer = w_mixer.reshape(width, 3 * chan)
    else:
        token_vals = tokens.astype(F32)
        first_inv = lax.rsqrt(jnp.mean(token_vals * token_vals, axis=-1, keepdims=True) + EPS)
        first_in = (token_vals * first_inv * premix_gain).astype(BF16)
        w_mixer = gather(jnp.concatenate([inner_proj, switch_proj, mixer_out], axis=1))
        w_small = lax.all_gather(jnp.concatenate([select_proj, step_proj], axis=0), "seq", axis=0)
    ffn_own = jnp.concatenate([ffn_gate, ffn_up, ffn_down], axis=1)
    ffn_own, w_small = lax.optimization_barrier((ffn_own, w_small))
    w_all = gather(ffn_own)
    w_first, w_mix = w_mixer[:, : 2 * chan], w_mixer[:, 2 * chan :]
    w_select = w_small[:, :rows_sel].reshape(-1, chan)
    w_step = w_small[:, rows_sel : rows_sel + rows_step].reshape(-1, chan)
    both = contract(first_in, w_first, "td,dc->tc")
    inner_act = both[:, :chan].astype(BF16)
    switch = both[:, chan:]

    goes_on = (1 - doc_start).astype(F32)
    before = jnp.concatenate([jnp.ones((edge,), F32), goes_on])
    after = jnp.concatenate([goes_on, jnp.ones((edge,), F32)])

    def same_back(lag):
        same = jnp.ones_like(goes_on)
        for j in range(lag):
            same = same * before[edge - j : edge - j + tok_count]
        return same[:, None]

    def same_ahead(lag):
        same = jnp.ones_like(goes_on)
        for j in range(1, lag + 1):
            same = same * after[j : j + tok_count]
        return same[:, None]

    one = jnp.ones((edge - 1,), F32)
    last_two, head = goes_on[-2:], goes_on[:edge]
    tail_keep = jnp.concatenate([last_two, one[:1]]) * jnp.concatenate([last_two[1:], one])
    head_keep = (
        head
        * jnp.concatenate([one[:1], head[:2]])
        * jnp.concatenate([one, head[:1]])
    )
    prev_rows = from_behind(inner_act[-edge:] * tail_keep[:, None].astype(BF16), "seq", 1)
    extended = jnp.concatenate([prev_rows, inner_act], axis=0).astype(F32)
    conv_out = jnp.zeros((tok_count, chan), F32) + conv_bias[None, :]
    for offset in range(KC):
        conv_out = (
            conv_out
            + conv_taps[offset][None, :]
            * extended[edge - offset : edge - offset + tok_count]
            * same_back(offset)
        )
    mixed_in = jax.nn.silu(conv_out).astype(BF16)
    mixed_f = mixed_in.astype(F32)
    (select,) = wt_sum(contract(w_select, mixed_in, "jc,tc->jt"), (), (), (), n_wt, n_seq, 0)
    low_rank = select[:R].astype(BF16)
    write_read = select[R:]
    step_pre = contract(low_rank, w_step, "rt,rc->tc") + step_bias[None, :]
    step_size = jax.nn.softplus(step_pre)
    decay = -jnp.exp(decay_log)
    decay2 = tiles(decay * LOG2E)
    step_a = tiles(jnp.where(doc_start[:, None] > 0, FAR, step_size))
    drive = tiles(step_size * mixed_f)
    scan_out, carried_in = fwd_scan(step_a, drive, write_read, decay2, n_seq, 1)

    scanned = flat(scan_out) + skip_gain[None, :] * mixed_f
    switch_act = jax.nn.silu(switch)
    gated = (scanned * switch_act).astype(BF16)
    mix_part = contract(gated, w_mix, "tc,dc->td").astype(BF16)
    tokens_own = lax.dynamic_slice_in_dim(tokens, z * own, own, 0).astype(F32)
    cot_own = lax.dynamic_slice_in_dim(cotangent, z * own, own, 0).astype(F32)
    second_in, residual = second_norm(mix_part, tokens_own, preffn_gain, n_wt, 2)
    if cube:
        line_up = lambda v: v.reshape(n_seq * tok_count, v.shape[-1])
        second_in, cot_own, head_keep, cot_t, first_t = lax.optimization_barrier(
            (second_in, cot_own, head_keep, line_up(cot_f).T, line_up(first_f).T)
        )
    acts, down_part, d_second = ffn(second_in, cotangent, w_all, gated)
    d_branch, d_residual, grad_preffn, *second_all = second_back(
        d_second, residual, cot_own, preffn_gain, (second_in,) if cube else (), n_wt, n_seq, 3
    )
    d_gated = contract(d_branch, w_mix, "td,dc->tc")
    d_scanned = d_gated * switch_act
    d_switch = (d_gated * scanned * silu_slope(switch)).astype(BF16)
    grad_skip = jnp.sum(d_scanned * mixed_f, axis=0)
    along, through_sum, grad_decay, d_write_read, block_own, *branch_all = bwd_scan(
        step_a, drive, write_read, tiles(d_scanned), decay2, carried_in,
        down_part, residual, (d_branch,) if cube else (), n_wt, n_seq, 4,
    )
    along = flat(along)
    d_step = along * mixed_f + flat(through_sum) * (1.0 / LOG2E)
    grad_decay_log = flat(grad_decay) * decay
    d_pre = d_step * jax.nn.sigmoid(step_pre)
    grad_step_bias = jnp.sum(d_pre, axis=0)
    d_pre_low = d_pre.astype(BF16)
    pad_rows = lambda v: jnp.pad(
        v.reshape(n_seq, -1, tok_count), ((0, 0), (0, -(v.shape[0] // n_seq) % 16), (0, 0))
    ).reshape(-1, tok_count)
    grad_step = contract(pad_rows(low_rank), d_pre_low, "rt,tc->rc").astype(BF16)
    d_select, *gathered, block_out = wt_sum(
        jnp.concatenate(
            [
                contract(w_step, d_pre_low, "rc,tc->rt"),
                d_write_read.reshape(2, tok_count, NS).swapaxes(1, 2).reshape(2 * NS, tok_count),
            ],
            axis=0,
        ),
        (d_switch,) if cube else (),
        (),
        (block_own,),
        n_wt,
        n_seq,
        5,
    )
    d_select = d_select.astype(BF16)
    grad_select = contract(pad_rows(d_select), mixed_in, "jt,tc->jc").astype(BF16)
    d_mixed = (
        along * step_size
        + skip_gain[None, :] * d_scanned
        + contract(d_select, w_select, "jt,jc->tc")
    )
    d_conv = (d_mixed * silu_slope(conv_out)).astype(BF16)
    d_conv_f = d_conv.astype(F32)
    grad_conv_bias = jnp.sum(d_conv_f, axis=0)
    next_rows = from_behind(d_conv[:edge] * head_keep[:, None].astype(BF16), "seq", -1)
    ext_grad = jnp.concatenate([d_conv, next_rows], axis=0).astype(F32)
    d_inner = jnp.zeros_like(d_conv_f)
    taps_rows = []
    for offset in range(KC):
        taps_rows.append(
            jnp.sum(
                d_conv_f
                * extended[edge - offset : edge - offset + tok_count]
                * same_back(offset),
                axis=0,
            )
        )
        d_inner = (
            d_inner
            + conv_taps[offset][None, :]
            * ext_grad[offset : offset + tok_count]
            * same_ahead(offset)
        )
    d_inner_low = d_inner.astype(BF16)
    d_first = contract(
        jnp.concatenate([d_inner_low, d_switch], axis=1), w_first, "tc,dc->td"
    ).astype(BF16)
    more = ()
    if cube:
        (switch_all,) = map(line_up, gathered)
        more = (cot_t, line_up(second_all[0]).T, line_up(branch_all[0]).T, gather(acts))
    tokens_grad, out_select, out_step, by_chan, gains, *others = last(
        d_first, tokens_own, d_residual, premix_gain, grad_preffn,
        grad_select.reshape(n_seq, -1, chan), grad_step.reshape(n_seq, -1, chan),
        jnp.stack(taps_rows, axis=0), grad_decay_log,
        jnp.stack([grad_conv_bias, grad_step_bias, grad_skip]),
        (d_inner_low,) if cube else (), more, n_wt, n_seq, 6,
    )
    share = -(-(KC + NS + 3) // n_seq)
    by_chan = by_chan[:, :share].reshape(n_seq * share, chan)
    gains = gains.reshape(2, width)
    if cube:
        out_down, out_gate, out_up, out_mix = others[1:]
        out_switch, out_inner = grads(
            (first_t,), (0, 0), (switch_all, line_up(others[0]))
        )
    else:
        scatter = lambda v: lax.psum_scatter(v, "seq", scatter_dimension=0, tiled=True)
        by_unit = acts.reshape(tok_count, units // UNITS, -1)
        hidden, d_gate, d_up = [
            by_unit[:, :, i * UNITS : (i + 1) * UNITS].reshape(tok_count, units) for i in range(3)
        ]
        out_down = scatter(contract(cotangent, hidden, "td,tf->df"))
        out_gate = scatter(contract(second_in, d_gate, "td,tf->df"))
        out_up = scatter(contract(second_in, d_up, "td,tf->df"))
        out_mix = scatter(contract(d_branch, gated, "td,tc->dc"))
        out_switch = scatter(contract(first_in, d_switch, "td,tc->dc"))
        out_inner = scatter(contract(first_in, d_inner_low, "td,tc->dc"))
    return (
        block_out,
        tokens_grad,
        gains[0],
        out_inner,
        out_switch,
        by_chan[:KC],
        by_chan[KC + NS],
        out_select[:rows_sel],
        out_step[:rows_step],
        by_chan[KC + NS + 1],
        by_chan[KC : KC + NS],
        by_chan[KC + NS + 2],
        out_mix,
        gains[1],
        out_gate,
        out_up,
        out_down,
    )


def solution(mesh):
    placed = (
        P("seq", None),
        P("seq", None),
        P("seq"),
        P(),
        P("seq", "wt"),
        P("seq", "wt"),
        P(None, "wt"),
        P("wt"),
        P("seq", "wt"),
        P("seq", "wt"),
        P("wt"),
        P(None, "wt"),
        P("wt"),
        P("seq", "wt"),
        P(),
        P("seq", "wt"),
        P("seq", "wt"),
        P("seq", "wt"),
    )
    return jax.shard_map(
        local,
        mesh=mesh,
        in_specs=placed,
        out_specs=(
            P("seq", None),
            P("seq", None),
            P(),
            P("seq", "wt"),
            P("seq", "wt"),
            P(None, "wt"),
            P("wt"),
            P("seq", "wt"),
            P("seq", "wt"),
            P("wt"),
            P(None, "wt"),
            P("wt"),
            P("seq", "wt"),
            P(),
            P("seq", "wt"),
            P("seq", "wt"),
            P("seq", "wt"),
        ),
        check_vma=False,
    )
```

```python
import functools

import jax
import jax.numpy as jnp
from jax import lax
from jax.experimental import pallas as pl
from jax.experimental.pallas import tpu as pltpu
from jax.sharding import PartitionSpec as P

NS = 16
R = 128
KC = 4
EPS = 1e-05
F32 = jnp.float32
BF16 = jnp.bfloat16
LOG2E = 1.4426950408889634
FAR = 1e30
MESH = pl.DeviceIdType.MESH
VMEM = pl.BlockSpec(memory_space=pltpu.VMEM)
SMEM = pl.BlockSpec(memory_space=pltpu.SMEM)
ANY = pl.BlockSpec(memory_space=pl.ANY)
VMEM_BYTES = 60 * 2**20


UNITS = 256


def nt(left_op, right_op):
    return lax.dot_general(
        left_op, right_op, (((1,), (1,)), ((), ())), preferred_element_type=F32
    )


def greet(axes):
    barrier = pltpu.get_barrier_semaphore()
    total = 0
    for axis in axes:
        n, me = lax.axis_size(axis), lax.axis_index(axis)
        for k in range(1, n):
            pl.semaphore_signal(
                barrier, inc=1, device_id={axis: lax.rem(me + k, n)}, device_id_type=MESH
            )
        total += n - 1
    pl.semaphore_wait(barrier, total)


def remote(src, dst, sems, slot, axis, peer):
    return pltpu.make_async_remote_copy(
        src_ref=src,
        dst_ref=dst,
        send_sem=sems.at[0, slot],
        recv_sem=sems.at[1, slot],
        device_id={axis: peer},
        device_id_type=MESH,
    )


def send(src, dst, sems, slot, axis, peer):
    copy = remote(src, dst, sems, slot, axis, peer)
    copy.start()
    return copy


def scatter_start(part, recv, sems, axis):
    n, me = lax.axis_size(axis), lax.axis_index(axis)
    rows = recv.shape[1]
    copies = []
    for k in range(1, n):
        peer = lax.rem(me + k, n)
        copies.append(
            send(part.at[pl.ds(peer * rows, rows)], recv.at[k - 1], sems, k - 1, axis, peer)
        )
    return copies


def gather_start(whole, rows, sems, axis):
    n, me = lax.axis_size(axis), lax.axis_index(axis)
    mine = whole.at[pl.ds(me * rows, rows)]
    return [send(mine, mine, sems, k - 1, axis, lax.rem(me + k, n)) for k in range(1, n)]


def arrived(copies):
    for copy in copies:
        copy.wait_recv()


def left(copies):
    for copy in copies:
        copy.wait_send()


def pair_sems(n):
    return pltpu.SemaphoreType.DMA((2, n - 1))


def summed(part, recv, at, step, row0):
    total = part[pl.ds(row0 + at, step)].astype(F32)
    for k in range(recv.shape[0]):
        total = total + recv[k, pl.ds(at, step)].astype(F32)
    return total


def step_rows(rows, step, body):
    def run(i, carry):
        body(pl.multiple_of(i * step, step))
        return carry

    lax.fori_loop(0, rows // step, run, 0)


def mates():
    z = lax.axis_index("wt")
    mate = z + 1 - 2 * lax.rem(z, 2)
    return z, mate, lax.rem(z + 2, 4), lax.rem(mate + 2, 4)


def line_scatter_start(part, recv, sems):
    if lax.axis_size("wt") != 4:
        return scatter_start(part, recv, sems, "wt")
    rows = recv.shape[1]
    _, mate, _, far_mate = mates()
    return [
        send(part.at[pl.ds(far_mate * rows, rows)], recv.at[0], sems, 0, "wt", mate),
        send(part.at[pl.ds(mate * rows, rows)], recv.at[1], sems, 1, "wt", mate),
    ]


def line_scatter_mid(part, recv, pend, sems, copies):
    if lax.axis_size("wt") != 4:
        return copies
    rows = recv.shape[1]
    _, _, far, _ = mates()
    copies[0].wait_recv()

    def body(at):
        mine = part[pl.ds(pl.multiple_of(far * rows + at, 16), 16)].astype(F32)
        pend[pl.ds(at, 16)] = (mine + recv[0, pl.ds(at, 16)].astype(F32)).astype(BF16)

    step_rows(rows, 16, body)
    return copies + [send(pend, recv.at[2], sems, 2, "wt", far)]


def line_scatter_end(copies):
    if lax.axis_size("wt") != 4:
        arrived(copies)
    else:
        arrived(copies[1:])


def line_summed(part, recv, at, step, row0):
    if lax.axis_size("wt") != 4:
        return summed(part, recv, at, step, row0)
    total = part[pl.ds(row0 + at, step)].astype(F32)
    return total + recv[1, pl.ds(at, step)].astype(F32) + recv[2, pl.ds(at, step)].astype(F32)


def line_gather_start(whole, rows, sems):
    if lax.axis_size("wt") != 4:
        return gather_start(whole, rows, sems, "wt")
    z, mate, far, _ = mates()
    mine = whole.at[pl.ds(z * rows, rows)]
    return [send(mine, mine, sems, 0, "wt", far), send(mine, mine, sems, 1, "wt", mate)]


def line_gather_mid(whole, rows, sems, copies):
    if lax.axis_size("wt") != 4:
        return copies
    _, mate, far, _ = mates()
    copies[0].wait_recv()
    piece = whole.at[pl.ds(far * rows, rows)]
    return copies + [send(piece, piece, sems, 2, "wt", mate)]


def line_gather_end(copies):
    if lax.axis_size("wt") != 4:
        arrived(copies)
    else:
        arrived(copies[1:])


def flips():
    seq = lax.axis_index("seq")
    core, x, y = lax.rem(seq, 2), lax.rem(seq // 2, 2), seq // 4

    def at(fy, fx, fc):
        return (
            (1 - y if fy else y) * 4 + (1 - x if fx else x) * 2 + (1 - core if fc else core)
        )

    return at


def cube_sems():
    return pltpu.SemaphoreType.DMA((2, 9))


def cube_first(block, whole, sems):
    at = flips()
    mine = whole.at[at(0, 0, 0)]
    return [
        send(block, mine, sems, 0, "seq", at(0, 1, 0)),
        send(block, mine, sems, 1, "seq", at(1, 0, 0)),
        send(block, mine, sems, 2, "seq", at(0, 0, 1)),
    ]


def keep(block, whole, sem):
    copy = pltpu.make_async_copy(block, whole.at[lax.axis_index("seq")], sem)
    copy.start()
    return copy


def spread(src, dst, sems, own_sem):
    seq, n_seq = lax.axis_index("seq"), lax.axis_size("seq")
    piece = dst.shape[2]

    def columns(peer):
        return src.at[:, pl.ds(pl.multiple_of(peer * piece, piece), piece)]

    out = []
    for k in range(1, n_seq):
        peer = lax.rem(seq + k, n_seq)
        out.append(send(columns(peer), dst.at[seq], sems, k - 1, "seq", peer))
    return out, keep(columns(seq), dst, own_sem)


def cube_second(whole, sems, first):
    at = flips()
    half = whole.shape[1] // 2
    first[0].wait_recv()
    block = whole.at[at(0, 1, 0)]
    top = block.at[pl.ds(0, half)]
    sent = [
        send(top, top, sems, 3, "seq", at(1, 0, 0)),
        send(block, block, sems, 5, "seq", at(0, 0, 1)),
    ]
    first[1].wait_recv()
    block = whole.at[at(1, 0, 0)]
    low = block.at[pl.ds(half, half)]
    sent += [
        send(low, low, sems, 4, "seq", at(0, 1, 0)),
        send(block, block, sems, 6, "seq", at(0, 0, 1)),
    ]
    return sent


def cube_third(whole, sems, second):
    at = flips()
    half = whole.shape[1] // 2
    block = whole.at[at(1, 1, 0)]
    sent = []
    for slot, came in ((0, second[0]), (1, second[2])):
        came.wait_recv()
        piece = block.at[pl.ds(slot * half, half)]
        sent.append(send(piece, piece, sems, 7 + slot, "seq", at(0, 0, 1)))
    return sent


def cube_end(first, second, third):
    first[2].wait_recv()
    second[1].wait_recv()
    second[3].wait_recv()
    arrived(third)
    for group in (first, second, third):
        left(group)


def share(src, dst, sems, own_sem):
    seq, n_seq, z = lax.axis_index("seq"), lax.axis_size("seq"), lax.axis_index("wt")
    own, piece = dst.shape[2:]
    rows = src.at[pl.ds(pl.multiple_of(z * own, own), own)]

    def columns(peer):
        return rows.at[:, pl.ds(pl.multiple_of(peer * piece, piece), piece)]

    sent = []
    for k in range(1, n_seq):
        peer = lax.rem(seq + k, n_seq)
        sent.append(send(columns(peer), dst.at[seq, z], sems, k - 1, "seq", peer))
    kept = pltpu.make_async_copy(columns(seq), dst.at[seq, z], own_sem)
    kept.start()
    return sent, kept


def pass_along(dst, sems):
    z, n_wt = lax.axis_index("wt"), lax.axis_size("wt")
    lines = dst.at[:, z]
    return [send(lines, lines, sems, k - 1, "wt", lax.rem(z + k, n_wt)) for k in range(1, n_wt)]


def first_kernel(
    pair, small, cot, tok, gain, taps, bias, masks,
    w_first, cot_f, act_f, w_small, inner, prev, switch, conv, mixed, select,
    first_in, w_near, ext, halo, part, recv,
    s_pair, s_small, s_own, s_cot, s_act, s_cz, s_az, s_halo, s_scatter, s_gather,
):
    seq, n_seq = lax.axis_index("seq"), lax.axis_size("seq")
    me = lax.axis_index("wt")
    count, width = tok.shape
    chan = inner.shape[1]
    kept = [keep(pair, w_near, s_own.at[0]), keep(small, w_small, s_own.at[1])]

    def norm(at):
        v = tok[pl.ds(at, 16)].astype(F32)
        inverse = lax.rsqrt(jnp.mean(v * v, axis=-1, keepdims=True) + EPS)
        first_in[pl.ds(at, 16)] = (v * inverse * gain[...]).astype(BF16)

    step_rows(count, 16, norm)
    greet(("seq", "wt"))
    little = cube_first(small, w_small, s_small)
    sent1, kept1 = share(cot, cot_f, s_cot, s_own.at[2])
    sent2, kept2 = share(first_in, act_f, s_act, s_own.at[3])
    pair1 = cube_first(pair, w_near, s_pair)
    sent = sent1 + sent2
    arrived(sent)
    kept1.wait()
    kept2.wait()
    along = pass_along(cot_f, s_cz) + pass_along(act_f, s_az)
    little2 = cube_second(w_small, s_small, little)
    little3 = cube_third(w_small, s_small, little2)
    pair2 = cube_second(w_near, s_pair, pair1)
    pair3 = cube_third(w_near, s_pair, pair2)
    cube_end(little, little2, little3)
    cube_end(pair1, pair2, pair3)
    for copy in kept:
        copy.wait()
    far = pltpu.make_async_copy(w_near, w_first, s_own.at[0])
    far.start()

    def project(target, first_tile):
        def one(j, carry):
            columns = pl.ds(pl.multiple_of(j * UNITS, UNITS), UNITS)
            source = pl.ds(pl.multiple_of((first_tile + j) * UNITS, UNITS), UNITS)
            tile = w_near[:, :, source].reshape(width, UNITS)
            out = jnp.dot(first_in[...], tile, preferred_element_type=F32)
            target[:, columns] = out.astype(target.dtype)
            return carry

        lax.fori_loop(0, chan // UNITS, one, 0)

    project(inner, 0)
    halo[0] = (inner[count - 16 :].astype(F32) * masks[count - 16 :, 3:4]).astype(BF16)
    ahead = remote(halo.at[0], halo.at[1], s_halo, 0, "seq", lax.rem(seq + 1, n_seq))

    @pl.when(seq + 1 < n_seq)
    def _():
        ahead.start()

    @pl.when(seq == 0)
    def _():
        halo[1] = jnp.zeros_like(halo[1])

    project(switch, chan // UNITS)
    ext[16:] = inner[...].astype(F32)

    @pl.when(seq > 0)
    def _():
        ahead.wait_recv()

    ext[:16] = halo[1].astype(F32)
    prev[...] = ext[8:16]

    def convolve(at):
        v = ext[pl.ds(pl.multiple_of(at + 8, 8), 24)]
        same = masks[pl.ds(at, 16)]
        out = bias[...] + taps[0:1] * v[8:]
        for k in range(1, KC):
            out = out + taps[k : k + 1] * v[8 - k : 24 - k] * same[:, k - 1 : k]
        conv[pl.ds(at, 16)] = out
        mixed[pl.ds(at, 16)] = (out * jax.nn.sigmoid(out)).astype(BF16)

    step_rows(count, 16, convolve)
    deep = w_small.shape[1]
    all_rows = nt(w_small[...].reshape(n_seq * deep, chan), mixed[...])
    rows = part.shape[0] // n_seq
    for j in range(n_seq):
        part[j * rows : (j + 1) * rows] = all_rows[j * deep + 16 : j * deep + 16 + rows]
    first = scatter_start(part, recv, s_scatter, "wt")
    rows = recv.shape[1]
    arrived(first)
    select[pl.ds(me * rows, rows)] = summed(part, recv, 0, rows, me * rows)
    second = gather_start(select, rows, s_gather, "wt")
    arrived(second)
    arrived(along)
    far.wait()

    @pl.when(seq + 1 < n_seq)
    def _():
        ahead.wait_send()

    for group in (along, sent, first, second):
        left(group)


def first_gather(pair, small, cot, tok, gain, taps, bias, masks, rows_sel, n_wt, n_seq, ident):
    count, width = cot.shape
    chan = pair.shape[1] // 2
    lines = rows_sel * n_seq
    share_shape = jax.ShapeDtypeStruct((n_seq, n_wt, count // n_wt, width // n_seq), BF16)
    return pl.pallas_call(
        first_kernel,
        out_shape=[
            jax.ShapeDtypeStruct((n_seq,) + pair.shape, BF16),
            share_shape,
            share_shape,
            jax.ShapeDtypeStruct((n_seq,) + small.shape, BF16),
            jax.ShapeDtypeStruct((count, chan), BF16),
            jax.ShapeDtypeStruct((8, chan), F32),
            jax.ShapeDtypeStruct((count, chan), F32),
            jax.ShapeDtypeStruct((count, chan), F32),
            jax.ShapeDtypeStruct((count, chan), BF16),
            jax.ShapeDtypeStruct((lines, count), F32),
        ],
        in_specs=[ANY] * 2 + [VMEM] * 6,
        out_specs=[ANY] * 3 + [VMEM] * 7,
        scratch_shapes=[
            pltpu.VMEM((count, width), BF16),
            pltpu.VMEM((n_seq,) + pair.shape, BF16),
            pltpu.VMEM((16 + count, chan), F32),
            pltpu.VMEM((2, 16, chan), BF16),
            pltpu.VMEM((lines, count), F32),
            pltpu.VMEM((n_wt - 1, lines // n_wt, count), F32),
            cube_sems(),
            cube_sems(),
            pltpu.SemaphoreType.DMA((4,)),
            pair_sems(n_seq),
            pair_sems(n_seq),
            pair_sems(n_wt),
            pair_sems(n_wt),
            pltpu.SemaphoreType.DMA((2, 1)),
            pair_sems(n_wt),
            pair_sems(n_wt),
        ],
        compiler_params=pltpu.CompilerParams(
            collective_id=ident, has_side_effects=True, vmem_limit_bytes=VMEM_BYTES
        ),
        cost_estimate=pl.CostEstimate(flops=10**9, bytes_accessed=10**8, transcendentals=0),
    )(pair, small, cot, tok, gain[None], taps, bias[None], masks)


def ffn_kernel(x, c, wg, wu, wd, gated, acts, down, d_second, acc_down, acc_second):
    step = pl.program_id(0)

    @pl.when(step == 0)
    def _():
        acc_down[...] = jnp.zeros_like(acc_down)
        acc_second[...] = jnp.zeros_like(acc_second)

    gate = jnp.dot(x[...], wg[...], preferred_element_type=F32)
    up = jnp.dot(x[...], wu[...], preferred_element_type=F32)
    d_hidden = jnp.dot(c[...], wd[...], preferred_element_type=F32)
    sigma = jax.nn.sigmoid(gate)
    act = gate * sigma
    hidden = (act * up).astype(BF16)
    d_gate = (d_hidden * up * (sigma * (1.0 + gate * (1.0 - sigma)))).astype(BF16)
    d_up = (d_hidden * act).astype(BF16)
    acts[:, :UNITS] = hidden
    acts[:, UNITS : 2 * UNITS] = d_gate
    acts[:, 2 * UNITS : 3 * UNITS] = d_up
    acts[:, 3 * UNITS :] = gated[...]
    acc_down[...] += nt(hidden, wd[...])
    acc_second[...] += nt(d_gate, wg[...]) + nt(d_up, wu[...])

    @pl.when(step == pl.num_programs(0) - 1)
    def _():
        down[...] = acc_down[...].astype(BF16)
        d_second[...] = acc_second[...].astype(BF16)


def ffn(x, c, w_all, gated):
    tok, width = x.shape
    units, chan = w_all.shape[1] // 3, gated.shape[1]
    steps = units // UNITS
    span = 3 * UNITS + chan // steps
    whole = pl.BlockSpec((tok, width), lambda i: (0, 0))
    tile = lambda part: pl.BlockSpec((width, UNITS), lambda i: (0, part * steps + i))
    return pl.pallas_call(
        ffn_kernel,
        grid=(steps,),
        in_specs=[whole, whole, tile(0), tile(1), tile(2)]
        + [pl.BlockSpec((tok, chan // steps), lambda i: (0, i))],
        out_specs=[pl.BlockSpec((tok, span), lambda i: (0, i)), whole, whole],
        out_shape=[
            jax.ShapeDtypeStruct((tok, 3 * units + chan), BF16),
            jax.ShapeDtypeStruct((tok, width), BF16),
            jax.ShapeDtypeStruct((tok, width), BF16),
        ],
        scratch_shapes=[pltpu.VMEM((tok, width), F32)] * 2,
        compiler_params=pltpu.CompilerParams(vmem_limit_bytes=VMEM_BYTES),
        cost_estimate=pl.CostEstimate(
            flops=12 * tok * width * units, bytes_accessed=6 * width * units, transcendentals=0
        ),
    )(x, c, w_all, w_all, w_all, gated)


def grads_kernel(lefts, *refs):
    n, m = max(lefts) + 1, len(lefts)
    for which, act, out in zip(lefts, refs[n : n + m], refs[n + m :]):
        out[...] = jnp.dot(refs[which][...], act[...], preferred_element_type=F32)


def grads(left_ops, lefts, acts):
    rows, tok = left_ops[0].shape
    cols = acts[0].shape[1]
    n = len(acts)
    return pl.pallas_call(
        functools.partial(grads_kernel, lefts),
        grid=(cols // UNITS,),
        in_specs=[pl.BlockSpec((rows, tok), lambda i: (0, 0))] * len(left_ops)
        + [pl.BlockSpec((tok, UNITS), lambda i: (0, i))] * n,
        out_specs=[pl.BlockSpec((rows, UNITS), lambda i: (0, i))] * n,
        out_shape=[jax.ShapeDtypeStruct((rows, cols), F32)] * n,
        compiler_params=pltpu.CompilerParams(vmem_limit_bytes=VMEM_BYTES),
        cost_estimate=pl.CostEstimate(
            flops=2 * n * tok * rows * cols, bytes_accessed=2 * n * tok * cols, transcendentals=0
        ),
    )(*left_ops, *acts)


def wt_sum_kernel(part, out, recv, s_scatter, s_gather):
    me = lax.axis_index("wt")
    rows = recv.shape[1]
    greet(("wt",))
    first = scatter_start(part, recv, s_scatter, "wt")
    arrived(first)
    out[pl.ds(me * rows, rows)] = summed(part, recv, 0, rows, me * rows)
    second = gather_start(out, rows, s_gather, "wt")
    arrived(second)
    left(first)
    left(second)


def wt_sum(part, n_wt, ident):
    rows, cols = part.shape
    return pl.pallas_call(
        wt_sum_kernel,
        out_shape=jax.ShapeDtypeStruct((rows, cols), F32),
        in_specs=[VMEM],
        out_specs=VMEM,
        scratch_shapes=[
            pltpu.VMEM((n_wt - 1, rows // n_wt, cols), F32),
            pair_sems(n_wt),
            pair_sems(n_wt),
        ],
        compiler_params=pltpu.CompilerParams(
            collective_id=ident, has_side_effects=True, vmem_limit_bytes=VMEM_BYTES
        ),
        cost_estimate=pl.CostEstimate(flops=10**5, bytes_accessed=10**6, transcendentals=0),
    )(part)


def second_norm_kernel(part, tok, gain, out, res, recv, pend, s_scatter, s_gather):
    me = lax.axis_index("wt")
    rows = recv.shape[1]
    greet(("wt",))
    first = line_scatter_start(part, recv, s_scatter)
    first = line_scatter_mid(part, recv, pend, s_scatter, first)
    line_scatter_end(first)
    row0 = me * rows

    def body(at):
        r = tok[pl.ds(at, 16)] + line_summed(part, recv, at, 16, row0)
        res[pl.ds(at, 16)] = r
        inverse = lax.rsqrt(jnp.mean(r * r, axis=-1, keepdims=True) + EPS)
        out[pl.ds(pl.multiple_of(row0 + at, 16), 16)] = (r * inverse * gain[...]).astype(BF16)

    step_rows(rows, 16, body)
    second = line_gather_start(out, rows, s_gather)
    second = line_gather_mid(out, rows, s_gather, second)
    line_gather_end(second)
    left(first)
    left(second)


def second_norm(part, tok_own, gain, n_wt, ident):
    rows, cols = part.shape
    own = rows // n_wt
    return pl.pallas_call(
        second_norm_kernel,
        out_shape=[
            jax.ShapeDtypeStruct((rows, cols), BF16),
            jax.ShapeDtypeStruct((own, cols), F32),
        ],
        in_specs=[VMEM] * 3,
        out_specs=[VMEM] * 2,
        scratch_shapes=[
            pltpu.VMEM((n_wt - 1, own, cols), BF16),
            pltpu.VMEM((own, cols), BF16),
            pair_sems(n_wt),
            pair_sems(n_wt),
        ],
        compiler_params=pltpu.CompilerParams(
            collective_id=ident, has_side_effects=True, vmem_limit_bytes=VMEM_BYTES
        ),
        cost_estimate=pl.CostEstimate(flops=10**6, bytes_accessed=10**8, transcendentals=0),
    )(part, tok_own, gain[None])


def norm_back_rows(grad, vals, gain):
    inverse = lax.rsqrt(jnp.mean(vals * vals, axis=-1, keepdims=True) + EPS)
    normed = vals * inverse
    scaled = grad * gain
    mean = jnp.mean(scaled * normed, axis=-1, keepdims=True)
    return inverse * (scaled - normed * mean), grad * normed


def second_back_kernel(n_spread, part, res, cot, gain, *refs):
    srcs, refs = refs[:n_spread], refs[n_spread:]
    out, d_res, gain_grad = refs[:3]
    dsts, refs = refs[3 : 3 + n_spread], refs[3 + n_spread :]
    recv, pend, s_scatter, s_gather = refs[:4]
    me = lax.axis_index("wt")
    rows = recv.shape[1]
    greet(("wt", "seq") if n_spread else ("wt",))
    first = line_scatter_start(part, recv, s_scatter)
    spreads = [
        spread(srcs[i], dsts[i], refs[4 + 2 * i], refs[5 + 2 * i]) for i in range(n_spread)
    ]
    gain_grad[...] = jnp.zeros_like(gain_grad)
    first = line_scatter_mid(part, recv, pend, s_scatter, first)
    line_scatter_end(first)
    row0 = me * rows

    def body(at):
        grad = line_summed(part, recv, at, 16, row0)
        back, prod = norm_back_rows(grad, res[pl.ds(at, 16)], gain[...])
        gain_grad[...] += prod[:8] + prod[8:]
        d = cot[pl.ds(at, 16)] + back
        d_res[pl.ds(at, 16)] = d
        out[pl.ds(pl.multiple_of(row0 + at, 16), 16)] = d.astype(BF16)

    step_rows(rows, 16, body)
    second = line_gather_start(out, rows, s_gather)
    second = line_gather_mid(out, rows, s_gather, second)
    line_gather_end(second)
    for sent, kept in spreads:
        kept.wait()
        arrived(sent)
        left(sent)
    left(first)
    left(second)


def second_back(part, res, cot_own, gain, srcs, n_wt, n_seq, ident):
    rows, cols = part.shape
    own = rows // n_wt
    return pl.pallas_call(
        functools.partial(second_back_kernel, len(srcs)),
        out_shape=[
            jax.ShapeDtypeStruct((rows, cols), BF16),
            jax.ShapeDtypeStruct((own, cols), F32),
            jax.ShapeDtypeStruct((8, cols), F32),
        ]
        + [jax.ShapeDtypeStruct((n_seq, rows, cols // n_seq), BF16)] * len(srcs),
        in_specs=[VMEM] * (4 + len(srcs)),
        out_specs=[VMEM] * 3 + [ANY] * len(srcs),
        scratch_shapes=[
            pltpu.VMEM((n_wt - 1, own, cols), BF16),
            pltpu.VMEM((own, cols), BF16),
            pair_sems(n_wt),
            pair_sems(n_wt),
        ]
        + [pair_sems(n_seq), pltpu.SemaphoreType.DMA] * len(srcs),
        compiler_params=pltpu.CompilerParams(
            collective_id=ident, has_side_effects=True, vmem_limit_bytes=VMEM_BYTES
        ),
        cost_estimate=pl.CostEstimate(flops=10**6, bytes_accessed=10**8, transcendentals=0),
    )(part, res, cot_own, gain[None], *srcs)


def last_kernel(cube, part, tok, d_res, gain, gain_grad2, sel, stp, taps, decays, bias3, line, *refs):
    blocks, refs = refs[:cube], refs[cube:]
    if cube:
        cot_t, second_t, branch_t, acts, refs = refs[0], refs[1], refs[2], refs[3], refs[4:]
    out, block_out, sel_out, stp_out, chan_out, gains_out = refs[:6]
    wholes, refs = refs[6 : 6 + cube], refs[6 + cube :]
    if cube:
        grad_outs, refs = refs[:4], refs[4:]
        tile, s_tile, refs = refs[0], refs[1], refs[2:]
        width = tile.shape[2]
        tiles = acts.shape[1] // width

        def fetch(j, slot):
            columns = acts.at[:, pl.ds(pl.multiple_of(j * width, width), width)]
            return pltpu.make_async_copy(columns, tile.at[slot], s_tile.at[slot])

        def one_tile(j, carry):
            slot = lax.rem(j, 2)

            @pl.when(j + 1 < tiles)
            def _():
                fetch(j + 1, 1 - slot).start()

            fetch(j, slot).wait()
            at = 0
            for left_op, out_ref in zip((cot_t, second_t, second_t, branch_t), grad_outs):
                wide = out_ref.shape[1] // tiles
                out_ref[:, pl.ds(pl.multiple_of(j * wide, wide), wide)] = jnp.dot(
                    left_op[...], tile[slot, :, at : at + wide], preferred_element_type=F32
                )
                at += wide
            return carry

        fetch(0, 0).start()
    recv, pend, recv_sel, recv_stp, recv_chan, pack, gain_buf, recv_gz, recv_gs = refs[:9]
    s_scatter, s_gather, s_sel, s_stp, s_chan, s_cg, s_gz, s_gs, s_block = refs[9:18]
    refs = refs[18:]
    me, n_wt = lax.axis_index("wt"), lax.axis_size("wt")
    seq, n_seq = lax.axis_index("seq"), lax.axis_size("seq")
    rows = recv.shape[1]
    block_out[pl.ds(pl.multiple_of(me * rows, 16), rows)] = line[...]
    greet(("wt", "seq"))
    first = line_scatter_start(part, recv, s_scatter)
    share = -(-(KC + NS + 3) // n_seq)
    lines = [(taps, i) for i in range(KC)] + [(decays, i) for i in range(NS)]
    lines += [(bias3, i) for i in range(3)]
    for at, (ref, i) in enumerate(lines):
        pack[at // share, at % share : at % share + 1] = ref[i : i + 1]
    smalls = []
    for src, dst, sems in ((sel, recv_sel, s_sel), (stp, recv_stp, s_stp), (pack, recv_chan, s_chan)):
        for k in range(1, n_seq):
            peer = lax.rem(seq + k, n_seq)
            smalls.append(send(src.at[peer], dst.at[k - 1], sems, k - 1, "seq", peer))
    cubes = []
    for i in range(cube):
        s_cube, s_own = refs[2 * i : 2 * i + 2]
        cubes.append([cube_first(blocks[i], wholes[i], s_cube), s_cube, wholes[i]])
        cubes[-1].append(keep(blocks[i], wholes[i], s_own))
    if cube:
        lax.fori_loop(0, 3, one_tile, 0)
    first = line_scatter_mid(part, recv, pend, s_scatter, first)
    if cube:
        lax.fori_loop(3, tiles - 2, one_tile, 0)
    arrived(smalls)
    for src, recv_one, one_out in ((sel, recv_sel, sel_out), (stp, recv_stp, stp_out)):
        total = src[seq].astype(F32)
        for k in range(n_seq - 1):
            total = total + recv_one[k].astype(F32)
        one_out[...] = total
    total = pack[seq]
    for k in range(n_seq - 1):
        total = total + recv_chan[k]
    chan_out[seq] = total
    mine = chan_out.at[seq]
    chans = [
        send(mine, mine, s_cg, k - 1, "seq", lax.rem(seq + k, n_seq)) for k in range(1, n_seq)
    ]
    line_scatter_end(first)
    row0 = me * rows
    gain_buf[...] = jnp.zeros_like(gain_buf)

    def body(at):
        grad = line_summed(part, recv, at, 16, row0)
        back, prod = norm_back_rows(grad, tok[pl.ds(at, 16)], gain[...])
        gain_buf[...] += prod[:8] + prod[8:]
        out[pl.ds(pl.multiple_of(row0 + at, 16), 16)] = (d_res[pl.ds(at, 16)] + back).astype(BF16)

    step_rows(rows, 16, body)
    second = line_gather_start(out, rows, s_gather)
    third = line_gather_start(block_out, rows, s_block)
    high = recv_gz.shape[1] // 2
    for i, grad in enumerate((gain_buf, gain_grad2)):
        line = jnp.sum(grad[...], axis=0, keepdims=True)
        for t in range(high):
            recv_gz[me, i * high + t : i * high + t + 1] = line[:, t * 128 : (t + 1) * 128]
    mine_z = recv_gz.at[me]
    zs = [send(mine_z, mine_z, s_gz, k - 1, "wt", lax.rem(me + k, n_wt)) for k in range(1, n_wt)]
    cubes2 = [cube_second(whole, sems, one) for one, sems, whole, _ in cubes]
    if cube:
        lax.fori_loop(tiles - 2, tiles, one_tile, 0)
    second = line_gather_mid(out, rows, s_gather, second)
    third = line_gather_mid(block_out, rows, s_block, third)
    arrived(zs)
    total = recv_gz[0]
    for pos in range(1, n_wt):
        total = total + recv_gz[pos]
    recv_gs[seq] = total
    mine_s = recv_gs.at[seq]
    ss = [
        send(mine_s, mine_s, s_gs, k - 1, "seq", lax.rem(seq + k, n_seq)) for k in range(1, n_seq)
    ]
    cubes3 = [cube_third(whole, sems, two) for (_, sems, whole, _), two in zip(cubes, cubes2)]
    arrived(ss)
    total = recv_gs[0]
    for pos in range(1, n_seq):
        total = total + recv_gs[pos]
    gains_out[...] = total
    arrived(chans)
    for (one, _, _, kept), two, three in zip(cubes, cubes2, cubes3):
        cube_end(one, two, three)
        kept.wait()
    line_gather_end(second)
    line_gather_end(third)
    for group in (first, second, third, smalls, chans, zs, ss):
        left(group)


def last(part, tok_own, d_res, gain, gain_grad2, sel, stp, taps, decays, bias3, line, blocks, more, n_wt, n_seq, ident):
    rows, cols = part.shape
    own = rows // n_wt
    chan = taps.shape[1]
    if more:
        deep, tok_all = more[0].shape
        units = (more[3].shape[1] - chan) // 3
        span = more[3].shape[1] // (units // UNITS)
    return pl.pallas_call(
        functools.partial(last_kernel, len(blocks)),
        out_shape=[
            jax.ShapeDtypeStruct((rows, cols), BF16),
            jax.ShapeDtypeStruct((rows, cols), BF16),
            jax.ShapeDtypeStruct(sel.shape[1:], F32),
            jax.ShapeDtypeStruct(stp.shape[1:], F32),
            jax.ShapeDtypeStruct((n_seq, 8, chan), F32),
            jax.ShapeDtypeStruct((2 * cols // 128, 128), F32),
        ]
        + [jax.ShapeDtypeStruct((n_seq,) + a.shape, BF16) for a in blocks]
        + ([jax.ShapeDtypeStruct((deep, w), F32) for w in (units, units, units, chan)] if more else []),
        in_specs=[VMEM] * 11 + [ANY] * len(blocks) + ([VMEM, VMEM, VMEM, ANY] if more else []),
        out_specs=[VMEM] * 6 + [ANY] * len(blocks) + ([VMEM] * 4 if more else []),
        scratch_shapes=(
            [pltpu.VMEM((2, tok_all, span), BF16), pltpu.SemaphoreType.DMA((2,))]
            if more
            else []
        )
        + [
            pltpu.VMEM((n_wt - 1, own, cols), BF16),
            pltpu.VMEM((own, cols), BF16),
            pltpu.VMEM((n_seq - 1,) + sel.shape[1:], BF16),
            pltpu.VMEM((n_seq - 1,) + stp.shape[1:], BF16),
            pltpu.VMEM((n_seq - 1, 8, chan), F32),
            pltpu.VMEM((n_seq, 8, chan), F32),
            pltpu.VMEM((8, cols), F32),
            pltpu.VMEM((n_wt, 2 * cols // 128, 128), F32),
            pltpu.VMEM((n_seq, 2 * cols // 128, 128), F32),
            pair_sems(n_wt),
            pair_sems(n_wt),
            pair_sems(n_seq),
            pair_sems(n_seq),
            pair_sems(n_seq),
            pair_sems(n_seq),
            pair_sems(n_wt),
            pair_sems(n_seq),
            pair_sems(n_wt),
        ]
        + [cube_sems(), pltpu.SemaphoreType.DMA] * len(blocks),
        compiler_params=pltpu.CompilerParams(
            collective_id=ident, has_side_effects=True, vmem_limit_bytes=VMEM_BYTES
        ),
        cost_estimate=pl.CostEstimate(flops=10**6, bytes_accessed=10**8, transcendentals=0),
    )(part, tok_own, d_res, gain[None], gain_grad2, sel, stp, taps, decays, bias3, line, *blocks, *more)


def load(ref):
    return tuple(ref[n] for n in range(NS))


def store(ref, values):
    for n in range(NS):
        ref[n] = values[n]


def fold(mine, box, recv, a2, carried, backward):
    n, me = lax.axis_size("seq"), lax.axis_index("seq")
    carried[...] = jnp.zeros_like(carried)
    for k in range(n - 1, 0, -1):

        @pl.when((me + k < n) if backward else (me >= k))
        def _():
            giver = me + k if backward else me - k
            remote(mine, recv.at[k - 1], box, k - 1, "seq", giver).wait_recv()
            through = recv[k - 1, NS]
            for s in range(NS):
                carried[s] = (
                    jnp.exp2(a2[s] * through) * carried[s] + recv[k - 1, s]
                )


def hand_on(mine, recv, box, backward):
    n, me = lax.axis_size("seq"), lax.axis_index("seq")
    for k in range(1, n):

        @pl.when((me >= k) if backward else (me + k < n))
        def _():
            peer = me - k if backward else me + k
            send(mine, recv.at[k - 1], box, k - 1, "seq", peer)


def handed(mine, recv, box, backward):
    n, me = lax.axis_size("seq"), lax.axis_index("seq")
    for k in range(1, n):

        @pl.when((me >= k) if backward else (me + k < n))
        def _():
            peer = me - k if backward else me + k
            remote(mine, recv.at[k - 1], box, k - 1, "seq", peer).wait_send()


def fwd_kernel(sa, dx, wr, a2, y, h0, mine, recv, box):
    tok = sa.shape[0]
    greet(("seq",))

    def end(t, carry):
        s, d = sa[t], dx[t]
        h, total = carry
        return (
            tuple(jnp.exp2(s * a2[n]) * h[n] + wr[n, t] * d for n in range(NS)),
            total + s,
        )

    zero = jnp.zeros(sa.shape[1:], F32)
    ends, total = lax.fori_loop(0, tok, end, ((zero,) * NS, zero), unroll=4)
    store(mine, ends)
    mine[NS] = total
    hand_on(mine, recv, box, False)
    fold(mine, box, recv, a2, h0, False)

    def body(t, h):
        s, d = sa[t], dx[t]
        new, sums = [], [None] * 4
        for n in range(NS):
            hn = jnp.exp2(s * a2[n]) * h[n] + wr[n, t] * d
            new.append(hn)
            c = wr[NS + n, t] * hn
            sums[n % 4] = c if sums[n % 4] is None else sums[n % 4] + c
        y[t] = (sums[0] + sums[1]) + (sums[2] + sums[3])
        return tuple(new)

    lax.fori_loop(0, tok, body, load(h0), unroll=4)
    handed(mine, recv, box, False)


def fwd_scan(sa, dx, wr, a2, n_seq, ident):
    tok, high = sa.shape[:2]
    return pl.pallas_call(
        fwd_kernel,
        out_shape=[
            jax.ShapeDtypeStruct((tok, high, 128), F32),
            jax.ShapeDtypeStruct((NS, high, 128), F32),
        ],
        in_specs=[VMEM, VMEM, SMEM, VMEM],
        out_specs=[VMEM] * 2,
        scratch_shapes=[
            pltpu.VMEM((NS + 1, high, 128), F32),
            pltpu.VMEM((n_seq - 1, NS + 1, high, 128), F32),
            pair_sems(n_seq),
        ],
        compiler_params=pltpu.CompilerParams(
            collective_id=ident, has_side_effects=True, vmem_limit_bytes=VMEM_BYTES
        ),
        cost_estimate=pl.CostEstimate(
            flops=10**8, bytes_accessed=8 * 10**7, transcendentals=2 * tok * NS * 1024
        ),
    )(sa, dx, wr, a2)


def bwd_kernel(
    cube, sa, dx, wr, do, a2, h0, part, res, *refs
):
    src, refs = refs[:cube], refs[cube:]
    along, ds2, grad_a, sums, out = refs[:5]
    dst, refs = refs[5 : 5 + cube], refs[5 + cube :]
    hs, qw, qr, pw, pr, g0, mine, recv, recv_z, box, s_scatter = refs[:11]
    tok = sa.shape[0]
    chunk = qw.shape[0] // (NS * 8)
    greet(("wt", "seq"))
    first = scatter_start(part, recv_z, s_scatter, "wt")

    def end(i, carry):
        t = tok - 1 - i
        s, d = sa[t], do[t]
        g, total = carry
        return (
            tuple(jnp.exp2(s * a2[n]) * (g[n] + wr[NS + n, t] * d) for n in range(NS)),
            total + s,
        )

    zero = jnp.zeros(sa.shape[1:], F32)
    ends, total = lax.fori_loop(0, tok, end, ((zero,) * NS, zero), unroll=4)
    store(mine, ends)
    mine[NS] = total
    hand_on(mine, recv, box, True)
    if cube:
        s_seq, s_wt, s_own = refs[11:]
        sent, kept = share(src[0], dst[0], s_seq, s_own)

    def again(t, h):
        s, d = sa[t], dx[t]
        new = []
        for n in range(NS):
            hs[t, n] = h[n]
            new.append(jnp.exp2(s * a2[n]) * h[n] + wr[n, t] * d)
        return tuple(new)

    lax.fori_loop(0, tok, again, load(h0), unroll=2)

    fold(mine, box, recv, a2, g0, True)
    if cube:
        arrived(sent)
        kept.wait()
        passed = pass_along(dst[0], s_wt)
    grad_a[...] = jnp.zeros_like(grad_a)

    def one_chunk(j, g):
        base = (tok // chunk - 1 - j) * chunk

        def body(i, g):
            at = chunk - 1 - i
            t = base + at
            s, d, o = sa[t], dx[t], do[t]
            al = d2 = None
            new = []
            for n in range(NS):
                hp = hs[t, n]
                f = jnp.exp2(s * a2[n])
                hn = f * hp + wr[n, t] * d
                gn = wr[NS + n, t] * o + g[n]
                adj = f * gn
                new.append(adj)
                th = adj * hp
                grad_a[n] += th * s
                x = wr[n, t] * gn
                al = x if al is None else al + x
                x = a2[n] * th
                d2 = x if d2 is None else d2 + x
                row = pl.multiple_of((at * NS + n) * 8, 8)
                qw[pl.ds(row, 8), :] = gn * d
                qr[pl.ds(row, 8), :] = hn * o
            along[t] = al
            ds2[t] = d2
            return tuple(new)

        g = lax.fori_loop(0, chunk, body, g)

        def lanes(i, carry):
            for q, p in ((qw, pw), (qr, pr)):
                acc = q[pl.ds(i * NS * 8, NS, stride=8), :]
                for s in range(1, 8):
                    acc = acc + q[pl.ds(i * NS * 8 + s, NS, stride=8), :]
                p[pl.ds(pl.multiple_of(i * NS, NS), NS), :] = acc
            return carry

        lax.fori_loop(0, chunk, lanes, 0, unroll=4)
        ones = jnp.ones((8, 128), BF16)
        for which, p in enumerate((pw, pr)):
            high = p[...].astype(BF16)
            low = (p[...] - high.astype(F32)).astype(BF16)
            row = which * (tok // chunk) + base // chunk
            sums[pl.ds(row, 1), :] = (nt(ones, high) + nt(ones, low))[:1]
        return g

    lax.fori_loop(0, tok // chunk, one_chunk, load(g0))
    handed(mine, recv, box, True)
    arrived(first)
    rows = recv_z.shape[1]
    row0 = lax.axis_index("wt") * rows

    def block_rows(at):
        out[pl.ds(at, 16)] = (res[pl.ds(at, 16)] + summed(part, recv_z, at, 16, row0)).astype(BF16)

    step_rows(rows, 16, block_rows)
    left(first)
    if cube:
        arrived(passed)
        left(sent)
        left(passed)


def bwd_scan(sa, dx, wr, do, a2, h0, part, res, src, n_wt, n_seq, ident):
    tok, high = sa.shape[:2]
    rows, cols = part.shape
    chunk = 32
    return pl.pallas_call(
        functools.partial(bwd_kernel, len(src)),
        out_shape=[
            jax.ShapeDtypeStruct((tok, high, 128), F32),
            jax.ShapeDtypeStruct((tok, high, 128), F32),
            jax.ShapeDtypeStruct((NS, high, 128), F32),
            jax.ShapeDtypeStruct((2 * tok // chunk, chunk * NS), F32),
            jax.ShapeDtypeStruct((rows // n_wt, cols), BF16),
        ]
        + [jax.ShapeDtypeStruct((n_seq, n_wt, rows // n_wt, cols // n_seq), BF16)] * len(src),
        in_specs=[VMEM, VMEM, SMEM] + [VMEM] * (5 + len(src)),
        out_specs=[VMEM] * 5 + [ANY] * len(src),
        scratch_shapes=[
            pltpu.VMEM((tok, NS, high, 128), F32),
            pltpu.VMEM((chunk * NS * 8, 128), F32),
            pltpu.VMEM((chunk * NS * 8, 128), F32),
            pltpu.VMEM((chunk * NS, 128), F32),
            pltpu.VMEM((chunk * NS, 128), F32),
            pltpu.VMEM((NS, high, 128), F32),
            pltpu.VMEM((NS + 1, high, 128), F32),
            pltpu.VMEM((n_seq - 1, NS + 1, high, 128), F32),
            pltpu.VMEM((n_wt - 1, rows // n_wt, cols), BF16),
            pair_sems(n_seq),
            pair_sems(n_wt),
        ]
        + [pair_sems(n_seq), pair_sems(n_wt), pltpu.SemaphoreType.DMA] * len(src),
        compiler_params=pltpu.CompilerParams(
            collective_id=ident, has_side_effects=True, vmem_limit_bytes=VMEM_BYTES
        ),
        cost_estimate=pl.CostEstimate(
            flops=10**8, bytes_accessed=15 * 10**7, transcendentals=3 * tok * NS * 1024
        ),
    )(sa, dx, wr, do, a2, h0, part, res, *src)


def gather(block):
    return lax.all_gather(block, "seq", axis=0, tiled=True)


def from_behind(block, axis, distance):
    devices = range(lax.axis_size(axis))
    route = [(i - distance, i) for i in devices if i - distance in devices]
    return lax.ppermute(block, axis, route)


def contract(left_op, right_op, pattern):
    return jnp.einsum(pattern, left_op, right_op, preferred_element_type=F32)


def silu_slope(values):
    sigma = jax.nn.sigmoid(values)
    return sigma * (1.0 + values * (1.0 - sigma))


def tiles(rows):
    return rows.reshape(rows.shape[0], rows.shape[1] // 128, 128)


def flat(rows):
    return rows.reshape(rows.shape[0], rows.shape[1] * rows.shape[2])


def local(
    tokens,
    cotangent,
    doc_start,
    premix_gain,
    inner_proj,
    switch_proj,
    conv_taps,
    conv_bias,
    select_proj,
    step_proj,
    step_bias,
    decay_log,
    skip_gain,
    mixer_out,
    preffn_gain,
    ffn_gate,
    ffn_up,
    ffn_down,
):
    tok_count, width = tokens.shape
    chan = inner_proj.shape[1]
    units = ffn_gate.shape[1]
    edge = KC - 1
    n_seq, n_wt = lax.axis_size("seq"), lax.axis_size("wt")
    z = lax.axis_index("wt")
    own = tok_count // n_wt
    cube = n_seq == 8 and n_seq * tok_count <= width

    rows_sel, rows_step = select_proj.shape[0], step_proj.shape[0]
    goes_on = (1 - doc_start).astype(F32)
    before = jnp.concatenate([jnp.ones((edge,), F32), goes_on])
    after = jnp.concatenate([goes_on, jnp.ones((edge,), F32)])

    def same_back(lag):
        same = jnp.ones_like(goes_on)
        for j in range(lag):
            same = same * before[edge - j : edge - j + tok_count]
        return same[:, None]

    def same_ahead(lag):
        same = jnp.ones_like(goes_on)
        for j in range(1, lag + 1):
            same = same * after[j : j + tok_count]
        return same[:, None]

    one = jnp.ones((edge - 1,), F32)
    last_two, head = goes_on[-2:], goes_on[:edge]
    tail_keep = jnp.concatenate([last_two, one[:1]]) * jnp.concatenate([last_two[1:], one])
    head_keep = (
        head
        * jnp.concatenate([one[:1], head[:2]])
        * jnp.concatenate([one, head[:1]])
    )
    if cube:
        fill = jnp.zeros((-(rows_sel + rows_step) % 32, chan), BF16)
        ones = jnp.ones((tok_count - edge,), F32)
        columns = [same_back(k)[:, 0] for k in range(1, KC)]
        columns += [jnp.concatenate([ones, tail_keep])] * (9 - KC)
        (
            w_first, cot_f, first_f, w_small,
            inner_act, prev_rows, switch, conv_out, mixed_in, select,
        ) = first_gather(
            jnp.concatenate([inner_proj, switch_proj], axis=1),
            jnp.concatenate([step_proj, select_proj, fill], axis=0),
            cotangent, tokens, premix_gain, conv_taps, conv_bias,
            jnp.stack(columns, axis=1), rows_sel, n_wt, n_seq, 7,
        )
        w_first = w_first.reshape(width, 2 * chan)
        w_mix = gather(mixer_out)
        prev_rows = prev_rows[8 - edge :]
    else:
        token_vals = tokens.astype(F32)
        first_inv = lax.rsqrt(jnp.mean(token_vals * token_vals, axis=-1, keepdims=True) + EPS)
        first_in = (token_vals * first_inv * premix_gain).astype(BF16)
        w_mixer = gather(jnp.concatenate([inner_proj, switch_proj, mixer_out], axis=1))
        w_first, w_mix = w_mixer[:, : 2 * chan], w_mixer[:, 2 * chan :]
        w_small = lax.all_gather(jnp.concatenate([step_proj, select_proj], axis=0), "seq", axis=0)
    w_all = gather(jnp.concatenate([ffn_gate, ffn_up, ffn_down], axis=1))
    w_step = w_small[:, :rows_step].reshape(-1, chan)
    w_select = w_small[:, rows_step : rows_step + rows_sel].reshape(-1, chan)
    if not cube:
        both = contract(first_in, w_first, "td,dc->tc")
        inner_act = both[:, :chan].astype(BF16)
        switch = both[:, chan:]
        prev_rows = from_behind(inner_act[-edge:] * tail_keep[:, None].astype(BF16), "seq", 1)
        extended = jnp.concatenate([prev_rows, inner_act], axis=0).astype(F32)
        conv_out = jnp.zeros((tok_count, chan), F32) + conv_bias[None, :]
        for offset in range(KC):
            conv_out = (
                conv_out
                + conv_taps[offset][None, :]
                * extended[edge - offset : edge - offset + tok_count]
                * same_back(offset)
            )
        mixed_in = jax.nn.silu(conv_out).astype(BF16)
        select = wt_sum(contract(w_select, mixed_in, "jc,tc->jt"), n_wt, 0)
    mixed_f = mixed_in.astype(F32)
    extended = jnp.concatenate([prev_rows.astype(F32), inner_act.astype(F32)], axis=0)
    low_rank = select[:R].astype(BF16)
    write_read = select[R:]
    step_pre = contract(low_rank, w_step, "rt,rc->tc") + step_bias[None, :]
    step_size = jax.nn.softplus(step_pre)
    decay = -jnp.exp(decay_log)
    decay2 = tiles(decay * LOG2E)
    step_a = tiles(jnp.where(doc_start[:, None] > 0, FAR, step_size))
    drive = tiles(step_size * mixed_f)
    scan_out, carried_in = fwd_scan(step_a, drive, write_read, decay2, n_seq, 1)

    scanned = flat(scan_out) + skip_gain[None, :] * mixed_f
    switch_act = jax.nn.silu(switch)
    gated = (scanned * switch_act).astype(BF16)
    mix_part = contract(gated, w_mix, "tc,dc->td").astype(BF16)
    tokens_own = lax.dynamic_slice_in_dim(tokens, z * own, own, 0).astype(F32)
    cot_own = lax.dynamic_slice_in_dim(cotangent, z * own, own, 0).astype(F32)
    second_in, residual = second_norm(mix_part, tokens_own, preffn_gain, n_wt, 2)
    if cube:
        line_up = lambda v: v.reshape(n_seq * tok_count, v.shape[-1])
        second_in, cot_own, head_keep, cot_t, first_t = lax.optimization_barrier(
            (second_in, cot_own, head_keep, line_up(cot_f).T, line_up(first_f).T)
        )
    acts, down_part, d_second = ffn(second_in, cotangent, w_all, gated)
    d_branch, d_residual, grad_preffn, *second_all = second_back(
        d_second, residual, cot_own, preffn_gain, (second_in,) if cube else (), n_wt, n_seq, 3
    )
    d_gated = contract(d_branch, w_mix, "td,dc->tc")
    d_scanned = d_gated * switch_act
    d_switch = (d_gated * scanned * silu_slope(switch)).astype(BF16)
    grad_skip = jnp.sum(d_scanned * mixed_f, axis=0)
    along, through_sum, grad_decay, d_write_read, block_own, *branch_all = bwd_scan(
        step_a, drive, write_read, tiles(d_scanned), decay2, carried_in,
        down_part, residual, (d_branch,) if cube else (), n_wt, n_seq, 4,
    )
    along = flat(along)
    d_step = along * mixed_f + flat(through_sum) * (1.0 / LOG2E)
    grad_decay_log = flat(grad_decay) * decay
    d_pre = d_step * jax.nn.sigmoid(step_pre)
    grad_step_bias = jnp.sum(d_pre, axis=0)
    d_pre_low = d_pre.astype(BF16)
    pad_rows = lambda v: jnp.pad(
        v.reshape(n_seq, -1, tok_count), ((0, 0), (0, -(v.shape[0] // n_seq) % 16), (0, 0))
    ).reshape(-1, tok_count)
    grad_step = contract(pad_rows(low_rank), d_pre_low, "rt,tc->rc").astype(BF16)
    d_select = wt_sum(
        jnp.concatenate(
            [
                contract(w_step, d_pre_low, "rc,tc->rt"),
                d_write_read.reshape(2, tok_count, NS).swapaxes(1, 2).reshape(2 * NS, tok_count),
            ],
            axis=0,
        ),
        n_wt,
        5,
    )
    d_select = d_select.astype(BF16)
    grad_select = contract(pad_rows(d_select), mixed_in, "jt,tc->jc").astype(BF16)
    d_mixed = (
        along * step_size
        + skip_gain[None, :] * d_scanned
        + contract(d_select, w_select, "jt,jc->tc")
    )
    d_conv = (d_mixed * silu_slope(conv_out)).astype(BF16)
    d_conv_f = d_conv.astype(F32)
    grad_conv_bias = jnp.sum(d_conv_f, axis=0)
    next_rows = from_behind(d_conv[:edge] * head_keep[:, None].astype(BF16), "seq", -1)
    ext_grad = jnp.concatenate([d_conv, next_rows], axis=0).astype(F32)
    d_inner = jnp.zeros_like(d_conv_f)
    taps_rows = []
    for offset in range(KC):
        taps_rows.append(
            jnp.sum(
                d_conv_f
                * extended[edge - offset : edge - offset + tok_count]
                * same_back(offset),
                axis=0,
            )
        )
        d_inner = (
            d_inner
            + conv_taps[offset][None, :]
            * ext_grad[offset : offset + tok_count]
            * same_ahead(offset)
        )
    d_inner_low = d_inner.astype(BF16)
    d_first = contract(
        jnp.concatenate([d_inner_low, d_switch], axis=1), w_first, "tc,dc->td"
    ).astype(BF16)
    more = ()
    if cube:
        more = (cot_t, line_up(second_all[0]).T, line_up(branch_all[0]).T, gather(acts))
    tokens_grad, block_out, out_select, out_step, by_chan, gains, *others = last(
        d_first, tokens_own, d_residual, premix_gain, grad_preffn,
        grad_select.reshape(n_seq, -1, chan), grad_step.reshape(n_seq, -1, chan),
        jnp.stack(taps_rows, axis=0), grad_decay_log,
        jnp.stack([grad_conv_bias, grad_step_bias, grad_skip]), block_own,
        (d_switch, d_inner_low) if cube else (), more, n_wt, n_seq, 6,
    )
    share = -(-(KC + NS + 3) // n_seq)
    by_chan = by_chan[:, :share].reshape(n_seq * share, chan)
    gains = gains.reshape(2, width)
    if cube:
        out_down, out_gate, out_up, out_mix = others[2:]
        out_switch, out_inner = grads(
            (first_t,), (0, 0), (line_up(others[0]), line_up(others[1]))
        )
    else:
        scatter = lambda v: lax.psum_scatter(v, "seq", scatter_dimension=0, tiled=True)
        by_unit = acts.reshape(tok_count, units // UNITS, -1)
        hidden, d_gate, d_up = [
            by_unit[:, :, i * UNITS : (i + 1) * UNITS].reshape(tok_count, units) for i in range(3)
        ]
        out_down = scatter(contract(cotangent, hidden, "td,tf->df"))
        out_gate = scatter(contract(second_in, d_gate, "td,tf->df"))
        out_up = scatter(contract(second_in, d_up, "td,tf->df"))
        out_mix = scatter(contract(d_branch, gated, "td,tc->dc"))
        out_switch = scatter(contract(first_in, d_switch, "td,tc->dc"))
        out_inner = scatter(contract(first_in, d_inner_low, "td,tc->dc"))
    return (
        block_out,
        tokens_grad,
        gains[0],
        out_inner,
        out_switch,
        by_chan[:KC],
        by_chan[KC + NS],
        out_select[:rows_sel],
        out_step[:rows_step],
        by_chan[KC + NS + 1],
        by_chan[KC : KC + NS],
        by_chan[KC + NS + 2],
        out_mix,
        gains[1],
        out_gate,
        out_up,
        out_down,
    )


def solution(mesh):
    placed = (
        P("seq", None),
        P("seq", None),
        P("seq"),
        P(),
        P("seq", "wt"),
        P("seq", "wt"),
        P(None, "wt"),
        P("wt"),
        P("seq", "wt"),
        P("seq", "wt"),
        P("wt"),
        P(None, "wt"),
        P("wt"),
        P("seq", "wt"),
        P(),
        P("seq", "wt"),
        P("seq", "wt"),
        P("seq", "wt"),
    )
    return jax.shard_map(
        local,
        mesh=mesh,
        in_specs=placed,
        out_specs=(
            P("seq", None),
            P("seq", None),
            P(),
            P("seq", "wt"),
            P("seq", "wt"),
            P(None, "wt"),
            P("wt"),
            P("seq", "wt"),
            P("seq", "wt"),
            P("wt"),
            P(None, "wt"),
            P("wt"),
            P("seq", "wt"),
            P(),
            P("seq", "wt"),
            P("seq", "wt"),
            P("seq", "wt"),
        ),
        check_vma=False,
    )
```

```python
import functools

import jax
import jax.numpy as jnp
from jax import lax
from jax.experimental import pallas as pl
from jax.experimental.pallas import tpu as pltpu
from jax.sharding import PartitionSpec as P

NS = 16
R = 128
KC = 4
EPS = 1e-05
F32 = jnp.float32
BF16 = jnp.bfloat16
LOG2E = 1.4426950408889634
FAR = 1e30
MESH = pl.DeviceIdType.MESH
VMEM = pl.BlockSpec(memory_space=pltpu.VMEM)
SMEM = pl.BlockSpec(memory_space=pltpu.SMEM)
ANY = pl.BlockSpec(memory_space=pl.ANY)
VMEM_BYTES = 60 * 2**20


UNITS = 256


def nt(left_op, right_op):
    return lax.dot_general(
        left_op, right_op, (((1,), (1,)), ((), ())), preferred_element_type=F32
    )


def greet(axes):
    barrier = pltpu.get_barrier_semaphore()
    total = 0
    for axis in axes:
        n, me = lax.axis_size(axis), lax.axis_index(axis)
        for k in range(1, n):
            pl.semaphore_signal(
                barrier, inc=1, device_id={axis: lax.rem(me + k, n)}, device_id_type=MESH
            )
        total += n - 1
    pl.semaphore_wait(barrier, total)


def remote(src, dst, sems, slot, axis, peer):
    return pltpu.make_async_remote_copy(
        src_ref=src,
        dst_ref=dst,
        send_sem=sems.at[0, slot],
        recv_sem=sems.at[1, slot],
        device_id={axis: peer},
        device_id_type=MESH,
    )


def send(src, dst, sems, slot, axis, peer):
    copy = remote(src, dst, sems, slot, axis, peer)
    copy.start()
    return copy


def scatter_start(part, recv, sems, axis):
    n, me = lax.axis_size(axis), lax.axis_index(axis)
    rows = recv.shape[1]
    copies = []
    for k in range(1, n):
        peer = lax.rem(me + k, n)
        copies.append(
            send(part.at[pl.ds(peer * rows, rows)], recv.at[k - 1], sems, k - 1, axis, peer)
        )
    return copies


def gather_start(whole, rows, sems, axis):
    n, me = lax.axis_size(axis), lax.axis_index(axis)
    mine = whole.at[pl.ds(me * rows, rows)]
    return [send(mine, mine, sems, k - 1, axis, lax.rem(me + k, n)) for k in range(1, n)]


def arrived(copies):
    for copy in copies:
        copy.wait_recv()


def left(copies):
    for copy in copies:
        copy.wait_send()


def pair_sems(n):
    return pltpu.SemaphoreType.DMA((2, n - 1))


def summed(part, recv, at, step, row0):
    total = part[pl.ds(row0 + at, step)].astype(F32)
    for k in range(recv.shape[0]):
        total = total + recv[k, pl.ds(at, step)].astype(F32)
    return total


def step_rows(rows, step, body):
    def run(i, carry):
        body(pl.multiple_of(i * step, step))
        return carry

    lax.fori_loop(0, rows // step, run, 0)


def mates():
    z = lax.axis_index("wt")
    mate = z + 1 - 2 * lax.rem(z, 2)
    return z, mate, lax.rem(z + 2, 4), lax.rem(mate + 2, 4)


def line_scatter_start(part, recv, sems):
    if lax.axis_size("wt") != 4:
        return scatter_start(part, recv, sems, "wt")
    rows = recv.shape[1]
    _, mate, _, far_mate = mates()
    return [
        send(part.at[pl.ds(far_mate * rows, rows)], recv.at[0], sems, 0, "wt", mate),
        send(part.at[pl.ds(mate * rows, rows)], recv.at[1], sems, 1, "wt", mate),
    ]


def line_scatter_mid(part, recv, pend, sems, copies):
    if lax.axis_size("wt") != 4:
        return copies
    rows = recv.shape[1]
    _, _, far, _ = mates()
    copies[0].wait_recv()

    def body(at):
        mine = part[pl.ds(pl.multiple_of(far * rows + at, 16), 16)].astype(F32)
        pend[pl.ds(at, 16)] = (mine + recv[0, pl.ds(at, 16)].astype(F32)).astype(BF16)

    step_rows(rows, 16, body)
    return copies + [send(pend, recv.at[2], sems, 2, "wt", far)]


def line_scatter_end(copies):
    if lax.axis_size("wt") != 4:
        arrived(copies)
    else:
        arrived(copies[1:])


def line_summed(part, recv, at, step, row0):
    if lax.axis_size("wt") != 4:
        return summed(part, recv, at, step, row0)
    total = part[pl.ds(row0 + at, step)].astype(F32)
    return total + recv[1, pl.ds(at, step)].astype(F32) + recv[2, pl.ds(at, step)].astype(F32)


def line_gather_start(whole, rows, sems):
    if lax.axis_size("wt") != 4:
        return gather_start(whole, rows, sems, "wt")
    z, mate, far, _ = mates()
    mine = whole.at[pl.ds(z * rows, rows)]
    return [send(mine, mine, sems, 0, "wt", far), send(mine, mine, sems, 1, "wt", mate)]


def line_gather_mid(whole, rows, sems, copies):
    if lax.axis_size("wt") != 4:
        return copies
    _, mate, far, _ = mates()
    copies[0].wait_recv()
    piece = whole.at[pl.ds(far * rows, rows)]
    return copies + [send(piece, piece, sems, 2, "wt", mate)]


def line_gather_end(copies):
    if lax.axis_size("wt") != 4:
        arrived(copies)
    else:
        arrived(copies[1:])


def flips():
    seq = lax.axis_index("seq")
    core, x, y = lax.rem(seq, 2), lax.rem(seq // 2, 2), seq // 4

    def at(fy, fx, fc):
        return (
            (1 - y if fy else y) * 4 + (1 - x if fx else x) * 2 + (1 - core if fc else core)
        )

    return at


def cube_sems():
    return pltpu.SemaphoreType.DMA((2, 9))


def cube_first(block, whole, sems):
    at = flips()
    mine = whole.at[at(0, 0, 0)]
    return [
        send(block, mine, sems, 0, "seq", at(0, 1, 0)),
        send(block, mine, sems, 1, "seq", at(1, 0, 0)),
        send(block, mine, sems, 2, "seq", at(0, 0, 1)),
    ]


def keep(block, whole, sem):
    copy = pltpu.make_async_copy(block, whole.at[lax.axis_index("seq")], sem)
    copy.start()
    return copy


def spread_plan(src, dst, sems, own_sem):
    seq, n_seq = lax.axis_index("seq"), lax.axis_size("seq")
    piece = dst.shape[2]

    def columns(peer):
        return src.at[:, pl.ds(pl.multiple_of(peer * piece, piece), piece)]

    out = []
    for k in range(1, n_seq):
        peer = lax.rem(seq + k, n_seq)
        out.append(remote(columns(peer), dst.at[seq], sems, k - 1, "seq", peer))
    return out, pltpu.make_async_copy(columns(seq), dst.at[seq], own_sem)


def spread(src, dst, sems, own_sem):
    out, own = spread_plan(src, dst, sems, own_sem)
    for copy in out + [own]:
        copy.start()
    return out, own


def cube_second(whole, sems, first):
    at = flips()
    half = whole.shape[1] // 2
    first[0].wait_recv()
    block = whole.at[at(0, 1, 0)]
    top = block.at[pl.ds(0, half)]
    sent = [
        send(top, top, sems, 3, "seq", at(1, 0, 0)),
        send(block, block, sems, 5, "seq", at(0, 0, 1)),
    ]
    first[1].wait_recv()
    block = whole.at[at(1, 0, 0)]
    low = block.at[pl.ds(half, half)]
    sent += [
        send(low, low, sems, 4, "seq", at(0, 1, 0)),
        send(block, block, sems, 6, "seq", at(0, 0, 1)),
    ]
    return sent


def cube_third(whole, sems, second):
    at = flips()
    half = whole.shape[1] // 2
    block = whole.at[at(1, 1, 0)]
    sent = []
    for slot, came in ((0, second[0]), (1, second[2])):
        came.wait_recv()
        piece = block.at[pl.ds(slot * half, half)]
        sent.append(send(piece, piece, sems, 7 + slot, "seq", at(0, 0, 1)))
    return sent


def cube_end(first, second, third):
    first[2].wait_recv()
    second[1].wait_recv()
    second[3].wait_recv()
    arrived(third)
    for group in (first, second, third):
        left(group)


def share(src, dst, sems, own_sem):
    seq, n_seq, z = lax.axis_index("seq"), lax.axis_size("seq"), lax.axis_index("wt")
    own, piece = dst.shape[2:]
    rows = src.at[pl.ds(pl.multiple_of(z * own, own), own)]

    def columns(peer):
        return rows.at[:, pl.ds(pl.multiple_of(peer * piece, piece), piece)]

    sent = []
    for k in range(1, n_seq):
        peer = lax.rem(seq + k, n_seq)
        sent.append(send(columns(peer), dst.at[seq, z], sems, k - 1, "seq", peer))
    kept = pltpu.make_async_copy(columns(seq), dst.at[seq, z], own_sem)
    kept.start()
    return sent, kept


def pass_along(dst, sems):
    z, n_wt = lax.axis_index("wt"), lax.axis_size("wt")
    lines = dst.at[:, z]
    return [send(lines, lines, sems, k - 1, "wt", lax.rem(z + k, n_wt)) for k in range(1, n_wt)]


def first_kernel(
    pair, small, cot, tok, gain, taps, bias, goes,
    w_first, cot_f, act_f, w_small, inner, prev, switch, conv, mixed, select,
    first_in, w_near, ext, before, halo, part, recv,
    s_pair, s_small, s_own, s_cot, s_act, s_cz, s_az, s_halo, s_scatter, s_gather,
):
    seq, n_seq = lax.axis_index("seq"), lax.axis_size("seq")
    me = lax.axis_index("wt")
    count, width = tok.shape
    chan = inner.shape[1]
    kept = [keep(pair, w_near, s_own.at[0]), keep(small, w_small, s_own.at[1])]

    def norm(at):
        v = tok[pl.ds(at, 16)].astype(F32)
        inverse = lax.rsqrt(jnp.mean(v * v, axis=-1, keepdims=True) + EPS)
        first_in[pl.ds(at, 16)] = (v * inverse * gain[...]).astype(BF16)

    step_rows(count, 16, norm)
    greet(("seq", "wt"))
    little = cube_first(small, w_small, s_small)
    sent1, kept1 = share(cot, cot_f, s_cot, s_own.at[2])
    sent2, kept2 = share(first_in, act_f, s_act, s_own.at[3])
    pair1 = cube_first(pair, w_near, s_pair)
    sent = sent1 + sent2
    arrived(sent)
    kept1.wait()
    kept2.wait()
    along = pass_along(cot_f, s_cz) + pass_along(act_f, s_az)
    little2 = cube_second(w_small, s_small, little)
    little3 = cube_third(w_small, s_small, little2)
    pair2 = cube_second(w_near, s_pair, pair1)
    pair3 = cube_third(w_near, s_pair, pair2)
    cube_end(little, little2, little3)
    cube_end(pair1, pair2, pair3)
    for copy in kept:
        copy.wait()
    far = pltpu.make_async_copy(w_near, w_first, s_own.at[0])
    far.start()

    def project(target, first_tile):
        def one(j, carry):
            columns = pl.ds(pl.multiple_of(j * UNITS, UNITS), UNITS)
            source = pl.ds(pl.multiple_of((first_tile + j) * UNITS, UNITS), UNITS)
            tile = w_near[:, :, source].reshape(width, UNITS)
            out = jnp.dot(first_in[...], tile, preferred_element_type=F32)
            target[:, columns] = out.astype(target.dtype)
            return carry

        lax.fori_loop(0, chan // UNITS, one, 0)

    project(inner, 0)
    last_row, row_before = goes[count - 1 :], goes[count - 2 : count - 1]
    cut = jnp.concatenate(
        [jnp.ones((13, 1), F32), (last_row * row_before)[:, :1], last_row[:, :1], jnp.ones((1, 1), F32)]
    )
    halo[0] = (inner[count - 16 :].astype(F32) * cut).astype(BF16)
    before[:16] = jnp.ones((16, 128), F32)
    before[16:] = goes[...]
    ahead = remote(halo.at[0], halo.at[1], s_halo, 0, "seq", lax.rem(seq + 1, n_seq))

    @pl.when(seq + 1 < n_seq)
    def _():
        ahead.start()

    @pl.when(seq == 0)
    def _():
        halo[1] = jnp.zeros_like(halo[1])

    project(switch, chan // UNITS)
    ext[16:] = inner[...].astype(F32)

    @pl.when(seq > 0)
    def _():
        ahead.wait_recv()

    ext[:16] = halo[1].astype(F32)
    prev[...] = ext[8:16]

    def convolve(at):
        v = ext[pl.ds(pl.multiple_of(at + 8, 8), 24)]
        g = before[pl.ds(pl.multiple_of(at + 8, 8), 24)]
        same = None
        out = bias[...] + taps[0:1] * v[8:]
        for k in range(1, KC):
            step = g[9 - k : 25 - k]
            same = step if same is None else same * step
            out = out + taps[k : k + 1] * v[8 - k : 24 - k] * same[:, :1]
        conv[pl.ds(at, 16)] = out
        mixed[pl.ds(at, 16)] = (out * jax.nn.sigmoid(out)).astype(BF16)

    step_rows(count, 16, convolve)
    deep = w_small.shape[1]
    all_rows = nt(w_small[...].reshape(n_seq * deep, chan), mixed[...])
    rows = part.shape[0] // n_seq
    for j in range(n_seq):
        part[j * rows : (j + 1) * rows] = all_rows[j * deep + 16 : j * deep + 16 + rows]
    first = scatter_start(part, recv, s_scatter, "wt")
    rows = recv.shape[1]
    arrived(first)
    select[pl.ds(me * rows, rows)] = summed(part, recv, 0, rows, me * rows)
    second = gather_start(select, rows, s_gather, "wt")
    arrived(second)
    arrived(along)
    far.wait()

    @pl.when(seq + 1 < n_seq)
    def _():
        ahead.wait_send()

    for group in (along, sent, first, second):
        left(group)


def first_gather(pair, small, cot, tok, gain, taps, bias, goes, rows_sel, n_wt, n_seq, ident):
    count, width = cot.shape
    chan = pair.shape[1] // 2
    lines = rows_sel * n_seq
    share_shape = jax.ShapeDtypeStruct((n_seq, n_wt, count // n_wt, width // n_seq), BF16)
    return pl.pallas_call(
        first_kernel,
        out_shape=[
            jax.ShapeDtypeStruct((n_seq,) + pair.shape, BF16),
            share_shape,
            share_shape,
            jax.ShapeDtypeStruct((n_seq,) + small.shape, BF16),
            jax.ShapeDtypeStruct((count, chan), BF16),
            jax.ShapeDtypeStruct((8, chan), F32),
            jax.ShapeDtypeStruct((count, chan), F32),
            jax.ShapeDtypeStruct((count, chan), F32),
            jax.ShapeDtypeStruct((count, chan), BF16),
            jax.ShapeDtypeStruct((lines, count), F32),
        ],
        in_specs=[ANY] * 2 + [VMEM] * 6,
        out_specs=[ANY] * 3 + [VMEM] * 7,
        scratch_shapes=[
            pltpu.VMEM((count, width), BF16),
            pltpu.VMEM((n_seq,) + pair.shape, BF16),
            pltpu.VMEM((16 + count, chan), F32),
            pltpu.VMEM((16 + count, 128), F32),
            pltpu.VMEM((2, 16, chan), BF16),
            pltpu.VMEM((lines, count), F32),
            pltpu.VMEM((n_wt - 1, lines // n_wt, count), F32),
            cube_sems(),
            cube_sems(),
            pltpu.SemaphoreType.DMA((4,)),
            pair_sems(n_seq),
            pair_sems(n_seq),
            pair_sems(n_wt),
            pair_sems(n_wt),
            pltpu.SemaphoreType.DMA((2, 1)),
            pair_sems(n_wt),
            pair_sems(n_wt),
        ],
        compiler_params=pltpu.CompilerParams(
            collective_id=ident, has_side_effects=True, vmem_limit_bytes=VMEM_BYTES
        ),
        cost_estimate=pl.CostEstimate(flops=10**9, bytes_accessed=10**8, transcendentals=0),
    )(pair, small, cot, tok, gain[None], taps, bias[None], goes)


def ffn_kernel(cube, x, c, wg, wu, wd, gated, acts, down, d_second, *refs):
    pieces, refs = refs[:cube], refs[cube:]
    acc_down, acc_second = refs[:2]
    step = pl.program_id(0)
    if cube:
        held, s_spread, s_own = refs[2:]
        sent, kept = spread_plan(held, pieces[0], s_spread, s_own)

        @pl.when(step == 0)
        def _():
            held[...] = x[...]
            greet(("seq",))
            for copy in sent + [kept]:
                copy.start()

    @pl.when(step == 0)
    def _():
        acc_down[...] = jnp.zeros_like(acc_down)
        acc_second[...] = jnp.zeros_like(acc_second)

    gate = jnp.dot(x[...], wg[...], preferred_element_type=F32)
    up = jnp.dot(x[...], wu[...], preferred_element_type=F32)
    d_hidden = jnp.dot(c[...], wd[...], preferred_element_type=F32)
    sigma = jax.nn.sigmoid(gate)
    act = gate * sigma
    hidden = (act * up).astype(BF16)
    d_gate = (d_hidden * up * (sigma * (1.0 + gate * (1.0 - sigma)))).astype(BF16)
    d_up = (d_hidden * act).astype(BF16)
    acts[:, :UNITS] = hidden
    acts[:, UNITS : 2 * UNITS] = d_gate
    acts[:, 2 * UNITS : 3 * UNITS] = d_up
    acts[:, 3 * UNITS :] = gated[...]
    acc_down[...] += nt(hidden, wd[...])
    acc_second[...] += nt(d_gate, wg[...]) + nt(d_up, wu[...])

    @pl.when(step == pl.num_programs(0) - 1)
    def _():
        down[...] = acc_down[...].astype(BF16)
        d_second[...] = acc_second[...].astype(BF16)
        if cube:
            kept.wait()
            arrived(sent)
            left(sent)


def ffn(x, c, w_all, gated, cube, n_seq, ident):
    tok, width = x.shape
    units, chan = w_all.shape[1] // 3, gated.shape[1]
    steps = units // UNITS
    span = 3 * UNITS + chan // steps
    whole = pl.BlockSpec((tok, width), lambda i: (0, 0))
    tile = lambda part: pl.BlockSpec((width, UNITS), lambda i: (0, part * steps + i))
    return pl.pallas_call(
        functools.partial(ffn_kernel, int(cube)),
        grid=(steps,),
        in_specs=[whole, whole, tile(0), tile(1), tile(2)]
        + [pl.BlockSpec((tok, chan // steps), lambda i: (0, i))],
        out_specs=[pl.BlockSpec((tok, span), lambda i: (0, i)), whole, whole] + [ANY] * cube,
        out_shape=[
            jax.ShapeDtypeStruct((tok, 3 * units + chan), BF16),
            jax.ShapeDtypeStruct((tok, width), BF16),
            jax.ShapeDtypeStruct((tok, width), BF16),
        ]
        + [jax.ShapeDtypeStruct((n_seq, tok, width // n_seq), BF16)] * cube,
        scratch_shapes=[pltpu.VMEM((tok, width), F32)] * 2
        + ([pltpu.VMEM((tok, width), BF16), pair_sems(n_seq), pltpu.SemaphoreType.DMA] if cube else []),
        compiler_params=pltpu.CompilerParams(
            vmem_limit_bytes=VMEM_BYTES,
            **(dict(collective_id=ident, has_side_effects=True) if cube else {}),
        ),
        cost_estimate=pl.CostEstimate(
            flops=12 * tok * width * units, bytes_accessed=6 * width * units, transcendentals=0
        ),
    )(x, c, w_all, w_all, w_all, gated)


def grads_kernel(lefts, *refs):
    n, m = max(lefts) + 1, len(lefts)
    for which, act, out in zip(lefts, refs[n : n + m], refs[n + m :]):
        out[...] = jnp.dot(refs[which][...], act[...], preferred_element_type=F32)


def grads(left_ops, lefts, acts):
    rows, tok = left_ops[0].shape
    cols = acts[0].shape[1]
    n = len(acts)
    return pl.pallas_call(
        functools.partial(grads_kernel, lefts),
        grid=(cols // UNITS,),
        in_specs=[pl.BlockSpec((rows, tok), lambda i: (0, 0))] * len(left_ops)
        + [pl.BlockSpec((tok, UNITS), lambda i: (0, i))] * n,
        out_specs=[pl.BlockSpec((rows, UNITS), lambda i: (0, i))] * n,
        out_shape=[jax.ShapeDtypeStruct((rows, cols), F32)] * n,
        compiler_params=pltpu.CompilerParams(vmem_limit_bytes=VMEM_BYTES),
        cost_estimate=pl.CostEstimate(
            flops=2 * n * tok * rows * cols, bytes_accessed=2 * n * tok * cols, transcendentals=0
        ),
    )(*left_ops, *acts)


def wt_sum_kernel(part, out, recv, s_scatter, s_gather):
    me = lax.axis_index("wt")
    rows = recv.shape[1]
    greet(("wt",))
    first = scatter_start(part, recv, s_scatter, "wt")
    arrived(first)
    out[pl.ds(me * rows, rows)] = summed(part, recv, 0, rows, me * rows)
    second = gather_start(out, rows, s_gather, "wt")
    arrived(second)
    left(first)
    left(second)


def wt_sum(part, n_wt, ident):
    rows, cols = part.shape
    return pl.pallas_call(
        wt_sum_kernel,
        out_shape=jax.ShapeDtypeStruct((rows, cols), F32),
        in_specs=[VMEM],
        out_specs=VMEM,
        scratch_shapes=[
            pltpu.VMEM((n_wt - 1, rows // n_wt, cols), F32),
            pair_sems(n_wt),
            pair_sems(n_wt),
        ],
        compiler_params=pltpu.CompilerParams(
            collective_id=ident, has_side_effects=True, vmem_limit_bytes=VMEM_BYTES
        ),
        cost_estimate=pl.CostEstimate(flops=10**5, bytes_accessed=10**6, transcendentals=0),
    )(part)


def second_norm_kernel(part, tok, gain, out, res, recv, pend, s_scatter, s_gather):
    me = lax.axis_index("wt")
    rows = recv.shape[1]
    greet(("wt",))
    first = line_scatter_start(part, recv, s_scatter)
    first = line_scatter_mid(part, recv, pend, s_scatter, first)
    line_scatter_end(first)
    row0 = me * rows

    def body(at):
        own = tok[pl.ds(pl.multiple_of(row0 + at, 16), 16)].astype(F32)
        r = own + line_summed(part, recv, at, 16, row0)
        res[pl.ds(at, 16)] = r
        inverse = lax.rsqrt(jnp.mean(r * r, axis=-1, keepdims=True) + EPS)
        out[pl.ds(pl.multiple_of(row0 + at, 16), 16)] = (r * inverse * gain[...]).astype(BF16)

    step_rows(rows, 16, body)
    second = line_gather_start(out, rows, s_gather)
    second = line_gather_mid(out, rows, s_gather, second)
    line_gather_end(second)
    left(first)
    left(second)


def second_norm(part, tok_own, gain, n_wt, ident):
    rows, cols = part.shape
    own = rows // n_wt
    return pl.pallas_call(
        second_norm_kernel,
        out_shape=[
            jax.ShapeDtypeStruct((rows, cols), BF16),
            jax.ShapeDtypeStruct((own, cols), F32),
        ],
        in_specs=[VMEM] * 3,
        out_specs=[VMEM] * 2,
        scratch_shapes=[
            pltpu.VMEM((n_wt - 1, own, cols), BF16),
            pltpu.VMEM((own, cols), BF16),
            pair_sems(n_wt),
            pair_sems(n_wt),
        ],
        compiler_params=pltpu.CompilerParams(
            collective_id=ident, has_side_effects=True, vmem_limit_bytes=VMEM_BYTES
        ),
        cost_estimate=pl.CostEstimate(flops=10**6, bytes_accessed=10**8, transcendentals=0),
    )(part, tok_own, gain[None])


def norm_back_rows(grad, vals, gain):
    inverse = lax.rsqrt(jnp.mean(vals * vals, axis=-1, keepdims=True) + EPS)
    normed = vals * inverse
    scaled = grad * gain
    mean = jnp.mean(scaled * normed, axis=-1, keepdims=True)
    return inverse * (scaled - normed * mean), grad * normed


def second_back_kernel(n_spread, part, res, cot, gain, *refs):
    srcs, refs = refs[:n_spread], refs[n_spread:]
    out, d_res, gain_grad = refs[:3]
    dsts, refs = refs[3 : 3 + n_spread], refs[3 + n_spread :]
    recv, pend, s_scatter, s_gather = refs[:4]
    me = lax.axis_index("wt")
    rows = recv.shape[1]
    greet(("wt", "seq") if n_spread else ("wt",))
    first = line_scatter_start(part, recv, s_scatter)
    spreads = [
        spread(srcs[i], dsts[i], refs[4 + 2 * i], refs[5 + 2 * i]) for i in range(n_spread)
    ]
    gain_grad[...] = jnp.zeros_like(gain_grad)
    first = line_scatter_mid(part, recv, pend, s_scatter, first)
    line_scatter_end(first)
    row0 = me * rows

    def body(at):
        grad = line_summed(part, recv, at, 16, row0)
        back, prod = norm_back_rows(grad, res[pl.ds(at, 16)], gain[...])
        gain_grad[...] += prod[:8] + prod[8:]
        d = cot[pl.ds(pl.multiple_of(row0 + at, 16), 16)].astype(F32) + back
        d_res[pl.ds(at, 16)] = d
        out[pl.ds(pl.multiple_of(row0 + at, 16), 16)] = d.astype(BF16)

    step_rows(rows, 16, body)
    second = line_gather_start(out, rows, s_gather)
    second = line_gather_mid(out, rows, s_gather, second)
    line_gather_end(second)
    for sent, kept in spreads:
        kept.wait()
        arrived(sent)
        left(sent)
    left(first)
    left(second)


def second_back(part, res, cot_own, gain, srcs, n_wt, n_seq, ident):
    rows, cols = part.shape
    own = rows // n_wt
    return pl.pallas_call(
        functools.partial(second_back_kernel, len(srcs)),
        out_shape=[
            jax.ShapeDtypeStruct((rows, cols), BF16),
            jax.ShapeDtypeStruct((own, cols), F32),
            jax.ShapeDtypeStruct((8, cols), F32),
        ]
        + [jax.ShapeDtypeStruct((n_seq, rows, cols // n_seq), BF16)] * len(srcs),
        in_specs=[VMEM] * (4 + len(srcs)),
        out_specs=[VMEM] * 3 + [ANY] * len(srcs),
        scratch_shapes=[
            pltpu.VMEM((n_wt - 1, own, cols), BF16),
            pltpu.VMEM((own, cols), BF16),
            pair_sems(n_wt),
            pair_sems(n_wt),
        ]
        + [pair_sems(n_seq), pltpu.SemaphoreType.DMA] * len(srcs),
        compiler_params=pltpu.CompilerParams(
            collective_id=ident, has_side_effects=True, vmem_limit_bytes=VMEM_BYTES
        ),
        cost_estimate=pl.CostEstimate(flops=10**6, bytes_accessed=10**8, transcendentals=0),
    )(part, res, cot_own, gain[None], *srcs)


def last_kernel(cube, part, tok, d_res, gain, gain_grad2, sel, stp, taps, decays, bias3, line, *refs):
    blocks, refs = refs[:cube], refs[cube:]
    if cube:
        cot_t, second_t, branch_t, first_t, acts = refs[:5]
        refs = refs[5:]
    out, block_out, sel_out, stp_out, taps_out, decays_out, *bias_outs = refs[:9]
    gain_outs, refs = refs[9:11], refs[11:]
    if cube:
        grad_outs, late_outs, refs = refs[:4], refs[4 : 4 + cube], refs[4 + cube :]
        tile, s_tile, wholes, refs = refs[0], refs[1], refs[2 : 2 + cube], refs[2 + cube :]
        width = tile.shape[2]
        tiles = acts.shape[1] // width

        def fetch(j, slot):
            columns = acts.at[:, pl.ds(pl.multiple_of(j * width, width), width)]
            return pltpu.make_async_copy(columns, tile.at[slot], s_tile.at[slot])

        def one_tile(j, carry):
            slot = lax.rem(j, 2)

            @pl.when(j + 1 < tiles)
            def _():
                fetch(j + 1, 1 - slot).start()

            fetch(j, slot).wait()
            at = 0
            for left_op, out_ref in zip((cot_t, second_t, second_t, branch_t), grad_outs):
                wide = out_ref.shape[1] // tiles
                out_ref[:, pl.ds(pl.multiple_of(j * wide, wide), wide)] = jnp.dot(
                    left_op[...], tile[slot, :, at : at + wide], preferred_element_type=F32
                )
                at += wide
            return carry

        fetch(0, 0).start()
    recv, pend, recv_sel, recv_stp, recv_chan, pack, chan_out, gain_buf, recv_gz, recv_gs = refs[:10]
    s_scatter, s_gather, s_sel, s_stp, s_chan, s_cg, s_gz, s_gs, s_block = refs[10:19]
    refs = refs[19:]
    me, n_wt = lax.axis_index("wt"), lax.axis_size("wt")
    seq, n_seq = lax.axis_index("seq"), lax.axis_size("seq")
    rows = recv.shape[1]
    block_out[pl.ds(pl.multiple_of(me * rows, 16), rows)] = line[...]
    greet(("wt", "seq"))
    first = line_scatter_start(part, recv, s_scatter)
    share = -(-(KC + NS + 3) // n_seq)
    lines = [(taps, i) for i in range(KC)] + [(decays, i) for i in range(NS)]
    lines += [(bias3, i) for i in range(3)]
    for at, (ref, i) in enumerate(lines):
        pack[at // share, at % share : at % share + 1] = ref[i : i + 1]
    smalls = []
    for src, dst, sems in ((sel, recv_sel, s_sel), (stp, recv_stp, s_stp), (pack, recv_chan, s_chan)):
        for k in range(1, n_seq):
            peer = lax.rem(seq + k, n_seq)
            smalls.append(send(src.at[peer], dst.at[k - 1], sems, k - 1, "seq", peer))
    cubes = []
    for i in range(cube):
        s_cube, s_own = refs[2 * i : 2 * i + 2]
        cubes.append([cube_first(blocks[i], wholes[i], s_cube), s_cube, wholes[i]])
        cubes[-1].append(keep(blocks[i], wholes[i], s_own))
    if cube:
        lax.fori_loop(0, 3, one_tile, 0)
    first = line_scatter_mid(part, recv, pend, s_scatter, first)
    if cube:
        lax.fori_loop(3, tiles - 2, one_tile, 0)
    arrived(smalls)
    for src, recv_one, one_out in ((sel, recv_sel, sel_out), (stp, recv_stp, stp_out)):
        total = src[seq].astype(F32)
        for k in range(n_seq - 1):
            total = total + recv_one[k].astype(F32)
        one_out[...] = total[: one_out.shape[0]]
    total = pack[seq]
    for k in range(n_seq - 1):
        total = total + recv_chan[k]
    chan_out[seq] = total
    mine = chan_out.at[seq]
    chans = [
        send(mine, mine, s_cg, k - 1, "seq", lax.rem(seq + k, n_seq)) for k in range(1, n_seq)
    ]
    line_scatter_end(first)
    row0 = me * rows
    gain_buf[...] = jnp.zeros_like(gain_buf)

    def body(at):
        grad = line_summed(part, recv, at, 16, row0)
        own = tok[pl.ds(pl.multiple_of(row0 + at, 16), 16)].astype(F32)
        back, prod = norm_back_rows(grad, own, gain[...])
        gain_buf[...] += prod[:8] + prod[8:]
        out[pl.ds(pl.multiple_of(row0 + at, 16), 16)] = (d_res[pl.ds(at, 16)] + back).astype(BF16)

    step_rows(rows, 16, body)
    second = line_gather_start(out, rows, s_gather)
    third = line_gather_start(block_out, rows, s_block)
    high = recv_gz.shape[1] // 2
    for i, grad in enumerate((gain_buf, gain_grad2)):
        line = jnp.sum(grad[...], axis=0, keepdims=True)
        for t in range(high):
            recv_gz[me, i * high + t : i * high + t + 1] = line[:, t * 128 : (t + 1) * 128]
    mine_z = recv_gz.at[me]
    zs = [send(mine_z, mine_z, s_gz, k - 1, "wt", lax.rem(me + k, n_wt)) for k in range(1, n_wt)]
    cubes2 = [cube_second(whole, sems, one) for one, sems, whole, _ in cubes]
    if cube:
        lax.fori_loop(tiles - 2, tiles, one_tile, 0)
    second = line_gather_mid(out, rows, s_gather, second)
    third = line_gather_mid(block_out, rows, s_block, third)
    arrived(zs)
    total = recv_gz[0]
    for pos in range(1, n_wt):
        total = total + recv_gz[pos]
    recv_gs[seq] = total
    mine_s = recv_gs.at[seq]
    ss = [
        send(mine_s, mine_s, s_gs, k - 1, "seq", lax.rem(seq + k, n_seq)) for k in range(1, n_seq)
    ]
    cubes3 = [cube_third(whole, sems, two) for (_, sems, whole, _), two in zip(cubes, cubes2)]
    arrived(ss)
    total = recv_gs[0]
    for pos in range(1, n_seq):
        total = total + recv_gs[pos]
    for i, gain_out in enumerate(gain_outs):
        for t in range(high):
            gain_out[:, t * 128 : (t + 1) * 128] = total[i * high + t : i * high + t + 1]
    arrived(chans)
    outs = [(taps_out, i) for i in range(KC)] + [(decays_out, i) for i in range(NS)]
    outs += [(bias_out, 0) for bias_out in bias_outs]
    for at, (ref, i) in enumerate(outs):
        ref[i : i + 1] = chan_out[at // share, at % share : at % share + 1]
    for k, ((one, _, whole, kept), two, three) in enumerate(zip(cubes, cubes2, cubes3)):
        cube_end(one, two, three)
        kept.wait()

        def late_tile(j, carry, whole=whole, late_out=late_outs[k]):
            columns = pl.ds(pl.multiple_of(j * UNITS, UNITS), UNITS)
            act = whole[:, :, columns].reshape(first_t.shape[1], UNITS)
            late_out[:, columns] = jnp.dot(first_t[...], act, preferred_element_type=F32)
            return carry

        lax.fori_loop(0, whole.shape[2] // UNITS, late_tile, 0)
    line_gather_end(second)
    line_gather_end(third)
    for group in (first, second, third, smalls, chans, zs, ss):
        left(group)


def last(
    part, tok_own, d_res, gain, gain_grad2, sel, stp, rows_small, taps, decays, bias3, line,
    blocks, more, n_wt, n_seq, ident,
):
    rows, cols = part.shape
    own = rows // n_wt
    chan = taps.shape[1]
    if more:
        deep, tok_all = more[0].shape
        units = (more[4].shape[1] - chan) // 3
        span = more[4].shape[1] // (units // UNITS)
    return pl.pallas_call(
        functools.partial(last_kernel, len(blocks)),
        out_shape=[
            jax.ShapeDtypeStruct((rows, cols), BF16),
            jax.ShapeDtypeStruct((rows, cols), BF16),
        ]
        + [
            jax.ShapeDtypeStruct((n, chan), F32)
            for n in rows_small + (taps.shape[0], decays.shape[0], 1, 1, 1)
        ]
        + [jax.ShapeDtypeStruct((1, cols), F32)] * 2
        + (
            [jax.ShapeDtypeStruct((deep, w), F32) for w in (units, units, units, chan)]
            + [jax.ShapeDtypeStruct((deep, a.shape[1]), F32) for a in blocks]
            if more
            else []
        ),
        in_specs=[VMEM] * 11 + [ANY] * len(blocks) + ([VMEM] * 4 + [ANY] if more else []),
        out_specs=[VMEM] * (11 + (4 + len(blocks) if more else 0)),
        scratch_shapes=(
            [pltpu.VMEM((2, tok_all, span), BF16), pltpu.SemaphoreType.DMA((2,))]
            + [pltpu.VMEM((n_seq,) + a.shape, BF16) for a in blocks]
            if more
            else []
        )
        + [
            pltpu.VMEM((n_wt - 1, own, cols), BF16),
            pltpu.VMEM((own, cols), BF16),
            pltpu.VMEM((n_seq - 1,) + sel.shape[1:], BF16),
            pltpu.VMEM((n_seq - 1,) + stp.shape[1:], BF16),
            pltpu.VMEM((n_seq - 1, 8, chan), F32),
            pltpu.VMEM((n_seq, 8, chan), F32),
            pltpu.VMEM((n_seq, 8, chan), F32),
            pltpu.VMEM((8, cols), F32),
            pltpu.VMEM((n_wt, 2 * cols // 128, 128), F32),
            pltpu.VMEM((n_seq, 2 * cols // 128, 128), F32),
            pair_sems(n_wt),
            pair_sems(n_wt),
            pair_sems(n_seq),
            pair_sems(n_seq),
            pair_sems(n_seq),
            pair_sems(n_seq),
            pair_sems(n_wt),
            pair_sems(n_seq),
            pair_sems(n_wt),
        ]
        + [cube_sems(), pltpu.SemaphoreType.DMA] * len(blocks),
        compiler_params=pltpu.CompilerParams(
            collective_id=ident, has_side_effects=True, vmem_limit_bytes=VMEM_BYTES
        ),
        cost_estimate=pl.CostEstimate(flops=10**6, bytes_accessed=10**8, transcendentals=0),
    )(part, tok_own, d_res, gain[None], gain_grad2, sel, stp, taps, decays, bias3, line, *blocks, *more)


def hand_out_kernel(n, *refs):
    srcs, dsts, held, sems = refs[:n], refs[n : 2 * n], refs[2 * n : 3 * n], refs[3 * n]
    into = [pltpu.make_async_copy(srcs[i], held[i], sems.at[0, i]) for i in range(n)]
    away = [pltpu.make_async_copy(held[i], dsts[i], sems.at[1, i]) for i in range(n)]
    for copy in into:
        copy.start()
    for first, second in zip(into, away):
        first.wait()
        second.start()
    for copy in away:
        copy.wait()


def hand_out(arrays):
    n = len(arrays)
    size = sum(a.size * a.dtype.itemsize for a in arrays)
    return pl.pallas_call(
        functools.partial(hand_out_kernel, n),
        out_shape=[jax.ShapeDtypeStruct(a.shape, a.dtype) for a in arrays],
        in_specs=[ANY] * n,
        out_specs=[ANY] * n,
        scratch_shapes=[pltpu.VMEM(a.shape, a.dtype) for a in arrays]
        + [pltpu.SemaphoreType.DMA((2, n))],
        compiler_params=pltpu.CompilerParams(vmem_limit_bytes=VMEM_BYTES),
        cost_estimate=pl.CostEstimate(flops=0, bytes_accessed=2 * size, transcendentals=0),
    )(*arrays)


def load(ref):
    return tuple(ref[n] for n in range(NS))


def store(ref, values):
    for n in range(NS):
        ref[n] = values[n]


def fold(mine, box, recv, a2, carried, backward):
    n, me = lax.axis_size("seq"), lax.axis_index("seq")
    carried[...] = jnp.zeros_like(carried)
    for k in range(n - 1, 0, -1):

        @pl.when((me + k < n) if backward else (me >= k))
        def _():
            giver = me + k if backward else me - k
            remote(mine, recv.at[k - 1], box, k - 1, "seq", giver).wait_recv()
            through = recv[k - 1, NS]
            for s in range(NS):
                carried[s] = (
                    jnp.exp2(a2[s] * through) * carried[s] + recv[k - 1, s]
                )


def hand_on(mine, recv, box, backward):
    n, me = lax.axis_size("seq"), lax.axis_index("seq")
    for k in range(1, n):

        @pl.when((me >= k) if backward else (me + k < n))
        def _():
            peer = me - k if backward else me + k
            send(mine, recv.at[k - 1], box, k - 1, "seq", peer)


def handed(mine, recv, box, backward):
    n, me = lax.axis_size("seq"), lax.axis_index("seq")
    for k in range(1, n):

        @pl.when((me >= k) if backward else (me + k < n))
        def _():
            peer = me - k if backward else me + k
            remote(mine, recv.at[k - 1], box, k - 1, "seq", peer).wait_send()


def fwd_kernel(sa, dx, wr, a2, y, h0, mine, recv, box):
    tok = sa.shape[0]
    greet(("seq",))

    def end(t, carry):
        s, d = sa[t], dx[t]
        h, total = carry
        return (
            tuple(jnp.exp2(s * a2[n]) * h[n] + wr[n, t] * d for n in range(NS)),
            total + s,
        )

    zero = jnp.zeros(sa.shape[1:], F32)
    ends, total = lax.fori_loop(0, tok, end, ((zero,) * NS, zero), unroll=4)
    store(mine, ends)
    mine[NS] = total
    hand_on(mine, recv, box, False)
    fold(mine, box, recv, a2, h0, False)

    def body(t, h):
        s, d = sa[t], dx[t]
        new, sums = [], [None] * 4
        for n in range(NS):
            hn = jnp.exp2(s * a2[n]) * h[n] + wr[n, t] * d
            new.append(hn)
            c = wr[NS + n, t] * hn
            sums[n % 4] = c if sums[n % 4] is None else sums[n % 4] + c
        y[t] = (sums[0] + sums[1]) + (sums[2] + sums[3])
        return tuple(new)

    lax.fori_loop(0, tok, body, load(h0), unroll=4)
    handed(mine, recv, box, False)


def fwd_scan(sa, dx, wr, a2, n_seq, ident):
    tok, high = sa.shape[:2]
    return pl.pallas_call(
        fwd_kernel,
        out_shape=[
            jax.ShapeDtypeStruct((tok, high, 128), F32),
            jax.ShapeDtypeStruct((NS, high, 128), F32),
        ],
        in_specs=[VMEM, VMEM, SMEM, VMEM],
        out_specs=[VMEM] * 2,
        scratch_shapes=[
            pltpu.VMEM((NS + 1, high, 128), F32),
            pltpu.VMEM((n_seq - 1, NS + 1, high, 128), F32),
            pair_sems(n_seq),
        ],
        compiler_params=pltpu.CompilerParams(
            collective_id=ident, has_side_effects=True, vmem_limit_bytes=VMEM_BYTES
        ),
        cost_estimate=pl.CostEstimate(
            flops=10**8, bytes_accessed=8 * 10**7, transcendentals=2 * tok * NS * 1024
        ),
    )(sa, dx, wr, a2)


def bwd_kernel(
    cube, sa, dx, wr, do, a2, h0, part, res, *refs
):
    src, refs = refs[:cube], refs[cube:]
    along, ds2, grad_a, sums, out = refs[:5]
    dst, refs = refs[5 : 5 + cube], refs[5 + cube :]
    hs, qw, qr, pw, pr, g0, mine, recv, recv_z, box, s_scatter = refs[:11]
    tok = sa.shape[0]
    chunk = qw.shape[0] // (NS * 8)
    greet(("wt", "seq"))
    first = scatter_start(part, recv_z, s_scatter, "wt")

    def end(i, carry):
        t = tok - 1 - i
        s, d = sa[t], do[t]
        g, total = carry
        return (
            tuple(jnp.exp2(s * a2[n]) * (g[n] + wr[NS + n, t] * d) for n in range(NS)),
            total + s,
        )

    zero = jnp.zeros(sa.shape[1:], F32)
    ends, total = lax.fori_loop(0, tok, end, ((zero,) * NS, zero), unroll=4)
    store(mine, ends)
    mine[NS] = total
    hand_on(mine, recv, box, True)
    if cube:
        s_seq, s_wt, s_own = refs[11:]
        sent, kept = share(src[0], dst[0], s_seq, s_own)

    def again(t, h):
        s, d = sa[t], dx[t]
        new = []
        for n in range(NS):
            hs[t, n] = h[n]
            new.append(jnp.exp2(s * a2[n]) * h[n] + wr[n, t] * d)
        return tuple(new)

    lax.fori_loop(0, tok, again, load(h0), unroll=2)

    fold(mine, box, recv, a2, g0, True)
    if cube:
        arrived(sent)
        kept.wait()
        passed = pass_along(dst[0], s_wt)
    grad_a[...] = jnp.zeros_like(grad_a)

    def one_chunk(j, g):
        base = (tok // chunk - 1 - j) * chunk

        def body(i, g):
            at = chunk - 1 - i
            t = base + at
            s, d, o = sa[t], dx[t], do[t]
            al = d2 = None
            new = []
            for n in range(NS):
                hp = hs[t, n]
                f = jnp.exp2(s * a2[n])
                hn = f * hp + wr[n, t] * d
                gn = wr[NS + n, t] * o + g[n]
                adj = f * gn
                new.append(adj)
                th = adj * hp
                grad_a[n] += th * s
                x = wr[n, t] * gn
                al = x if al is None else al + x
                x = a2[n] * th
                d2 = x if d2 is None else d2 + x
                row = pl.multiple_of((at * NS + n) * 8, 8)
                qw[pl.ds(row, 8), :] = gn * d
                qr[pl.ds(row, 8), :] = hn * o
            along[t] = al
            ds2[t] = d2
            return tuple(new)

        g = lax.fori_loop(0, chunk, body, g)

        def lanes(i, carry):
            for q, p in ((qw, pw), (qr, pr)):
                acc = q[pl.ds(i * NS * 8, NS, stride=8), :]
                for s in range(1, 8):
                    acc = acc + q[pl.ds(i * NS * 8 + s, NS, stride=8), :]
                p[pl.ds(pl.multiple_of(i * NS, NS), NS), :] = acc
            return carry

        lax.fori_loop(0, chunk, lanes, 0, unroll=4)
        ones = jnp.ones((8, 128), BF16)
        for which, p in enumerate((pw, pr)):
            high = p[...].astype(BF16)
            low = (p[...] - high.astype(F32)).astype(BF16)
            row = which * (tok // chunk) + base // chunk
            sums[pl.ds(row, 1), :] = (nt(ones, high) + nt(ones, low))[:1]
        return g

    lax.fori_loop(0, tok // chunk, one_chunk, load(g0))
    handed(mine, recv, box, True)
    arrived(first)
    rows = recv_z.shape[1]
    row0 = lax.axis_index("wt") * rows

    def block_rows(at):
        out[pl.ds(at, 16)] = (res[pl.ds(at, 16)] + summed(part, recv_z, at, 16, row0)).astype(BF16)

    step_rows(rows, 16, block_rows)
    left(first)
    if cube:
        arrived(passed)
        left(sent)
        left(passed)


def bwd_scan(sa, dx, wr, do, a2, h0, part, res, src, n_wt, n_seq, ident):
    tok, high = sa.shape[:2]
    rows, cols = part.shape
    chunk = 32
    return pl.pallas_call(
        functools.partial(bwd_kernel, len(src)),
        out_shape=[
            jax.ShapeDtypeStruct((tok, high, 128), F32),
            jax.ShapeDtypeStruct((tok, high, 128), F32),
            jax.ShapeDtypeStruct((NS, high, 128), F32),
            jax.ShapeDtypeStruct((2 * tok // chunk, chunk * NS), F32),
            jax.ShapeDtypeStruct((rows // n_wt, cols), BF16),
        ]
        + [jax.ShapeDtypeStruct((n_seq, n_wt, rows // n_wt, cols // n_seq), BF16)] * len(src),
        in_specs=[VMEM, VMEM, SMEM] + [VMEM] * (5 + len(src)),
        out_specs=[VMEM] * 5 + [ANY] * len(src),
        scratch_shapes=[
            pltpu.VMEM((tok, NS, high, 128), F32),
            pltpu.VMEM((chunk * NS * 8, 128), F32),
            pltpu.VMEM((chunk * NS * 8, 128), F32),
            pltpu.VMEM((chunk * NS, 128), F32),
            pltpu.VMEM((chunk * NS, 128), F32),
            pltpu.VMEM((NS, high, 128), F32),
            pltpu.VMEM((NS + 1, high, 128), F32),
            pltpu.VMEM((n_seq - 1, NS + 1, high, 128), F32),
            pltpu.VMEM((n_wt - 1, rows // n_wt, cols), BF16),
            pair_sems(n_seq),
            pair_sems(n_wt),
        ]
        + [pair_sems(n_seq), pair_sems(n_wt), pltpu.SemaphoreType.DMA] * len(src),
        compiler_params=pltpu.CompilerParams(
            collective_id=ident, has_side_effects=True, vmem_limit_bytes=VMEM_BYTES
        ),
        cost_estimate=pl.CostEstimate(
            flops=10**8, bytes_accessed=15 * 10**7, transcendentals=3 * tok * NS * 1024
        ),
    )(sa, dx, wr, do, a2, h0, part, res, *src)


def gather(block):
    return lax.all_gather(block, "seq", axis=0, tiled=True)


def from_behind(block, axis, distance):
    devices = range(lax.axis_size(axis))
    route = [(i - distance, i) for i in devices if i - distance in devices]
    return lax.ppermute(block, axis, route)


def contract(left_op, right_op, pattern):
    return jnp.einsum(pattern, left_op, right_op, preferred_element_type=F32)


def silu_slope(values):
    sigma = jax.nn.sigmoid(values)
    return sigma * (1.0 + values * (1.0 - sigma))


def tiles(rows):
    return rows.reshape(rows.shape[0], rows.shape[1] // 128, 128)


def flat(rows):
    return rows.reshape(rows.shape[0], rows.shape[1] * rows.shape[2])


def local(
    tokens,
    cotangent,
    doc_start,
    premix_gain,
    inner_proj,
    switch_proj,
    conv_taps,
    conv_bias,
    select_proj,
    step_proj,
    step_bias,
    decay_log,
    skip_gain,
    mixer_out,
    preffn_gain,
    ffn_gate,
    ffn_up,
    ffn_down,
):
    tok_count, width = tokens.shape
    chan = inner_proj.shape[1]
    units = ffn_gate.shape[1]
    edge = KC - 1
    n_seq, n_wt = lax.axis_size("seq"), lax.axis_size("wt")
    z = lax.axis_index("wt")
    own = tok_count // n_wt
    cube = n_seq == 8 and n_seq * tok_count <= width

    rows_sel, rows_step = select_proj.shape[0], step_proj.shape[0]
    goes_on = (1 - doc_start).astype(F32)
    before = jnp.concatenate([jnp.ones((edge,), F32), goes_on])
    after = jnp.concatenate([goes_on, jnp.ones((edge,), F32)])

    def same_back(lag):
        same = jnp.ones_like(goes_on)
        for j in range(lag):
            same = same * before[edge - j : edge - j + tok_count]
        return same[:, None]

    def same_ahead(lag):
        same = jnp.ones_like(goes_on)
        for j in range(1, lag + 1):
            same = same * after[j : j + tok_count]
        return same[:, None]

    one = jnp.ones((edge - 1,), F32)
    last_two, head = goes_on[-2:], goes_on[:edge]
    tail_keep = jnp.concatenate([last_two, one[:1]]) * jnp.concatenate([last_two[1:], one])
    head_keep = (
        head
        * jnp.concatenate([one[:1], head[:2]])
        * jnp.concatenate([one, head[:1]])
    )
    if cube:
        fill = jnp.zeros((-(rows_sel + rows_step) % 32, chan), BF16)
        (
            w_first, cot_f, first_f, w_small,
            inner_act, prev_rows, switch, conv_out, mixed_in, select,
        ) = first_gather(
            jnp.concatenate([inner_proj, switch_proj], axis=1),
            jnp.concatenate([step_proj, select_proj, fill], axis=0),
            cotangent, tokens, premix_gain, conv_taps, conv_bias,
            jnp.broadcast_to(goes_on[:, None], (tok_count, 128)), rows_sel, n_wt, n_seq, 7,
        )
        w_first = w_first.reshape(width, 2 * chan)
        w_mix = gather(mixer_out)
        prev_rows = prev_rows[8 - edge :]
    else:
        token_vals = tokens.astype(F32)
        first_inv = lax.rsqrt(jnp.mean(token_vals * token_vals, axis=-1, keepdims=True) + EPS)
        first_in = (token_vals * first_inv * premix_gain).astype(BF16)
        w_mixer = gather(jnp.concatenate([inner_proj, switch_proj, mixer_out], axis=1))
        w_first, w_mix = w_mixer[:, : 2 * chan], w_mixer[:, 2 * chan :]
        w_small = lax.all_gather(jnp.concatenate([step_proj, select_proj], axis=0), "seq", axis=0)
    w_all = gather(jnp.concatenate([ffn_gate, ffn_up, ffn_down], axis=1))
    w_step = w_small[:, :rows_step].reshape(-1, chan)
    w_select = w_small[:, rows_step : rows_step + rows_sel].reshape(-1, chan)
    if not cube:
        both = contract(first_in, w_first, "td,dc->tc")
        inner_act = both[:, :chan].astype(BF16)
        switch = both[:, chan:]
        prev_rows = from_behind(inner_act[-edge:] * tail_keep[:, None].astype(BF16), "seq", 1)
        extended = jnp.concatenate([prev_rows, inner_act], axis=0).astype(F32)
        conv_out = jnp.zeros((tok_count, chan), F32) + conv_bias[None, :]
        for offset in range(KC):
            conv_out = (
                conv_out
                + conv_taps[offset][None, :]
                * extended[edge - offset : edge - offset + tok_count]
                * same_back(offset)
            )
        mixed_in = jax.nn.silu(conv_out).astype(BF16)
        select = wt_sum(contract(w_select, mixed_in, "jc,tc->jt"), n_wt, 0)
    mixed_f = mixed_in.astype(F32)
    extended = jnp.concatenate([prev_rows.astype(F32), inner_act.astype(F32)], axis=0)
    low_rank = select[:R].astype(BF16)
    write_read = select[R:]
    step_pre = contract(low_rank, w_step, "rt,rc->tc") + step_bias[None, :]
    step_size = jax.nn.softplus(step_pre)
    decay = -jnp.exp(decay_log)
    decay2 = tiles(decay * LOG2E)
    step_a = tiles(jnp.where(doc_start[:, None] > 0, FAR, step_size))
    drive = tiles(step_size * mixed_f)
    scan_out, carried_in = fwd_scan(step_a, drive, write_read, decay2, n_seq, 1)

    scanned = flat(scan_out) + skip_gain[None, :] * mixed_f
    switch_act = jax.nn.silu(switch)
    gated = (scanned * switch_act).astype(BF16)
    mix_part = contract(gated, w_mix, "tc,dc->td").astype(BF16)
    second_in, residual = second_norm(mix_part, tokens, preffn_gain, n_wt, 2)
    if cube:
        line_up = lambda v: v.reshape(n_seq * tok_count, v.shape[-1])
        second_in, head_keep, extended, cot_t, first_t = lax.optimization_barrier(
            (second_in, head_keep, extended, line_up(cot_f).T, line_up(first_f).T)
        )
    acts, down_part, d_second, *second_all = ffn(
        second_in, cotangent, w_all, gated, cube, n_seq, 8
    )
    d_branch, d_residual, grad_preffn = second_back(
        d_second, residual, cotangent, preffn_gain, (), n_wt, n_seq, 3
    )
    d_gated = contract(d_branch, w_mix, "td,dc->tc")
    d_scanned = d_gated * switch_act
    d_switch = (d_gated * scanned * silu_slope(switch)).astype(BF16)
    grad_skip = jnp.sum(d_scanned * mixed_f, axis=0)
    along, through_sum, grad_decay, d_write_read, block_own, *branch_all = bwd_scan(
        step_a, drive, write_read, tiles(d_scanned), decay2, carried_in,
        down_part, residual, (d_branch,) if cube else (), n_wt, n_seq, 4,
    )
    along = flat(along)
    d_step = along * mixed_f + flat(through_sum) * (1.0 / LOG2E)
    grad_decay_log = flat(grad_decay) * decay
    d_pre = d_step * jax.nn.sigmoid(step_pre)
    grad_step_bias = jnp.sum(d_pre, axis=0)
    d_pre_low = d_pre.astype(BF16)
    pad_rows = lambda v: jnp.pad(
        v.reshape(n_seq, -1, tok_count), ((0, 0), (0, -(v.shape[0] // n_seq) % 16), (0, 0))
    ).reshape(-1, tok_count)
    grad_step = contract(pad_rows(low_rank), d_pre_low, "rt,tc->rc").astype(BF16)
    d_select = wt_sum(
        jnp.concatenate(
            [
                contract(w_step, d_pre_low, "rc,tc->rt"),
                d_write_read.reshape(2, tok_count, NS).swapaxes(1, 2).reshape(2 * NS, tok_count),
            ],
            axis=0,
        ),
        n_wt,
        5,
    )
    d_select = d_select.astype(BF16)
    grad_select = contract(pad_rows(d_select), mixed_in, "jt,tc->jc").astype(BF16)
    d_mixed = (
        along * step_size
        + skip_gain[None, :] * d_scanned
        + contract(d_select, w_select, "jt,jc->tc")
    )
    d_conv = (d_mixed * silu_slope(conv_out)).astype(BF16)
    d_conv_f = d_conv.astype(F32)
    grad_conv_bias = jnp.sum(d_conv_f, axis=0)
    next_rows = from_behind(d_conv[:edge] * head_keep[:, None].astype(BF16), "seq", -1)
    ext_grad = jnp.concatenate([d_conv, next_rows], axis=0).astype(F32)
    d_inner = jnp.zeros_like(d_conv_f)
    taps_rows = []
    for offset in range(KC):
        taps_rows.append(
            jnp.sum(
                d_conv_f
                * extended[edge - offset : edge - offset + tok_count]
                * same_back(offset),
                axis=0,
            )
        )
        d_inner = (
            d_inner
            + conv_taps[offset][None, :]
            * ext_grad[offset : offset + tok_count]
            * same_ahead(offset)
        )
    d_inner_low = d_inner.astype(BF16)
    d_first = contract(
        jnp.concatenate([d_inner_low, d_switch], axis=1), w_first, "tc,dc->td"
    ).astype(BF16)
    more = ()
    if cube:
        more = (cot_t, line_up(second_all[0]).T, line_up(branch_all[0]).T, first_t, gather(acts))
    results = last(
        d_first, tokens, d_residual, premix_gain, grad_preffn,
        grad_select.reshape(n_seq, -1, chan), grad_step.reshape(n_seq, -1, chan), (rows_sel, rows_step),
        jnp.stack(taps_rows, axis=0), grad_decay_log,
        jnp.stack([grad_conv_bias, grad_step_bias, grad_skip]), block_own,
        (d_switch, d_inner_low) if cube else (), more, n_wt, n_seq, 6,
    )
    (
        tokens_grad, block_out, out_select, out_step, g_taps, g_decay, g_conv, g_step, g_skip,
        *others,
    ) = hand_out(results)
    if cube:
        out_down, out_gate, out_up, out_mix, out_switch, out_inner = others[2:]
    else:
        scatter = lambda v: lax.psum_scatter(v, "seq", scatter_dimension=0, tiled=True)
        by_unit = acts.reshape(tok_count, units // UNITS, -1)
        hidden, d_gate, d_up = [
            by_unit[:, :, i * UNITS : (i + 1) * UNITS].reshape(tok_count, units) for i in range(3)
        ]
        out_down = scatter(contract(cotangent, hidden, "td,tf->df"))
        out_gate = scatter(contract(second_in, d_gate, "td,tf->df"))
        out_up = scatter(contract(second_in, d_up, "td,tf->df"))
        out_mix = scatter(contract(d_branch, gated, "td,tc->dc"))
        out_switch = scatter(contract(first_in, d_switch, "td,tc->dc"))
        out_inner = scatter(contract(first_in, d_inner_low, "td,tc->dc"))
    return (
        block_out,
        tokens_grad,
        others[0][0],
        out_inner,
        out_switch,
        g_taps,
        g_conv[0],
        out_select,
        out_step,
        g_step[0],
        g_decay,
        g_skip[0],
        out_mix,
        others[1][0],
        out_gate,
        out_up,
        out_down,
    )


def solution(mesh):
    placed = (
        P("seq", None),
        P("seq", None),
        P("seq"),
        P(),
        P("seq", "wt"),
        P("seq", "wt"),
        P(None, "wt"),
        P("wt"),
        P("seq", "wt"),
        P("seq", "wt"),
        P("wt"),
        P(None, "wt"),
        P("wt"),
        P("seq", "wt"),
        P(),
        P("seq", "wt"),
        P("seq", "wt"),
        P("seq", "wt"),
    )
    return jax.shard_map(
        local,
        mesh=mesh,
        in_specs=placed,
        out_specs=(
            P("seq", None),
            P("seq", None),
            P(),
            P("seq", "wt"),
            P("seq", "wt"),
            P(None, "wt"),
            P("wt"),
            P("seq", "wt"),
            P("seq", "wt"),
            P("wt"),
            P(None, "wt"),
            P("wt"),
            P("seq", "wt"),
            P(),
            P("seq", "wt"),
            P("seq", "wt"),
            P("seq", "wt"),
        ),
        check_vma=False,
    )
```

```python
import functools

import jax
import jax.numpy as jnp
from jax import lax
from jax.experimental import pallas as pl
from jax.experimental.pallas import tpu as pltpu
from jax.sharding import PartitionSpec as P

NS = 16
R = 128
KC = 4
EPS = 1e-05
F32 = jnp.float32
BF16 = jnp.bfloat16
LOG2E = 1.4426950408889634
FAR = 1e30
MESH = pl.DeviceIdType.MESH
VMEM = pl.BlockSpec(memory_space=pltpu.VMEM)
SMEM = pl.BlockSpec(memory_space=pltpu.SMEM)
ANY = pl.BlockSpec(memory_space=pl.ANY)
VMEM_BYTES = 60 * 2**20


UNITS = 256


def nt(left_op, right_op):
    return lax.dot_general(
        left_op, right_op, (((1,), (1,)), ((), ())), preferred_element_type=F32
    )


def greet(axes):
    barrier = pltpu.get_barrier_semaphore()
    total = 0
    for axis in axes:
        n, me = lax.axis_size(axis), lax.axis_index(axis)
        for k in range(1, n):
            pl.semaphore_signal(
                barrier, inc=1, device_id={axis: lax.rem(me + k, n)}, device_id_type=MESH
            )
        total += n - 1
    pl.semaphore_wait(barrier, total)


def remote(src, dst, sems, slot, axis, peer):
    return pltpu.make_async_remote_copy(
        src_ref=src,
        dst_ref=dst,
        send_sem=sems.at[0, slot],
        recv_sem=sems.at[1, slot],
        device_id={axis: peer},
        device_id_type=MESH,
    )


def send(src, dst, sems, slot, axis, peer):
    copy = remote(src, dst, sems, slot, axis, peer)
    copy.start()
    return copy


def scatter_start(part, recv, sems, axis):
    n, me = lax.axis_size(axis), lax.axis_index(axis)
    rows = recv.shape[1]
    copies = []
    for k in range(1, n):
        peer = lax.rem(me + k, n)
        copies.append(
            send(part.at[pl.ds(peer * rows, rows)], recv.at[k - 1], sems, k - 1, axis, peer)
        )
    return copies


def gather_start(whole, rows, sems, axis):
    n, me = lax.axis_size(axis), lax.axis_index(axis)
    mine = whole.at[pl.ds(me * rows, rows)]
    return [send(mine, mine, sems, k - 1, axis, lax.rem(me + k, n)) for k in range(1, n)]


def arrived(copies):
    for copy in copies:
        copy.wait_recv()


def left(copies):
    for copy in copies:
        copy.wait_send()


def pair_sems(n):
    return pltpu.SemaphoreType.DMA((2, n - 1))


def summed(part, recv, at, step, row0):
    total = part[pl.ds(row0 + at, step)].astype(F32)
    for k in range(recv.shape[0]):
        total = total + recv[k, pl.ds(at, step)].astype(F32)
    return total


def step_rows(rows, step, body):
    def run(i, carry):
        body(pl.multiple_of(i * step, step))
        return carry

    lax.fori_loop(0, rows // step, run, 0)


def mates():
    z = lax.axis_index("wt")
    mate = z + 1 - 2 * lax.rem(z, 2)
    return z, mate, lax.rem(z + 2, 4), lax.rem(mate + 2, 4)


def line_scatter_start(part, recv, sems):
    if lax.axis_size("wt") != 4:
        return scatter_start(part, recv, sems, "wt")
    rows = recv.shape[1]
    _, mate, _, far_mate = mates()
    return [
        send(part.at[pl.ds(far_mate * rows, rows)], recv.at[0], sems, 0, "wt", mate),
        send(part.at[pl.ds(mate * rows, rows)], recv.at[1], sems, 1, "wt", mate),
    ]


def line_scatter_mid(part, recv, pend, sems, copies):
    if lax.axis_size("wt") != 4:
        return copies
    rows = recv.shape[1]
    _, _, far, _ = mates()
    copies[0].wait_recv()

    def body(at):
        mine = part[pl.ds(pl.multiple_of(far * rows + at, 16), 16)].astype(F32)
        pend[pl.ds(at, 16)] = (mine + recv[0, pl.ds(at, 16)].astype(F32)).astype(BF16)

    step_rows(rows, 16, body)
    return copies + [send(pend, recv.at[2], sems, 2, "wt", far)]


def line_scatter_end(copies):
    if lax.axis_size("wt") != 4:
        arrived(copies)
    else:
        arrived(copies[1:])


def line_summed(part, recv, at, step, row0):
    if lax.axis_size("wt") != 4:
        return summed(part, recv, at, step, row0)
    total = part[pl.ds(row0 + at, step)].astype(F32)
    return total + recv[1, pl.ds(at, step)].astype(F32) + recv[2, pl.ds(at, step)].astype(F32)


def line_gather_start(whole, rows, sems):
    if lax.axis_size("wt") != 4:
        return gather_start(whole, rows, sems, "wt")
    z, mate, far, _ = mates()
    mine = whole.at[pl.ds(z * rows, rows)]
    return [send(mine, mine, sems, 0, "wt", far), send(mine, mine, sems, 1, "wt", mate)]


def line_gather_mid(whole, rows, sems, copies):
    if lax.axis_size("wt") != 4:
        return copies
    _, mate, far, _ = mates()
    copies[0].wait_recv()
    piece = whole.at[pl.ds(far * rows, rows)]
    return copies + [send(piece, piece, sems, 2, "wt", mate)]


def line_gather_end(copies):
    if lax.axis_size("wt") != 4:
        arrived(copies)
    else:
        arrived(copies[1:])


def flips():
    seq = lax.axis_index("seq")
    core, x, y = lax.rem(seq, 2), lax.rem(seq // 2, 2), seq // 4

    def at(fy, fx, fc):
        return (
            (1 - y if fy else y) * 4 + (1 - x if fx else x) * 2 + (1 - core if fc else core)
        )

    return at


def cube_sems():
    return pltpu.SemaphoreType.DMA((2, 9))


def cube_first(block, whole, sems):
    at = flips()
    mine = whole.at[at(0, 0, 0)]
    return [
        send(block, mine, sems, 0, "seq", at(0, 1, 0)),
        send(block, mine, sems, 1, "seq", at(1, 0, 0)),
        send(block, mine, sems, 2, "seq", at(0, 0, 1)),
    ]


def keep(block, whole, sem):
    copy = pltpu.make_async_copy(block, whole.at[lax.axis_index("seq")], sem)
    copy.start()
    return copy


def spread_plan(src, dst, sems, own_sem):
    seq, n_seq = lax.axis_index("seq"), lax.axis_size("seq")
    piece = dst.shape[2]

    def columns(peer):
        return src.at[:, pl.ds(pl.multiple_of(peer * piece, piece), piece)]

    out = []
    for k in range(1, n_seq):
        peer = lax.rem(seq + k, n_seq)
        out.append(remote(columns(peer), dst.at[seq], sems, k - 1, "seq", peer))
    return out, pltpu.make_async_copy(columns(seq), dst.at[seq], own_sem)


def spread(src, dst, sems, own_sem):
    out, own = spread_plan(src, dst, sems, own_sem)
    for copy in out + [own]:
        copy.start()
    return out, own


def cube_second(whole, sems, first):
    at = flips()
    half = whole.shape[1] // 2
    first[0].wait_recv()
    block = whole.at[at(0, 1, 0)]
    top = block.at[pl.ds(0, half)]
    sent = [
        send(top, top, sems, 3, "seq", at(1, 0, 0)),
        send(block, block, sems, 5, "seq", at(0, 0, 1)),
    ]
    first[1].wait_recv()
    block = whole.at[at(1, 0, 0)]
    low = block.at[pl.ds(half, half)]
    sent += [
        send(low, low, sems, 4, "seq", at(0, 1, 0)),
        send(block, block, sems, 6, "seq", at(0, 0, 1)),
    ]
    return sent


def cube_third(whole, sems, second):
    at = flips()
    half = whole.shape[1] // 2
    block = whole.at[at(1, 1, 0)]
    sent = []
    for slot, came in ((0, second[0]), (1, second[2])):
        came.wait_recv()
        piece = block.at[pl.ds(slot * half, half)]
        sent.append(send(piece, piece, sems, 7 + slot, "seq", at(0, 0, 1)))
    return sent


def cube_end(first, second, third):
    first[2].wait_recv()
    second[1].wait_recv()
    second[3].wait_recv()
    arrived(third)
    for group in (first, second, third):
        left(group)


def share(src, dst, sems, own_sem):
    seq, n_seq, z = lax.axis_index("seq"), lax.axis_size("seq"), lax.axis_index("wt")
    own, piece = dst.shape[2:]
    rows = src.at[pl.ds(pl.multiple_of(z * own, own), own)]

    def columns(peer):
        return rows.at[:, pl.ds(pl.multiple_of(peer * piece, piece), piece)]

    sent = []
    for k in range(1, n_seq):
        peer = lax.rem(seq + k, n_seq)
        sent.append(send(columns(peer), dst.at[seq, z], sems, k - 1, "seq", peer))
    kept = pltpu.make_async_copy(columns(seq), dst.at[seq, z], own_sem)
    kept.start()
    return sent, kept


def pass_along(dst, sems):
    z, n_wt = lax.axis_index("wt"), lax.axis_size("wt")
    lines = dst.at[:, z]
    return [send(lines, lines, sems, k - 1, "wt", lax.rem(z + k, n_wt)) for k in range(1, n_wt)]


def pass_pairs(dst, sems):
    z, mate, far, _ = mates()
    lines = dst.at[:, z]
    return [send(lines, lines, sems, 0, "wt", far), send(lines, lines, sems, 1, "wt", mate)]


def pass_pairs_on(dst, sems, copies):
    _, mate, far, _ = mates()
    copies[0].wait_recv()
    lines = dst.at[:, far]
    return copies + [send(lines, lines, sems, 2, "wt", mate)]


def first_kernel(
    left_w, right_w, small, cot, tok, gain, taps, bias, goes,
    w_first, cot_f, act_f, w_small, inner, prev, switch, conv, mixed, select,
    first_in, w_near, ext, before, halo, part, recv,
    s_pair, s_small, s_own, s_cot, s_act, s_cz, s_az, s_halo, s_scatter, s_gather,
):
    seq, n_seq = lax.axis_index("seq"), lax.axis_size("seq")
    me = lax.axis_index("wt")
    count, width = tok.shape
    chan = inner.shape[1]
    half = left_w.shape[1]
    own_block = w_near.at[seq]
    placed = [
        pltpu.make_async_copy(left_w, own_block.at[:, pl.ds(0, half)], s_own.at[0]),
        pltpu.make_async_copy(right_w, own_block.at[:, pl.ds(half, half)], s_own.at[4]),
    ]
    for copy in placed:
        copy.start()
    kept = [keep(small, w_small, s_own.at[1])]

    def norm(at):
        v = tok[pl.ds(at, 16)].astype(F32)
        inverse = lax.rsqrt(jnp.mean(v * v, axis=-1, keepdims=True) + EPS)
        first_in[pl.ds(at, 16)] = (v * inverse * gain[...]).astype(BF16)

    step_rows(count, 16, norm)
    greet(("seq", "wt"))
    little = cube_first(small, w_small, s_small)
    sent1, kept1 = share(cot, cot_f, s_cot, s_own.at[2])
    sent2, kept2 = share(first_in, act_f, s_act, s_own.at[3])
    for copy in placed:
        copy.wait()
    pair1 = cube_first(own_block, w_near, s_pair)
    sent = sent1 + sent2
    arrived(sent)
    kept1.wait()
    kept2.wait()
    along = pass_along(cot_f, s_cz) + pass_along(act_f, s_az)
    little2 = cube_second(w_small, s_small, little)
    little3 = cube_third(w_small, s_small, little2)
    pair2 = cube_second(w_near, s_pair, pair1)
    pair3 = cube_third(w_near, s_pair, pair2)
    cube_end(little, little2, little3)
    cube_end(pair1, pair2, pair3)
    for copy in kept:
        copy.wait()
    far = pltpu.make_async_copy(w_near, w_first, s_own.at[0])
    far.start()

    def project(target, first_tile):
        def one(j, carry):
            columns = pl.ds(pl.multiple_of(j * UNITS, UNITS), UNITS)
            source = pl.ds(pl.multiple_of((first_tile + j) * UNITS, UNITS), UNITS)
            tile = w_near[:, :, source].reshape(width, UNITS)
            out = jnp.dot(first_in[...], tile, preferred_element_type=F32)
            target[:, columns] = out.astype(target.dtype)
            return carry

        lax.fori_loop(0, chan // UNITS, one, 0)

    project(inner, 0)
    last_row, row_before = goes[count - 1 :], goes[count - 2 : count - 1]
    cut = jnp.concatenate(
        [jnp.ones((13, 1), F32), (last_row * row_before)[:, :1], last_row[:, :1], jnp.ones((1, 1), F32)]
    )
    halo[0] = (inner[count - 16 :].astype(F32) * cut).astype(BF16)
    before[:16] = jnp.ones((16, 128), F32)
    before[16:] = goes[...]
    ahead = remote(halo.at[0], halo.at[1], s_halo, 0, "seq", lax.rem(seq + 1, n_seq))

    @pl.when(seq + 1 < n_seq)
    def _():
        ahead.start()

    @pl.when(seq == 0)
    def _():
        halo[1] = jnp.zeros_like(halo[1])

    project(switch, chan // UNITS)
    ext[16:] = inner[...].astype(F32)

    @pl.when(seq > 0)
    def _():
        ahead.wait_recv()

    ext[:16] = halo[1].astype(F32)
    prev[...] = ext[8:16]

    def convolve(at):
        v = ext[pl.ds(pl.multiple_of(at + 8, 8), 24)]
        g = before[pl.ds(pl.multiple_of(at + 8, 8), 24)]
        same = None
        out = bias[...] + taps[0:1] * v[8:]
        for k in range(1, KC):
            step = g[9 - k : 25 - k]
            same = step if same is None else same * step
            out = out + taps[k : k + 1] * v[8 - k : 24 - k] * same[:, :1]
        conv[pl.ds(at, 16)] = out
        mixed[pl.ds(at, 16)] = (out * jax.nn.sigmoid(out)).astype(BF16)

    step_rows(count, 16, convolve)
    deep = w_small.shape[1]
    all_rows = nt(w_small[...].reshape(n_seq * deep, chan), mixed[...])
    rows = part.shape[0] // n_seq
    for j in range(n_seq):
        part[j * rows : (j + 1) * rows] = all_rows[j * deep + 16 : j * deep + 16 + rows]
    first = scatter_start(part, recv, s_scatter, "wt")
    rows = recv.shape[1]
    arrived(first)
    select[pl.ds(me * rows, rows)] = summed(part, recv, 0, rows, me * rows)
    second = gather_start(select, rows, s_gather, "wt")
    arrived(second)
    arrived(along)
    far.wait()

    @pl.when(seq + 1 < n_seq)
    def _():
        ahead.wait_send()

    for group in (along, sent, first, second):
        left(group)


def first_gather(left_w, right_w, small, cot, tok, gain, taps, bias, goes, rows_sel, n_wt, n_seq, ident):
    count, width = cot.shape
    rows, chan = left_w.shape
    pair_shape = (n_seq, rows, 2 * chan)
    lines = rows_sel * n_seq
    share_shape = jax.ShapeDtypeStruct((n_seq, n_wt, count // n_wt, width // n_seq), BF16)
    return pl.pallas_call(
        first_kernel,
        out_shape=[
            jax.ShapeDtypeStruct(pair_shape, BF16),
            share_shape,
            share_shape,
            jax.ShapeDtypeStruct((n_seq,) + small.shape, BF16),
            jax.ShapeDtypeStruct((count, chan), BF16),
            jax.ShapeDtypeStruct((8, chan), F32),
            jax.ShapeDtypeStruct((count, chan), F32),
            jax.ShapeDtypeStruct((count, chan), F32),
            jax.ShapeDtypeStruct((count, chan), BF16),
            jax.ShapeDtypeStruct((lines, count), F32),
        ],
        in_specs=[ANY] * 3 + [VMEM] * 6,
        out_specs=[ANY] * 3 + [VMEM] * 7,
        scratch_shapes=[
            pltpu.VMEM((count, width), BF16),
            pltpu.VMEM(pair_shape, BF16),
            pltpu.VMEM((16 + count, chan), F32),
            pltpu.VMEM((16 + count, 128), F32),
            pltpu.VMEM((2, 16, chan), BF16),
            pltpu.VMEM((lines, count), F32),
            pltpu.VMEM((n_wt - 1, lines // n_wt, count), F32),
            cube_sems(),
            cube_sems(),
            pltpu.SemaphoreType.DMA((5,)),
            pair_sems(n_seq),
            pair_sems(n_seq),
            pair_sems(n_wt),
            pair_sems(n_wt),
            pltpu.SemaphoreType.DMA((2, 1)),
            pair_sems(n_wt),
            pair_sems(n_wt),
        ],
        compiler_params=pltpu.CompilerParams(
            collective_id=ident, has_side_effects=True, vmem_limit_bytes=VMEM_BYTES
        ),
        cost_estimate=pl.CostEstimate(flops=10**9, bytes_accessed=10**8, transcendentals=0),
    )(left_w, right_w, small, cot, tok, gain[None], taps, bias[None], goes)


def ffn_kernel(cube, x, c, wg, wu, wd, gated, acts, down, d_second, *refs):
    pieces, refs = refs[:cube], refs[cube:]
    acc_down, acc_second = refs[:2]
    step = pl.program_id(0)
    if cube:
        held, s_spread, s_own = refs[2:]
        sent, kept = spread_plan(held, pieces[0], s_spread, s_own)

        @pl.when(step == 0)
        def _():
            held[...] = x[...]
            greet(("seq",))
            for copy in sent + [kept]:
                copy.start()

    @pl.when(step == 0)
    def _():
        acc_down[...] = jnp.zeros_like(acc_down)
        acc_second[...] = jnp.zeros_like(acc_second)

    gate = jnp.dot(x[...], wg[...], preferred_element_type=F32)
    up = jnp.dot(x[...], wu[...], preferred_element_type=F32)
    d_hidden = jnp.dot(c[...], wd[...], preferred_element_type=F32)
    sigma = jax.nn.sigmoid(gate)
    act = gate * sigma
    hidden = (act * up).astype(BF16)
    d_gate = (d_hidden * up * (sigma * (1.0 + gate * (1.0 - sigma)))).astype(BF16)
    d_up = (d_hidden * act).astype(BF16)
    acts[:, :UNITS] = hidden
    acts[:, UNITS : 2 * UNITS] = d_gate
    acts[:, 2 * UNITS : 3 * UNITS] = d_up
    acts[:, 3 * UNITS :] = gated[...]
    acc_down[...] += nt(hidden, wd[...])
    acc_second[...] += nt(d_gate, wg[...]) + nt(d_up, wu[...])

    @pl.when(step == pl.num_programs(0) - 1)
    def _():
        down[...] = acc_down[...].astype(BF16)
        d_second[...] = acc_second[...].astype(BF16)
        if cube:
            kept.wait()
            arrived(sent)
            left(sent)


def ffn(x, c, w_all, gated, cube, n_seq, ident):
    tok, width = x.shape
    units, chan = w_all.shape[1] // 3, gated.shape[1]
    steps = units // UNITS
    span = 3 * UNITS + chan // steps
    whole = pl.BlockSpec((tok, width), lambda i: (0, 0))
    tile = lambda part: pl.BlockSpec((width, UNITS), lambda i: (0, part * steps + i))
    return pl.pallas_call(
        functools.partial(ffn_kernel, int(cube)),
        grid=(steps,),
        in_specs=[whole, whole, tile(0), tile(1), tile(2)]
        + [pl.BlockSpec((tok, chan // steps), lambda i: (0, i))],
        out_specs=[pl.BlockSpec((tok, span), lambda i: (0, i)), whole, whole] + [ANY] * cube,
        out_shape=[
            jax.ShapeDtypeStruct((tok, 3 * units + chan), BF16),
            jax.ShapeDtypeStruct((tok, width), BF16),
            jax.ShapeDtypeStruct((tok, width), BF16),
        ]
        + [jax.ShapeDtypeStruct((n_seq, tok, width // n_seq), BF16)] * cube,
        scratch_shapes=[pltpu.VMEM((tok, width), F32)] * 2
        + ([pltpu.VMEM((tok, width), BF16), pair_sems(n_seq), pltpu.SemaphoreType.DMA] if cube else []),
        compiler_params=pltpu.CompilerParams(
            vmem_limit_bytes=VMEM_BYTES,
            **(dict(collective_id=ident, has_side_effects=True) if cube else {}),
        ),
        cost_estimate=pl.CostEstimate(
            flops=12 * tok * width * units, bytes_accessed=6 * width * units, transcendentals=0
        ),
    )(x, c, w_all, w_all, w_all, gated)


def grads_kernel(lefts, *refs):
    n, m = max(lefts) + 1, len(lefts)
    for which, act, out in zip(lefts, refs[n : n + m], refs[n + m :]):
        out[...] = jnp.dot(refs[which][...], act[...], preferred_element_type=F32)


def grads(left_ops, lefts, acts):
    rows, tok = left_ops[0].shape
    cols = acts[0].shape[1]
    n = len(acts)
    return pl.pallas_call(
        functools.partial(grads_kernel, lefts),
        grid=(cols // UNITS,),
        in_specs=[pl.BlockSpec((rows, tok), lambda i: (0, 0))] * len(left_ops)
        + [pl.BlockSpec((tok, UNITS), lambda i: (0, i))] * n,
        out_specs=[pl.BlockSpec((rows, UNITS), lambda i: (0, i))] * n,
        out_shape=[jax.ShapeDtypeStruct((rows, cols), F32)] * n,
        compiler_params=pltpu.CompilerParams(vmem_limit_bytes=VMEM_BYTES),
        cost_estimate=pl.CostEstimate(
            flops=2 * n * tok * rows * cols, bytes_accessed=2 * n * tok * cols, transcendentals=0
        ),
    )(*left_ops, *acts)


def wt_sum_kernel(part, out, recv, s_scatter, s_gather):
    me = lax.axis_index("wt")
    rows = recv.shape[1]
    greet(("wt",))
    first = scatter_start(part, recv, s_scatter, "wt")
    arrived(first)
    out[pl.ds(me * rows, rows)] = summed(part, recv, 0, rows, me * rows)
    second = gather_start(out, rows, s_gather, "wt")
    arrived(second)
    left(first)
    left(second)


def wt_sum(part, n_wt, ident):
    rows, cols = part.shape
    return pl.pallas_call(
        wt_sum_kernel,
        out_shape=jax.ShapeDtypeStruct((rows, cols), F32),
        in_specs=[VMEM],
        out_specs=VMEM,
        scratch_shapes=[
            pltpu.VMEM((n_wt - 1, rows // n_wt, cols), F32),
            pair_sems(n_wt),
            pair_sems(n_wt),
        ],
        compiler_params=pltpu.CompilerParams(
            collective_id=ident, has_side_effects=True, vmem_limit_bytes=VMEM_BYTES
        ),
        cost_estimate=pl.CostEstimate(flops=10**5, bytes_accessed=10**6, transcendentals=0),
    )(part)


def second_norm_kernel(part, tok, gain, out, res, recv, pend, s_scatter, s_gather):
    me = lax.axis_index("wt")
    rows = recv.shape[1]
    greet(("wt",))
    first = line_scatter_start(part, recv, s_scatter)
    first = line_scatter_mid(part, recv, pend, s_scatter, first)
    line_scatter_end(first)
    row0 = me * rows

    def body(at):
        own = tok[pl.ds(pl.multiple_of(row0 + at, 16), 16)].astype(F32)
        r = own + line_summed(part, recv, at, 16, row0)
        res[pl.ds(at, 16)] = r
        inverse = lax.rsqrt(jnp.mean(r * r, axis=-1, keepdims=True) + EPS)
        out[pl.ds(pl.multiple_of(row0 + at, 16), 16)] = (r * inverse * gain[...]).astype(BF16)

    step_rows(rows, 16, body)
    second = line_gather_start(out, rows, s_gather)
    second = line_gather_mid(out, rows, s_gather, second)
    line_gather_end(second)
    left(first)
    left(second)


def second_norm(part, tok_own, gain, n_wt, ident):
    rows, cols = part.shape
    own = rows // n_wt
    return pl.pallas_call(
        second_norm_kernel,
        out_shape=[
            jax.ShapeDtypeStruct((rows, cols), BF16),
            jax.ShapeDtypeStruct((own, cols), F32),
        ],
        in_specs=[VMEM] * 3,
        out_specs=[VMEM] * 2,
        scratch_shapes=[
            pltpu.VMEM((n_wt - 1, own, cols), BF16),
            pltpu.VMEM((own, cols), BF16),
            pair_sems(n_wt),
            pair_sems(n_wt),
        ],
        compiler_params=pltpu.CompilerParams(
            collective_id=ident, has_side_effects=True, vmem_limit_bytes=VMEM_BYTES
        ),
        cost_estimate=pl.CostEstimate(flops=10**6, bytes_accessed=10**8, transcendentals=0),
    )(part, tok_own, gain[None])


def norm_back_rows(grad, vals, gain):
    inverse = lax.rsqrt(jnp.mean(vals * vals, axis=-1, keepdims=True) + EPS)
    normed = vals * inverse
    scaled = grad * gain
    mean = jnp.mean(scaled * normed, axis=-1, keepdims=True)
    return inverse * (scaled - normed * mean), grad * normed


def second_back_kernel(n_spread, part, res, cot, gain, *refs):
    srcs, refs = refs[:n_spread], refs[n_spread:]
    out, d_res, gain_grad = refs[:3]
    dsts, refs = refs[3 : 3 + n_spread], refs[3 + n_spread :]
    recv, pend, s_scatter, s_gather = refs[:4]
    me = lax.axis_index("wt")
    rows = recv.shape[1]
    greet(("wt", "seq") if n_spread else ("wt",))
    first = line_scatter_start(part, recv, s_scatter)
    spreads = [
        spread(srcs[i], dsts[i], refs[4 + 2 * i], refs[5 + 2 * i]) for i in range(n_spread)
    ]
    gain_grad[...] = jnp.zeros_like(gain_grad)
    first = line_scatter_mid(part, recv, pend, s_scatter, first)
    line_scatter_end(first)
    row0 = me * rows

    def body(at):
        grad = line_summed(part, recv, at, 16, row0)
        back, prod = norm_back_rows(grad, res[pl.ds(at, 16)], gain[...])
        gain_grad[...] += prod[:8] + prod[8:]
        d = cot[pl.ds(pl.multiple_of(row0 + at, 16), 16)].astype(F32) + back
        d_res[pl.ds(at, 16)] = d
        out[pl.ds(pl.multiple_of(row0 + at, 16), 16)] = d.astype(BF16)

    step_rows(rows, 16, body)
    second = line_gather_start(out, rows, s_gather)
    second = line_gather_mid(out, rows, s_gather, second)
    line_gather_end(second)
    for sent, kept in spreads:
        kept.wait()
        arrived(sent)
        left(sent)
    left(first)
    left(second)


def second_back(part, res, cot_own, gain, srcs, n_wt, n_seq, ident):
    rows, cols = part.shape
    own = rows // n_wt
    return pl.pallas_call(
        functools.partial(second_back_kernel, len(srcs)),
        out_shape=[
            jax.ShapeDtypeStruct((rows, cols), BF16),
            jax.ShapeDtypeStruct((own, cols), F32),
            jax.ShapeDtypeStruct((8, cols), F32),
        ]
        + [jax.ShapeDtypeStruct((n_seq, rows, cols // n_seq), BF16)] * len(srcs),
        in_specs=[VMEM] * (4 + len(srcs)),
        out_specs=[VMEM] * 3 + [ANY] * len(srcs),
        scratch_shapes=[
            pltpu.VMEM((n_wt - 1, own, cols), BF16),
            pltpu.VMEM((own, cols), BF16),
            pair_sems(n_wt),
            pair_sems(n_wt),
        ]
        + [pair_sems(n_seq), pltpu.SemaphoreType.DMA] * len(srcs),
        compiler_params=pltpu.CompilerParams(
            collective_id=ident, has_side_effects=True, vmem_limit_bytes=VMEM_BYTES
        ),
        cost_estimate=pl.CostEstimate(flops=10**6, bytes_accessed=10**8, transcendentals=0),
    )(part, res, cot_own, gain[None], *srcs)


def last_kernel(cube, part, tok, d_res, gain, gain_grad2, sel, stp, taps, decays, bias3, line, *refs):
    blocks, refs = refs[:cube], refs[cube:]
    if cube:
        cot_t, second_t, branch_t, first_t, acts = refs[:5]
        refs = refs[5:]
    out, block_out, sel_out, stp_out, taps_out, decays_out, *bias_outs = refs[:9]
    gain_outs, refs = refs[9:11], refs[11:]
    if cube:
        grad_outs, late_outs, refs = refs[:4], refs[4 : 4 + cube], refs[4 + cube :]
        tile, s_tile, wholes, refs = refs[0], refs[1], refs[2 : 2 + cube], refs[2 + cube :]
        width = tile.shape[2]
        tiles = acts.shape[1] // width

        def fetch(j, slot):
            columns = acts.at[:, pl.ds(pl.multiple_of(j * width, width), width)]
            return pltpu.make_async_copy(columns, tile.at[slot], s_tile.at[slot])

        def one_tile(j, carry):
            slot = lax.rem(j, 2)

            @pl.when(j + 1 < tiles)
            def _():
                fetch(j + 1, 1 - slot).start()

            fetch(j, slot).wait()
            at = 0
            for left_op, out_ref in zip((cot_t, second_t, second_t, branch_t), grad_outs):
                wide = out_ref.shape[1] // tiles
                out_ref[:, pl.ds(pl.multiple_of(j * wide, wide), wide)] = jnp.dot(
                    left_op[...], tile[slot, :, at : at + wide], preferred_element_type=F32
                )
                at += wide
            return carry

        fetch(0, 0).start()
    recv, pend, recv_sel, recv_stp, recv_chan, pack, chan_out, gain_buf, recv_gz, recv_gs = refs[:10]
    s_scatter, s_gather, s_sel, s_stp, s_chan, s_cg, s_gz, s_gs, s_block = refs[10:19]
    refs = refs[19:]
    me, n_wt = lax.axis_index("wt"), lax.axis_size("wt")
    seq, n_seq = lax.axis_index("seq"), lax.axis_size("seq")
    rows = recv.shape[1]
    block_out[pl.ds(pl.multiple_of(me * rows, 16), rows)] = line[...]
    greet(("wt", "seq"))
    first = line_scatter_start(part, recv, s_scatter)
    cubes = []
    for i in range(cube):
        s_cube, s_own = refs[2 * i : 2 * i + 2]
        cubes.append([cube_first(blocks[i], wholes[i], s_cube), s_cube, wholes[i]])
        cubes[-1].append(keep(blocks[i], wholes[i], s_own))
    share = -(-(KC + NS + 3) // n_seq)
    lines = [(taps, i) for i in range(KC)] + [(decays, i) for i in range(NS)]
    lines += [(bias3, i) for i in range(3)]
    for at, (ref, i) in enumerate(lines):
        pack[at // share, at % share : at % share + 1] = ref[i : i + 1]
    smalls = []
    for src, dst, sems in ((sel, recv_sel, s_sel), (stp, recv_stp, s_stp), (pack, recv_chan, s_chan)):
        for k in range(1, n_seq):
            peer = lax.rem(seq + k, n_seq)
            smalls.append(send(src.at[peer], dst.at[k - 1], sems, k - 1, "seq", peer))
    if cube:
        lax.fori_loop(0, 3, one_tile, 0)
    first = line_scatter_mid(part, recv, pend, s_scatter, first)
    if cube:
        lax.fori_loop(3, tiles - 2, one_tile, 0)
    line_scatter_end(first)
    row0 = me * rows
    gain_buf[...] = jnp.zeros_like(gain_buf)

    def body(at):
        grad = line_summed(part, recv, at, 16, row0)
        own = tok[pl.ds(pl.multiple_of(row0 + at, 16), 16)].astype(F32)
        back, prod = norm_back_rows(grad, own, gain[...])
        gain_buf[...] += prod[:8] + prod[8:]
        out[pl.ds(pl.multiple_of(row0 + at, 16), 16)] = (d_res[pl.ds(at, 16)] + back).astype(BF16)

    step_rows(rows, 16, body)
    second = line_gather_start(out, rows, s_gather)
    third = line_gather_start(block_out, rows, s_block)
    high = recv_gz.shape[1] // 2
    for i, grad in enumerate((gain_buf, gain_grad2)):
        line = jnp.sum(grad[...], axis=0, keepdims=True)
        for t in range(high):
            recv_gz[me, i * high + t : i * high + t + 1] = line[:, t * 128 : (t + 1) * 128]
    mine_z = recv_gz.at[me]
    zs = [send(mine_z, mine_z, s_gz, k - 1, "wt", lax.rem(me + k, n_wt)) for k in range(1, n_wt)]
    cubes2 = [cube_second(whole, sems, one) for one, sems, whole, _ in cubes]
    if cube:
        lax.fori_loop(tiles - 2, tiles, one_tile, 0)
    arrived(smalls)
    for src, recv_one, one_out in ((sel, recv_sel, sel_out), (stp, recv_stp, stp_out)):
        total = src[seq].astype(F32)
        for k in range(n_seq - 1):
            total = total + recv_one[k].astype(F32)
        one_out[...] = total[: one_out.shape[0]]
    total = pack[seq]
    for k in range(n_seq - 1):
        total = total + recv_chan[k]
    chan_out[seq] = total
    mine = chan_out.at[seq]
    chans = [
        send(mine, mine, s_cg, k - 1, "seq", lax.rem(seq + k, n_seq)) for k in range(1, n_seq)
    ]
    second = line_gather_mid(out, rows, s_gather, second)
    third = line_gather_mid(block_out, rows, s_block, third)
    arrived(zs)
    total = recv_gz[0]
    for pos in range(1, n_wt):
        total = total + recv_gz[pos]
    recv_gs[seq] = total
    mine_s = recv_gs.at[seq]
    ss = [
        send(mine_s, mine_s, s_gs, k - 1, "seq", lax.rem(seq + k, n_seq)) for k in range(1, n_seq)
    ]
    cubes3 = [cube_third(whole, sems, two) for (_, sems, whole, _), two in zip(cubes, cubes2)]
    arrived(ss)
    total = recv_gs[0]
    for pos in range(1, n_seq):
        total = total + recv_gs[pos]
    for i, gain_out in enumerate(gain_outs):
        for t in range(high):
            gain_out[:, t * 128 : (t + 1) * 128] = total[i * high + t : i * high + t + 1]
    arrived(chans)
    outs = [(taps_out, i) for i in range(KC)] + [(decays_out, i) for i in range(NS)]
    outs += [(bias_out, 0) for bias_out in bias_outs]
    for at, (ref, i) in enumerate(outs):
        ref[i : i + 1] = chan_out[at // share, at % share : at % share + 1]
    for k, ((one, _, whole, kept), two, three) in enumerate(zip(cubes, cubes2, cubes3)):
        cube_end(one, two, three)
        kept.wait()

        def late_tile(j, carry, whole=whole, late_out=late_outs[k]):
            columns = pl.ds(pl.multiple_of(j * UNITS, UNITS), UNITS)
            act = whole[:, :, columns].reshape(first_t.shape[1], UNITS)
            late_out[:, columns] = jnp.dot(first_t[...], act, preferred_element_type=F32)
            return carry

        lax.fori_loop(0, whole.shape[2] // UNITS, late_tile, 0)
    line_gather_end(second)
    line_gather_end(third)
    for group in (first, second, third, smalls, chans, zs, ss):
        left(group)


def last(
    part, tok_own, d_res, gain, gain_grad2, sel, stp, rows_small, taps, decays, bias3, line,
    blocks, more, n_wt, n_seq, ident,
):
    rows, cols = part.shape
    own = rows // n_wt
    chan = taps.shape[1]
    if more:
        deep, tok_all = more[0].shape
        units = (more[4].shape[1] - chan) // 3
        span = more[4].shape[1] // (units // UNITS)
    return pl.pallas_call(
        functools.partial(last_kernel, len(blocks)),
        out_shape=[
            jax.ShapeDtypeStruct((rows, cols), BF16),
            jax.ShapeDtypeStruct((rows, cols), BF16),
        ]
        + [
            jax.ShapeDtypeStruct((n, chan), F32)
            for n in rows_small + (taps.shape[0], decays.shape[0], 1, 1, 1)
        ]
        + [jax.ShapeDtypeStruct((1, cols), F32)] * 2
        + (
            [jax.ShapeDtypeStruct((deep, w), F32) for w in (units, units, units, chan)]
            + [jax.ShapeDtypeStruct((deep, a.shape[1]), F32) for a in blocks]
            if more
            else []
        ),
        in_specs=[VMEM] * 11 + [ANY] * len(blocks) + ([VMEM] * 4 + [ANY] if more else []),
        out_specs=[VMEM] * (11 + (4 + len(blocks) if more else 0)),
        scratch_shapes=(
            [pltpu.VMEM((2, tok_all, span), BF16), pltpu.SemaphoreType.DMA((2,))]
            + [pltpu.VMEM((n_seq,) + a.shape, BF16) for a in blocks]
            if more
            else []
        )
        + [
            pltpu.VMEM((n_wt - 1, own, cols), BF16),
            pltpu.VMEM((own, cols), BF16),
            pltpu.VMEM((n_seq - 1,) + sel.shape[1:], BF16),
            pltpu.VMEM((n_seq - 1,) + stp.shape[1:], BF16),
            pltpu.VMEM((n_seq - 1, 8, chan), F32),
            pltpu.VMEM((n_seq, 8, chan), F32),
            pltpu.VMEM((n_seq, 8, chan), F32),
            pltpu.VMEM((8, cols), F32),
            pltpu.VMEM((n_wt, 2 * cols // 128, 128), F32),
            pltpu.VMEM((n_seq, 2 * cols // 128, 128), F32),
            pair_sems(n_wt),
            pair_sems(n_wt),
            pair_sems(n_seq),
            pair_sems(n_seq),
            pair_sems(n_seq),
            pair_sems(n_seq),
            pair_sems(n_wt),
            pair_sems(n_seq),
            pair_sems(n_wt),
        ]
        + [cube_sems(), pltpu.SemaphoreType.DMA] * len(blocks),
        compiler_params=pltpu.CompilerParams(
            collective_id=ident, has_side_effects=True, vmem_limit_bytes=VMEM_BYTES
        ),
        cost_estimate=pl.CostEstimate(flops=10**6, bytes_accessed=10**8, transcendentals=0),
    )(part, tok_own, d_res, gain[None], gain_grad2, sel, stp, taps, decays, bias3, line, *blocks, *more)


def hand_out_kernel(n, *refs):
    srcs, dsts, held, sems = refs[:n], refs[n : 2 * n], refs[2 * n : 3 * n], refs[3 * n]
    into = [pltpu.make_async_copy(srcs[i], held[i], sems.at[0, i]) for i in range(n)]
    away = [pltpu.make_async_copy(held[i], dsts[i], sems.at[1, i]) for i in range(n)]
    for copy in into:
        copy.start()
    for first, second in zip(into, away):
        first.wait()
        second.start()
    for copy in away:
        copy.wait()


def hand_out(arrays):
    n = len(arrays)
    size = sum(a.size * a.dtype.itemsize for a in arrays)
    return pl.pallas_call(
        functools.partial(hand_out_kernel, n),
        out_shape=[jax.ShapeDtypeStruct(a.shape, a.dtype) for a in arrays],
        in_specs=[ANY] * n,
        out_specs=[ANY] * n,
        scratch_shapes=[pltpu.VMEM(a.shape, a.dtype) for a in arrays]
        + [pltpu.SemaphoreType.DMA((2, n))],
        compiler_params=pltpu.CompilerParams(vmem_limit_bytes=VMEM_BYTES),
        cost_estimate=pl.CostEstimate(flops=0, bytes_accessed=2 * size, transcendentals=0),
    )(*arrays)


def load(ref):
    return tuple(ref[n] for n in range(NS))


def store(ref, values):
    for n in range(NS):
        ref[n] = values[n]


def fold(mine, box, recv, a2, carried, backward):
    n, me = lax.axis_size("seq"), lax.axis_index("seq")
    carried[...] = jnp.zeros_like(carried)
    for k in range(n - 1, 0, -1):

        @pl.when((me + k < n) if backward else (me >= k))
        def _():
            giver = me + k if backward else me - k
            remote(mine, recv.at[k - 1], box, k - 1, "seq", giver).wait_recv()
            through = recv[k - 1, NS]
            for s in range(NS):
                carried[s] = (
                    jnp.exp2(a2[s] * through) * carried[s] + recv[k - 1, s]
                )


def hand_on(mine, recv, box, backward):
    n, me = lax.axis_size("seq"), lax.axis_index("seq")
    for k in range(1, n):

        @pl.when((me >= k) if backward else (me + k < n))
        def _():
            peer = me - k if backward else me + k
            send(mine, recv.at[k - 1], box, k - 1, "seq", peer)


def handed(mine, recv, box, backward):
    n, me = lax.axis_size("seq"), lax.axis_index("seq")
    for k in range(1, n):

        @pl.when((me >= k) if backward else (me + k < n))
        def _():
            peer = me - k if backward else me + k
            remote(mine, recv.at[k - 1], box, k - 1, "seq", peer).wait_send()


def fwd_kernel(sa, dx, wr, a2, y, h0, mine, recv, box):
    tok = sa.shape[0]
    greet(("seq",))

    def end(t, carry):
        s, d = sa[t], dx[t]
        h, total = carry
        return (
            tuple(jnp.exp2(s * a2[n]) * h[n] + wr[n, t] * d for n in range(NS)),
            total + s,
        )

    zero = jnp.zeros(sa.shape[1:], F32)
    ends, total = lax.fori_loop(0, tok, end, ((zero,) * NS, zero), unroll=4)
    store(mine, ends)
    mine[NS] = total
    hand_on(mine, recv, box, False)
    fold(mine, box, recv, a2, h0, False)

    def body(t, h):
        s, d = sa[t], dx[t]
        new, sums = [], [None] * 4
        for n in range(NS):
            hn = jnp.exp2(s * a2[n]) * h[n] + wr[n, t] * d
            new.append(hn)
            c = wr[NS + n, t] * hn
            sums[n % 4] = c if sums[n % 4] is None else sums[n % 4] + c
        y[t] = (sums[0] + sums[1]) + (sums[2] + sums[3])
        return tuple(new)

    lax.fori_loop(0, tok, body, load(h0), unroll=4)
    handed(mine, recv, box, False)


def fwd_scan(sa, dx, wr, a2, n_seq, ident):
    tok, high = sa.shape[:2]
    return pl.pallas_call(
        fwd_kernel,
        out_shape=[
            jax.ShapeDtypeStruct((tok, high, 128), F32),
            jax.ShapeDtypeStruct((NS, high, 128), F32),
        ],
        in_specs=[VMEM, VMEM, SMEM, VMEM],
        out_specs=[VMEM] * 2,
        scratch_shapes=[
            pltpu.VMEM((NS + 1, high, 128), F32),
            pltpu.VMEM((n_seq - 1, NS + 1, high, 128), F32),
            pair_sems(n_seq),
        ],
        compiler_params=pltpu.CompilerParams(
            collective_id=ident, has_side_effects=True, vmem_limit_bytes=VMEM_BYTES
        ),
        cost_estimate=pl.CostEstimate(
            flops=10**8, bytes_accessed=8 * 10**7, transcendentals=2 * tok * NS * 1024
        ),
    )(sa, dx, wr, a2)


def bwd_kernel(
    cube, sa, dx, wr, do_flat, a2, h0, part, res, *refs
):
    src, refs = refs[:cube], refs[cube:]
    along, ds2, grad_a, sums, out = refs[:5]
    dst, refs = refs[5 : 5 + cube], refs[5 + cube :]
    hs, qw, qr, pw, pr, g0, mine, recv, recv_z, pend, do, al2, d22, box, s_scatter = refs[:15]
    tok = sa.shape[0]
    chunk = qw.shape[0] // (NS * 8)
    high = sa.shape[1]
    for c in range(high):
        do[pl.ds(c, tok, stride=high), :] = do_flat[:, c * 128 : (c + 1) * 128]
    greet(("wt", "seq"))
    first = line_scatter_start(part, recv_z, s_scatter)

    def end(i, carry):
        t = tok - 1 - i
        s, d = sa[t], do[pl.ds(pl.multiple_of(t * high, high), high), :]
        g, total = carry
        return (
            tuple(jnp.exp2(s * a2[n]) * (g[n] + wr[NS + n, t] * d) for n in range(NS)),
            total + s,
        )

    zero = jnp.zeros(sa.shape[1:], F32)
    ends, total = lax.fori_loop(0, tok, end, ((zero,) * NS, zero), unroll=4)
    store(mine, ends)
    mine[NS] = total
    hand_on(mine, recv, box, True)
    if cube:
        s_seq, s_wt, s_own = refs[15:]
        sent, kept = share(src[0], dst[0], s_seq, s_own)
    first = line_scatter_mid(part, recv_z, pend, s_scatter, first)

    def again(t, h):
        s, d = sa[t], dx[t]
        new = []
        for n in range(NS):
            hs[t, n] = h[n]
            new.append(jnp.exp2(s * a2[n]) * h[n] + wr[n, t] * d)
        return tuple(new)

    lax.fori_loop(0, tok, again, load(h0), unroll=2)

    fold(mine, box, recv, a2, g0, True)
    if cube:
        arrived(sent)
        kept.wait()
        passed = pass_pairs(dst[0], s_wt)
    grad_a[...] = jnp.zeros_like(grad_a)

    def one_chunk(j, g):
        base = (tok // chunk - 1 - j) * chunk

        def body(i, g):
            at = chunk - 1 - i
            t = base + at
            s, d, o = sa[t], dx[t], do[pl.ds(pl.multiple_of(t * high, high), high), :]
            al = d2 = None
            new = []
            for n in range(NS):
                hp = hs[t, n]
                f = jnp.exp2(s * a2[n])
                hn = f * hp + wr[n, t] * d
                gn = wr[NS + n, t] * o + g[n]
                adj = f * gn
                new.append(adj)
                th = adj * hp
                grad_a[n] += th * s
                x = wr[n, t] * gn
                al = x if al is None else al + x
                x = a2[n] * th
                d2 = x if d2 is None else d2 + x
                row = pl.multiple_of((at * NS + n) * 8, 8)
                qw[pl.ds(row, 8), :] = gn * d
                qr[pl.ds(row, 8), :] = hn * o
            al2[pl.ds(pl.multiple_of(at * high, high), high), :] = al
            d22[pl.ds(pl.multiple_of(at * high, high), high), :] = d2
            return tuple(new)

        g = lax.fori_loop(0, chunk, body, g)

        def lanes(i, carry):
            for q, p in ((qw, pw), (qr, pr)):
                acc = q[pl.ds(i * NS * 8, NS, stride=8), :]
                for s in range(1, 8):
                    acc = acc + q[pl.ds(i * NS * 8 + s, NS, stride=8), :]
                p[pl.ds(pl.multiple_of(i * NS, NS), NS), :] = acc
            return carry

        lax.fori_loop(0, chunk, lanes, 0, unroll=4)
        lines = pl.ds(pl.multiple_of(base, chunk), chunk)
        for c in range(high):
            columns = slice(c * 128, (c + 1) * 128)
            along[lines, columns] = al2[pl.ds(c, chunk, stride=high), :]
            ds2[lines, columns] = d22[pl.ds(c, chunk, stride=high), :]
        ones = jnp.ones((8, 128), BF16)
        for which, p in enumerate((pw, pr)):
            upper = p[...].astype(BF16)
            lower = (p[...] - upper.astype(F32)).astype(BF16)
            row = which * (tok // chunk) + base // chunk
            sums[pl.ds(row, 1), :] = (nt(ones, upper) + nt(ones, lower))[:1]
        return g

    half = tok // chunk // 2
    g = lax.fori_loop(0, half, one_chunk, load(g0))
    if cube:
        passed = pass_pairs_on(dst[0], s_wt, passed)
    lax.fori_loop(half, tok // chunk, one_chunk, g)
    handed(mine, recv, box, True)
    line_scatter_end(first)
    rows = recv_z.shape[1]
    row0 = lax.axis_index("wt") * rows

    def block_rows(at):
        out[pl.ds(at, 16)] = (res[pl.ds(at, 16)] + line_summed(part, recv_z, at, 16, row0)).astype(BF16)

    step_rows(rows, 16, block_rows)
    left(first)
    if cube:
        arrived(passed[1:])
        left(sent)
        left(passed)


def bwd_scan(sa, dx, wr, do, a2, h0, part, res, src, n_wt, n_seq, ident):
    tok, high = sa.shape[:2]
    rows, cols = part.shape
    chunk = 32
    return pl.pallas_call(
        functools.partial(bwd_kernel, len(src)),
        out_shape=[
            jax.ShapeDtypeStruct((tok, high * 128), F32),
            jax.ShapeDtypeStruct((tok, high * 128), F32),
            jax.ShapeDtypeStruct((NS, high, 128), F32),
            jax.ShapeDtypeStruct((2 * tok // chunk, chunk * NS), F32),
            jax.ShapeDtypeStruct((rows // n_wt, cols), BF16),
        ]
        + [jax.ShapeDtypeStruct((n_seq, n_wt, rows // n_wt, cols // n_seq), BF16)] * len(src),
        in_specs=[VMEM, VMEM, SMEM] + [VMEM] * (5 + len(src)),
        out_specs=[VMEM] * 5 + [ANY] * len(src),
        scratch_shapes=[
            pltpu.VMEM((tok, NS, high, 128), F32),
            pltpu.VMEM((chunk * NS * 8, 128), F32),
            pltpu.VMEM((chunk * NS * 8, 128), F32),
            pltpu.VMEM((chunk * NS, 128), F32),
            pltpu.VMEM((chunk * NS, 128), F32),
            pltpu.VMEM((NS, high, 128), F32),
            pltpu.VMEM((NS + 1, high, 128), F32),
            pltpu.VMEM((n_seq - 1, NS + 1, high, 128), F32),
            pltpu.VMEM((n_wt - 1, rows // n_wt, cols), BF16),
            pltpu.VMEM((rows // n_wt, cols), BF16),
            pltpu.VMEM((tok * high, 128), F32),
            pltpu.VMEM((chunk * high, 128), F32),
            pltpu.VMEM((chunk * high, 128), F32),
            pair_sems(n_seq),
            pair_sems(n_wt),
        ]
        + [pair_sems(n_seq), pair_sems(n_wt), pltpu.SemaphoreType.DMA] * len(src),
        compiler_params=pltpu.CompilerParams(
            collective_id=ident, has_side_effects=True, vmem_limit_bytes=VMEM_BYTES
        ),
        cost_estimate=pl.CostEstimate(
            flops=10**8, bytes_accessed=15 * 10**7, transcendentals=3 * tok * NS * 1024
        ),
    )(sa, dx, wr, do, a2, h0, part, res, *src)


def gather(block):
    return lax.all_gather(block, "seq", axis=0, tiled=True)


def from_behind(block, axis, distance):
    devices = range(lax.axis_size(axis))
    route = [(i - distance, i) for i in devices if i - distance in devices]
    return lax.ppermute(block, axis, route)


def contract(left_op, right_op, pattern):
    return jnp.einsum(pattern, left_op, right_op, preferred_element_type=F32)


def silu_slope(values):
    sigma = jax.nn.sigmoid(values)
    return sigma * (1.0 + values * (1.0 - sigma))


def tiles(rows):
    return rows.reshape(rows.shape[0], rows.shape[1] // 128, 128)


def flat(rows):
    return rows.reshape(rows.shape[0], rows.shape[1] * rows.shape[2])


def local(
    tokens,
    cotangent,
    doc_start,
    premix_gain,
    inner_proj,
    switch_proj,
    conv_taps,
    conv_bias,
    select_proj,
    step_proj,
    step_bias,
    decay_log,
    skip_gain,
    mixer_out,
    preffn_gain,
    ffn_gate,
    ffn_up,
    ffn_down,
):
    tok_count, width = tokens.shape
    chan = inner_proj.shape[1]
    units = ffn_gate.shape[1]
    edge = KC - 1
    n_seq, n_wt = lax.axis_size("seq"), lax.axis_size("wt")
    z = lax.axis_index("wt")
    own = tok_count // n_wt
    cube = n_seq == 8 and n_wt == 4 and n_seq * tok_count <= width

    rows_sel, rows_step = select_proj.shape[0], step_proj.shape[0]
    goes_on = (1 - doc_start).astype(F32)
    before = jnp.concatenate([jnp.ones((edge,), F32), goes_on])
    after = jnp.concatenate([goes_on, jnp.ones((edge,), F32)])

    def same_back(lag):
        same = jnp.ones_like(goes_on)
        for j in range(lag):
            same = same * before[edge - j : edge - j + tok_count]
        return same[:, None]

    def same_ahead(lag):
        same = jnp.ones_like(goes_on)
        for j in range(1, lag + 1):
            same = same * after[j : j + tok_count]
        return same[:, None]

    one = jnp.ones((edge - 1,), F32)
    last_two, head = goes_on[-2:], goes_on[:edge]
    tail_keep = jnp.concatenate([last_two, one[:1]]) * jnp.concatenate([last_two[1:], one])
    head_keep = (
        head
        * jnp.concatenate([one[:1], head[:2]])
        * jnp.concatenate([one, head[:1]])
    )
    if cube:
        fill = jnp.zeros((-(rows_sel + rows_step) % 32, chan), BF16)
        (
            w_first, cot_f, first_f, w_small,
            inner_act, prev_rows, switch, conv_out, mixed_in, select,
        ) = first_gather(
            inner_proj, switch_proj,
            jnp.concatenate([step_proj, select_proj, fill], axis=0),
            cotangent, tokens, premix_gain, conv_taps, conv_bias,
            jnp.broadcast_to(goes_on[:, None], (tok_count, 128)), rows_sel, n_wt, n_seq, 7,
        )
        w_first = w_first.reshape(width, 2 * chan)
        w_mix = gather(mixer_out)
        prev_rows = prev_rows[8 - edge :]
    else:
        token_vals = tokens.astype(F32)
        first_inv = lax.rsqrt(jnp.mean(token_vals * token_vals, axis=-1, keepdims=True) + EPS)
        first_in = (token_vals * first_inv * premix_gain).astype(BF16)
        w_mixer = gather(jnp.concatenate([inner_proj, switch_proj, mixer_out], axis=1))
        w_first, w_mix = w_mixer[:, : 2 * chan], w_mixer[:, 2 * chan :]
        w_small = lax.all_gather(jnp.concatenate([step_proj, select_proj], axis=0), "seq", axis=0)
    w_all = gather(jnp.concatenate([ffn_gate, ffn_up, ffn_down], axis=1))
    w_step = w_small[:, :rows_step].reshape(-1, chan)
    w_select = w_small[:, rows_step : rows_step + rows_sel].reshape(-1, chan)
    if not cube:
        both = contract(first_in, w_first, "td,dc->tc")
        inner_act = both[:, :chan].astype(BF16)
        switch = both[:, chan:]
        prev_rows = from_behind(inner_act[-edge:] * tail_keep[:, None].astype(BF16), "seq", 1)
        extended = jnp.concatenate([prev_rows, inner_act], axis=0).astype(F32)
        conv_out = jnp.zeros((tok_count, chan), F32) + conv_bias[None, :]
        for offset in range(KC):
            conv_out = (
                conv_out
                + conv_taps[offset][None, :]
                * extended[edge - offset : edge - offset + tok_count]
                * same_back(offset)
            )
        mixed_in = jax.nn.silu(conv_out).astype(BF16)
        select = wt_sum(contract(w_select, mixed_in, "jc,tc->jt"), n_wt, 0)
    mixed_f = mixed_in.astype(F32)
    extended = jnp.concatenate([prev_rows.astype(F32), inner_act.astype(F32)], axis=0)
    low_rank = select[:R].astype(BF16)
    write_read = select[R:]
    step_pre = contract(low_rank, w_step, "rt,rc->tc") + step_bias[None, :]
    step_size = jax.nn.softplus(step_pre)
    decay = -jnp.exp(decay_log)
    decay2 = tiles(decay * LOG2E)
    step_a = tiles(jnp.where(doc_start[:, None] > 0, FAR, step_size))
    drive = tiles(step_size * mixed_f)
    scan_out, carried_in = fwd_scan(step_a, drive, write_read, decay2, n_seq, 1)

    scanned = flat(scan_out) + skip_gain[None, :] * mixed_f
    switch_act = jax.nn.silu(switch)
    gated = (scanned * switch_act).astype(BF16)
    mix_part = contract(gated, w_mix, "tc,dc->td").astype(BF16)
    second_in, residual = second_norm(mix_part, tokens, preffn_gain, n_wt, 2)
    if cube:
        line_up = lambda v: v.reshape(n_seq * tok_count, v.shape[-1])
        second_in, head_keep, extended, cot_t, first_t = lax.optimization_barrier(
            (second_in, head_keep, extended, line_up(cot_f).T, line_up(first_f).T)
        )
    acts, down_part, d_second, *second_all = ffn(
        second_in, cotangent, w_all, gated, cube, n_seq, 8
    )
    d_branch, d_residual, grad_preffn = second_back(
        d_second, residual, cotangent, preffn_gain, (), n_wt, n_seq, 3
    )
    d_gated = contract(d_branch, w_mix, "td,dc->tc")
    d_scanned = d_gated * switch_act
    d_switch = (d_gated * scanned * silu_slope(switch)).astype(BF16)
    grad_skip = jnp.sum(d_scanned * mixed_f, axis=0)
    along, through_sum, grad_decay, d_write_read, block_own, *branch_all = bwd_scan(
        step_a, drive, write_read, d_scanned, decay2, carried_in,
        down_part, residual, (d_branch,) if cube else (), n_wt, n_seq, 4,
    )
    d_step = along * mixed_f + through_sum * (1.0 / LOG2E)
    grad_decay_log = flat(grad_decay) * decay
    d_pre = d_step * jax.nn.sigmoid(step_pre)
    grad_step_bias = jnp.sum(d_pre, axis=0)
    d_pre_low = d_pre.astype(BF16)
    pad_rows = lambda v: jnp.pad(
        v.reshape(n_seq, -1, tok_count), ((0, 0), (0, -(v.shape[0] // n_seq) % 16), (0, 0))
    ).reshape(-1, tok_count)
    grad_step = contract(pad_rows(low_rank), d_pre_low, "rt,tc->rc").astype(BF16)
    d_select = wt_sum(
        jnp.concatenate(
            [
                contract(w_step, d_pre_low, "rc,tc->rt"),
                d_write_read.reshape(2, tok_count, NS).swapaxes(1, 2).reshape(2 * NS, tok_count),
            ],
            axis=0,
        ),
        n_wt,
        5,
    )
    d_select = d_select.astype(BF16)
    grad_select = contract(pad_rows(d_select), mixed_in, "jt,tc->jc").astype(BF16)
    d_mixed = (
        along * step_size
        + skip_gain[None, :] * d_scanned
        + contract(d_select, w_select, "jt,jc->tc")
    )
    d_conv = (d_mixed * silu_slope(conv_out)).astype(BF16)
    d_conv_f = d_conv.astype(F32)
    grad_conv_bias = jnp.sum(d_conv_f, axis=0)
    next_rows = from_behind(d_conv[:edge] * head_keep[:, None].astype(BF16), "seq", -1)
    ext_grad = jnp.concatenate([d_conv, next_rows], axis=0).astype(F32)
    d_inner = jnp.zeros_like(d_conv_f)
    taps_rows = []
    for offset in range(KC):
        taps_rows.append(
            jnp.sum(
                d_conv_f
                * extended[edge - offset : edge - offset + tok_count]
                * same_back(offset),
                axis=0,
            )
        )
        d_inner = (
            d_inner
            + conv_taps[offset][None, :]
            * ext_grad[offset : offset + tok_count]
            * same_ahead(offset)
        )
    d_inner_low = d_inner.astype(BF16)
    d_first = contract(
        jnp.concatenate([d_inner_low, d_switch], axis=1), w_first, "tc,dc->td"
    ).astype(BF16)
    more = ()
    if cube:
        more = (cot_t, line_up(second_all[0]).T, line_up(branch_all[0]).T, first_t, gather(acts))
    results = last(
        d_first, tokens, d_residual, premix_gain, grad_preffn,
        grad_select.reshape(n_seq, -1, chan), grad_step.reshape(n_seq, -1, chan), (rows_sel, rows_step),
        jnp.stack(taps_rows, axis=0), grad_decay_log,
        jnp.stack([grad_conv_bias, grad_step_bias, grad_skip]), block_own,
        (d_switch, d_inner_low) if cube else (), more, n_wt, n_seq, 6,
    )
    (
        tokens_grad, block_out, out_select, out_step, g_taps, g_decay, g_conv, g_step, g_skip,
        *others,
    ) = hand_out(results)
    if cube:
        out_down, out_gate, out_up, out_mix, out_switch, out_inner = others[2:]
    else:
        scatter = lambda v: lax.psum_scatter(v, "seq", scatter_dimension=0, tiled=True)
        by_unit = acts.reshape(tok_count, units // UNITS, -1)
        hidden, d_gate, d_up = [
            by_unit[:, :, i * UNITS : (i + 1) * UNITS].reshape(tok_count, units) for i in range(3)
        ]
        out_down = scatter(contract(cotangent, hidden, "td,tf->df"))
        out_gate = scatter(contract(second_in, d_gate, "td,tf->df"))
        out_up = scatter(contract(second_in, d_up, "td,tf->df"))
        out_mix = scatter(contract(d_branch, gated, "td,tc->dc"))
        out_switch = scatter(contract(first_in, d_switch, "td,tc->dc"))
        out_inner = scatter(contract(first_in, d_inner_low, "td,tc->dc"))
    return (
        block_out,
        tokens_grad,
        others[0][0],
        out_inner,
        out_switch,
        g_taps,
        g_conv[0],
        out_select,
        out_step,
        g_step[0],
        g_decay,
        g_skip[0],
        out_mix,
        others[1][0],
        out_gate,
        out_up,
        out_down,
    )


def solution(mesh):
    placed = (
        P("seq", None),
        P("seq", None),
        P("seq"),
        P(),
        P("seq", "wt"),
        P("seq", "wt"),
        P(None, "wt"),
        P("wt"),
        P("seq", "wt"),
        P("seq", "wt"),
        P("wt"),
        P(None, "wt"),
        P("wt"),
        P("seq", "wt"),
        P(),
        P("seq", "wt"),
        P("seq", "wt"),
        P("seq", "wt"),
    )
    return jax.shard_map(
        local,
        mesh=mesh,
        in_specs=placed,
        out_specs=(
            P("seq", None),
            P("seq", None),
            P(),
            P("seq", "wt"),
            P("seq", "wt"),
            P(None, "wt"),
            P("wt"),
            P("seq", "wt"),
            P("seq", "wt"),
            P("wt"),
            P(None, "wt"),
            P("wt"),
            P("seq", "wt"),
            P(),
            P("seq", "wt"),
            P("seq", "wt"),
            P("seq", "wt"),
        ),
        check_vma=False,
    )
```

```python
import functools

import jax
import jax.numpy as jnp
from jax import lax
from jax.experimental import pallas as pl
from jax.experimental.pallas import tpu as pltpu
from jax.sharding import PartitionSpec as P

NS = 16
R = 128
KC = 4
EPS = 1e-05
F32 = jnp.float32
BF16 = jnp.bfloat16
LOG2E = 1.4426950408889634
FAR = 1e30
MESH = pl.DeviceIdType.MESH
VMEM = pl.BlockSpec(memory_space=pltpu.VMEM)
SMEM = pl.BlockSpec(memory_space=pltpu.SMEM)
ANY = pl.BlockSpec(memory_space=pl.ANY)
VMEM_BYTES = 60 * 2**20


UNITS = 256


def nt(left_op, right_op):
    return lax.dot_general(
        left_op, right_op, (((1,), (1,)), ((), ())), preferred_element_type=F32
    )


def greet(axes):
    barrier = pltpu.get_barrier_semaphore()
    total = 0
    for axis in axes:
        n, me = lax.axis_size(axis), lax.axis_index(axis)
        for k in range(1, n):
            pl.semaphore_signal(
                barrier, inc=1, device_id={axis: lax.rem(me + k, n)}, device_id_type=MESH
            )
        total += n - 1
    pl.semaphore_wait(barrier, total)


def remote(src, dst, sems, slot, axis, peer):
    return pltpu.make_async_remote_copy(
        src_ref=src,
        dst_ref=dst,
        send_sem=sems.at[0, slot],
        recv_sem=sems.at[1, slot],
        device_id={axis: peer},
        device_id_type=MESH,
    )


def send(src, dst, sems, slot, axis, peer):
    copy = remote(src, dst, sems, slot, axis, peer)
    copy.start()
    return copy


def scatter_start(part, recv, sems, axis):
    n, me = lax.axis_size(axis), lax.axis_index(axis)
    rows = recv.shape[1]
    copies = []
    for k in range(1, n):
        peer = lax.rem(me + k, n)
        copies.append(
            send(part.at[pl.ds(peer * rows, rows)], recv.at[k - 1], sems, k - 1, axis, peer)
        )
    return copies


def gather_start(whole, rows, sems, axis):
    n, me = lax.axis_size(axis), lax.axis_index(axis)
    mine = whole.at[pl.ds(me * rows, rows)]
    return [send(mine, mine, sems, k - 1, axis, lax.rem(me + k, n)) for k in range(1, n)]


def arrived(copies):
    for copy in copies:
        copy.wait_recv()


def left(copies):
    for copy in copies:
        copy.wait_send()


def pair_sems(n):
    return pltpu.SemaphoreType.DMA((2, n - 1))


def summed(part, recv, at, step, row0):
    total = part[pl.ds(row0 + at, step)].astype(F32)
    for k in range(recv.shape[0]):
        total = total + recv[k, pl.ds(at, step)].astype(F32)
    return total


def step_rows(rows, step, body):
    def run(i, carry):
        body(pl.multiple_of(i * step, step))
        return carry

    lax.fori_loop(0, rows // step, run, 0)


def mates():
    z = lax.axis_index("wt")
    mate = z + 1 - 2 * lax.rem(z, 2)
    return z, mate, lax.rem(z + 2, 4), lax.rem(mate + 2, 4)


def line_scatter_start(part, recv, sems):
    if lax.axis_size("wt") != 4:
        return scatter_start(part, recv, sems, "wt")
    rows = recv.shape[1]
    _, mate, _, far_mate = mates()
    return [
        send(part.at[pl.ds(far_mate * rows, rows)], recv.at[0], sems, 0, "wt", mate),
        send(part.at[pl.ds(mate * rows, rows)], recv.at[1], sems, 1, "wt", mate),
    ]


def line_scatter_mid(part, recv, pend, sems, copies):
    if lax.axis_size("wt") != 4:
        return copies
    rows = recv.shape[1]
    _, _, far, _ = mates()
    copies[0].wait_recv()

    def body(at):
        mine = part[pl.ds(pl.multiple_of(far * rows + at, 16), 16)].astype(F32)
        pend[pl.ds(at, 16)] = (mine + recv[0, pl.ds(at, 16)].astype(F32)).astype(BF16)

    step_rows(rows, 16, body)
    return copies + [send(pend, recv.at[2], sems, 2, "wt", far)]


def line_scatter_end(copies):
    if lax.axis_size("wt") != 4:
        arrived(copies)
    else:
        arrived(copies[1:])


def line_summed(part, recv, at, step, row0):
    if lax.axis_size("wt") != 4:
        return summed(part, recv, at, step, row0)
    total = part[pl.ds(row0 + at, step)].astype(F32)
    return total + recv[1, pl.ds(at, step)].astype(F32) + recv[2, pl.ds(at, step)].astype(F32)


def line_gather_start(whole, rows, sems):
    if lax.axis_size("wt") != 4:
        return gather_start(whole, rows, sems, "wt")
    z, mate, far, _ = mates()
    mine = whole.at[pl.ds(z * rows, rows)]
    return [send(mine, mine, sems, 0, "wt", far), send(mine, mine, sems, 1, "wt", mate)]


def line_gather_mid(whole, rows, sems, copies):
    if lax.axis_size("wt") != 4:
        return copies
    _, mate, far, _ = mates()
    copies[0].wait_recv()
    piece = whole.at[pl.ds(far * rows, rows)]
    return copies + [send(piece, piece, sems, 2, "wt", mate)]


def line_gather_end(copies):
    if lax.axis_size("wt") != 4:
        arrived(copies)
    else:
        arrived(copies[1:])


def flips():
    seq = lax.axis_index("seq")
    core, x, y = lax.rem(seq, 2), lax.rem(seq // 2, 2), seq // 4

    def at(fy, fx, fc):
        return (
            (1 - y if fy else y) * 4 + (1 - x if fx else x) * 2 + (1 - core if fc else core)
        )

    return at


def cube_sems():
    return pltpu.SemaphoreType.DMA((2, 9))


def cube_first(block, whole, sems):
    at = flips()
    mine = whole.at[at(0, 0, 0)]
    return [
        send(block, mine, sems, 0, "seq", at(0, 1, 0)),
        send(block, mine, sems, 1, "seq", at(1, 0, 0)),
        send(block, mine, sems, 2, "seq", at(0, 0, 1)),
    ]


def keep(block, whole, sem):
    copy = pltpu.make_async_copy(block, whole.at[lax.axis_index("seq")], sem)
    copy.start()
    return copy


def spread_plan(src, dst, sems, own_sem):
    seq, n_seq = lax.axis_index("seq"), lax.axis_size("seq")
    piece = dst.shape[2]

    def columns(peer):
        return src.at[:, pl.ds(pl.multiple_of(peer * piece, piece), piece)]

    out = []
    for k in range(1, n_seq):
        peer = lax.rem(seq + k, n_seq)
        out.append(remote(columns(peer), dst.at[seq], sems, k - 1, "seq", peer))
    return out, pltpu.make_async_copy(columns(seq), dst.at[seq], own_sem)


def spread(src, dst, sems, own_sem):
    out, own = spread_plan(src, dst, sems, own_sem)
    for copy in out + [own]:
        copy.start()
    return out, own


def cube_second(whole, sems, first):
    at = flips()
    half = whole.shape[1] // 2
    first[0].wait_recv()
    block = whole.at[at(0, 1, 0)]
    top = block.at[pl.ds(0, half)]
    sent = [
        send(top, top, sems, 3, "seq", at(1, 0, 0)),
        send(block, block, sems, 5, "seq", at(0, 0, 1)),
    ]
    first[1].wait_recv()
    block = whole.at[at(1, 0, 0)]
    low = block.at[pl.ds(half, half)]
    sent += [
        send(low, low, sems, 4, "seq", at(0, 1, 0)),
        send(block, block, sems, 6, "seq", at(0, 0, 1)),
    ]
    return sent


def cube_third(whole, sems, second):
    at = flips()
    half = whole.shape[1] // 2
    block = whole.at[at(1, 1, 0)]
    sent = []
    for slot, came in ((0, second[0]), (1, second[2])):
        came.wait_recv()
        piece = block.at[pl.ds(slot * half, half)]
        sent.append(send(piece, piece, sems, 7 + slot, "seq", at(0, 0, 1)))
    return sent


def cube_end(first, second, third):
    first[2].wait_recv()
    second[1].wait_recv()
    second[3].wait_recv()
    arrived(third)
    for group in (first, second, third):
        left(group)


def share(src, dst, sems, own_sem):
    seq, n_seq, z = lax.axis_index("seq"), lax.axis_size("seq"), lax.axis_index("wt")
    own, piece = dst.shape[2:]
    rows = src.at[pl.ds(pl.multiple_of(z * own, own), own)]

    def columns(peer):
        return rows.at[:, pl.ds(pl.multiple_of(peer * piece, piece), piece)]

    sent = []
    for k in range(1, n_seq):
        peer = lax.rem(seq + k, n_seq)
        sent.append(send(columns(peer), dst.at[seq, z], sems, k - 1, "seq", peer))
    kept = pltpu.make_async_copy(columns(seq), dst.at[seq, z], own_sem)
    kept.start()
    return sent, kept


def pass_along(dst, sems):
    z, n_wt = lax.axis_index("wt"), lax.axis_size("wt")
    lines = dst.at[:, z]
    return [send(lines, lines, sems, k - 1, "wt", lax.rem(z + k, n_wt)) for k in range(1, n_wt)]


def pass_pairs(dst, sems):
    z, mate, far, _ = mates()
    lines = dst.at[:, z]
    return [send(lines, lines, sems, 0, "wt", far), send(lines, lines, sems, 1, "wt", mate)]


def pass_pairs_on(dst, sems, copies):
    _, mate, far, _ = mates()
    copies[0].wait_recv()
    lines = dst.at[:, far]
    return copies + [send(lines, lines, sems, 2, "wt", mate)]


def first_kernel(
    left_w, right_w, step_w, select_w, cot, tok, gain, taps, bias, goes,
    w_first, cot_f, act_f, w_small, inner, prev, switch, conv, mixed, select,
    first_in, w_near, ext, before, halo, part, recv,
    s_pair, s_small, s_own, s_cot, s_act, s_cz, s_az, s_halo, s_scatter, s_gather,
):
    seq, n_seq = lax.axis_index("seq"), lax.axis_size("seq")
    me = lax.axis_index("wt")
    count, width = tok.shape
    chan = inner.shape[1]
    half = left_w.shape[1]
    own_block = w_near.at[seq]
    placed = [
        pltpu.make_async_copy(left_w, own_block.at[:, pl.ds(0, half)], s_own.at[0]),
        pltpu.make_async_copy(right_w, own_block.at[:, pl.ds(half, half)], s_own.at[4]),
    ]
    for copy in placed:
        copy.start()
    lines = step_w.shape[0]
    w_small[seq, 2 * lines :] = jnp.zeros_like(w_small[seq, 2 * lines :])
    w_small[seq, :lines] = step_w[...]
    w_small[seq, lines : lines + select_w.shape[0]] = select_w[...]

    def norm(at):
        v = tok[pl.ds(at, 16)].astype(F32)
        inverse = lax.rsqrt(jnp.mean(v * v, axis=-1, keepdims=True) + EPS)
        first_in[pl.ds(at, 16)] = (v * inverse * gain[...]).astype(BF16)

    step_rows(count, 16, norm)
    greet(("seq", "wt"))
    little = cube_first(w_small.at[seq], w_small, s_small)
    sent1, kept1 = share(cot, cot_f, s_cot, s_own.at[2])
    sent2, kept2 = share(first_in, act_f, s_act, s_own.at[3])
    for copy in placed:
        copy.wait()
    pair1 = cube_first(own_block, w_near, s_pair)
    sent = sent1 + sent2
    arrived(sent)
    kept1.wait()
    kept2.wait()
    along = pass_along(cot_f, s_cz) + pass_along(act_f, s_az)
    little2 = cube_second(w_small, s_small, little)
    little3 = cube_third(w_small, s_small, little2)
    pair2 = cube_second(w_near, s_pair, pair1)
    pair3 = cube_third(w_near, s_pair, pair2)
    cube_end(little, little2, little3)
    cube_end(pair1, pair2, pair3)
    far = pltpu.make_async_copy(w_near, w_first, s_own.at[0])
    far.start()

    def project(target, first_tile):
        def one(j, carry):
            columns = pl.ds(pl.multiple_of(j * UNITS, UNITS), UNITS)
            source = pl.ds(pl.multiple_of((first_tile + j) * UNITS, UNITS), UNITS)
            tile = w_near[:, :, source].reshape(width, UNITS)
            out = jnp.dot(first_in[...], tile, preferred_element_type=F32)
            target[:, columns] = out.astype(target.dtype)
            return carry

        lax.fori_loop(0, chan // UNITS, one, 0)

    project(inner, 0)
    last_row, row_before = goes[count - 1 :], goes[count - 2 : count - 1]
    cut = jnp.concatenate(
        [jnp.ones((13, 1), F32), (last_row * row_before)[:, :1], last_row[:, :1], jnp.ones((1, 1), F32)]
    )
    halo[0] = (inner[count - 16 :].astype(F32) * cut).astype(BF16)
    before[:16] = jnp.ones((16, 128), F32)
    before[16:] = goes[...]
    ahead = remote(halo.at[0], halo.at[1], s_halo, 0, "seq", lax.rem(seq + 1, n_seq))

    @pl.when(seq + 1 < n_seq)
    def _():
        ahead.start()

    @pl.when(seq == 0)
    def _():
        halo[1] = jnp.zeros_like(halo[1])

    project(switch, chan // UNITS)
    ext[16:] = inner[...].astype(F32)

    @pl.when(seq > 0)
    def _():
        ahead.wait_recv()

    ext[:16] = halo[1].astype(F32)
    prev[...] = ext[8:16]

    def convolve(at):
        v = ext[pl.ds(pl.multiple_of(at + 8, 8), 24)]
        g = before[pl.ds(pl.multiple_of(at + 8, 8), 24)]
        same = None
        out = bias[...] + taps[0:1] * v[8:]
        for k in range(1, KC):
            step = g[9 - k : 25 - k]
            same = step if same is None else same * step
            out = out + taps[k : k + 1] * v[8 - k : 24 - k] * same[:, :1]
        conv[pl.ds(at, 16)] = out
        mixed[pl.ds(at, 16)] = (out * jax.nn.sigmoid(out)).astype(BF16)

    step_rows(count, 16, convolve)
    deep = w_small.shape[1]
    all_rows = nt(w_small[...].reshape(n_seq * deep, chan), mixed[...])
    rows = part.shape[0] // n_seq
    for j in range(n_seq):
        part[j * rows : (j + 1) * rows] = all_rows[j * deep + 16 : j * deep + 16 + rows]
    first = scatter_start(part, recv, s_scatter, "wt")
    rows = recv.shape[1]
    arrived(first)
    select[pl.ds(me * rows, rows)] = summed(part, recv, 0, rows, me * rows)
    second = gather_start(select, rows, s_gather, "wt")
    arrived(second)
    arrived(along)
    far.wait()

    @pl.when(seq + 1 < n_seq)
    def _():
        ahead.wait_send()

    for group in (along, sent, first, second):
        left(group)


def first_gather(left_w, right_w, step_w, select_w, cot, tok, gain, taps, bias, goes, rows_sel, n_wt, n_seq, ident):
    count, width = cot.shape
    rows, chan = left_w.shape
    pair_shape = (n_seq, rows, 2 * chan)
    lines = rows_sel * n_seq
    share_shape = jax.ShapeDtypeStruct((n_seq, n_wt, count // n_wt, width // n_seq), BF16)
    return pl.pallas_call(
        first_kernel,
        out_shape=[
            jax.ShapeDtypeStruct(pair_shape, BF16),
            share_shape,
            share_shape,
            jax.ShapeDtypeStruct((n_seq, 64, chan), BF16),
            jax.ShapeDtypeStruct((count, chan), BF16),
            jax.ShapeDtypeStruct((8, chan), F32),
            jax.ShapeDtypeStruct((count, chan), F32),
            jax.ShapeDtypeStruct((count, chan), F32),
            jax.ShapeDtypeStruct((count, chan), BF16),
            jax.ShapeDtypeStruct((lines, count), F32),
        ],
        in_specs=[ANY] * 2 + [VMEM] * 8,
        out_specs=[ANY] * 3 + [VMEM] * 7,
        scratch_shapes=[
            pltpu.VMEM((count, width), BF16),
            pltpu.VMEM(pair_shape, BF16),
            pltpu.VMEM((16 + count, chan), F32),
            pltpu.VMEM((16 + count, 128), F32),
            pltpu.VMEM((2, 16, chan), BF16),
            pltpu.VMEM((lines, count), F32),
            pltpu.VMEM((n_wt - 1, lines // n_wt, count), F32),
            cube_sems(),
            cube_sems(),
            pltpu.SemaphoreType.DMA((5,)),
            pair_sems(n_seq),
            pair_sems(n_seq),
            pair_sems(n_wt),
            pair_sems(n_wt),
            pltpu.SemaphoreType.DMA((2, 1)),
            pair_sems(n_wt),
            pair_sems(n_wt),
        ],
        compiler_params=pltpu.CompilerParams(
            collective_id=ident, has_side_effects=True, vmem_limit_bytes=VMEM_BYTES
        ),
        cost_estimate=pl.CostEstimate(flops=10**9, bytes_accessed=10**8, transcendentals=0),
    )(left_w, right_w, step_w, select_w, cot, tok, gain[None], taps, bias[None], goes)


def ffn_kernel(cube, x, c, wg, wu, wd, gated, acts, down, d_second, *refs):
    pieces, refs = refs[:cube], refs[cube:]
    acc_down, acc_second = refs[:2]
    step = pl.program_id(0)
    if cube:
        held, s_spread, s_own = refs[2:]
        sent, kept = spread_plan(held, pieces[0], s_spread, s_own)

        @pl.when(step == 0)
        def _():
            held[...] = x[...]
            greet(("seq",))
            for copy in sent + [kept]:
                copy.start()

    @pl.when(step == 0)
    def _():
        acc_down[...] = jnp.zeros_like(acc_down)
        acc_second[...] = jnp.zeros_like(acc_second)

    gate = jnp.dot(x[...], wg[...], preferred_element_type=F32)
    up = jnp.dot(x[...], wu[...], preferred_element_type=F32)
    d_hidden = jnp.dot(c[...], wd[...], preferred_element_type=F32)
    sigma = jax.nn.sigmoid(gate)
    act = gate * sigma
    hidden = (act * up).astype(BF16)
    d_gate = (d_hidden * up * (sigma * (1.0 + gate * (1.0 - sigma)))).astype(BF16)
    d_up = (d_hidden * act).astype(BF16)
    acts[:, :UNITS] = hidden
    acts[:, UNITS : 2 * UNITS] = d_gate
    acts[:, 2 * UNITS : 3 * UNITS] = d_up
    acts[:, 3 * UNITS :] = gated[...]
    acc_down[...] += nt(hidden, wd[...])
    acc_second[...] += nt(d_gate, wg[...]) + nt(d_up, wu[...])

    @pl.when(step == pl.num_programs(0) - 1)
    def _():
        down[...] = acc_down[...].astype(BF16)
        d_second[...] = acc_second[...].astype(BF16)
        if cube:
            kept.wait()
            arrived(sent)
            left(sent)


def ffn(x, c, w_all, gated, cube, n_seq, ident):
    tok, width = x.shape
    units, chan = w_all.shape[1] // 3, gated.shape[1]
    steps = units // UNITS
    span = 3 * UNITS + chan // steps
    whole = pl.BlockSpec((tok, width), lambda i: (0, 0))
    tile = lambda part: pl.BlockSpec((width, UNITS), lambda i: (0, part * steps + i))
    return pl.pallas_call(
        functools.partial(ffn_kernel, int(cube)),
        grid=(steps,),
        in_specs=[whole, whole, tile(0), tile(1), tile(2)]
        + [pl.BlockSpec((tok, chan // steps), lambda i: (0, i))],
        out_specs=[pl.BlockSpec((tok, span), lambda i: (0, i)), whole, whole] + [ANY] * cube,
        out_shape=[
            jax.ShapeDtypeStruct((tok, 3 * units + chan), BF16),
            jax.ShapeDtypeStruct((tok, width), BF16),
            jax.ShapeDtypeStruct((tok, width), BF16),
        ]
        + [jax.ShapeDtypeStruct((n_seq, tok, width // n_seq), BF16)] * cube,
        scratch_shapes=[pltpu.VMEM((tok, width), F32)] * 2
        + ([pltpu.VMEM((tok, width), BF16), pair_sems(n_seq), pltpu.SemaphoreType.DMA] if cube else []),
        compiler_params=pltpu.CompilerParams(
            vmem_limit_bytes=VMEM_BYTES,
            **(dict(collective_id=ident, has_side_effects=True) if cube else {}),
        ),
        cost_estimate=pl.CostEstimate(
            flops=12 * tok * width * units, bytes_accessed=6 * width * units, transcendentals=0
        ),
    )(x, c, w_all, w_all, w_all, gated)


def grads_kernel(lefts, *refs):
    n, m = max(lefts) + 1, len(lefts)
    for which, act, out in zip(lefts, refs[n : n + m], refs[n + m :]):
        out[...] = jnp.dot(refs[which][...], act[...], preferred_element_type=F32)


def grads(left_ops, lefts, acts):
    rows, tok = left_ops[0].shape
    cols = acts[0].shape[1]
    n = len(acts)
    return pl.pallas_call(
        functools.partial(grads_kernel, lefts),
        grid=(cols // UNITS,),
        in_specs=[pl.BlockSpec((rows, tok), lambda i: (0, 0))] * len(left_ops)
        + [pl.BlockSpec((tok, UNITS), lambda i: (0, i))] * n,
        out_specs=[pl.BlockSpec((rows, UNITS), lambda i: (0, i))] * n,
        out_shape=[jax.ShapeDtypeStruct((rows, cols), F32)] * n,
        compiler_params=pltpu.CompilerParams(vmem_limit_bytes=VMEM_BYTES),
        cost_estimate=pl.CostEstimate(
            flops=2 * n * tok * rows * cols, bytes_accessed=2 * n * tok * cols, transcendentals=0
        ),
    )(*left_ops, *acts)


def wt_sum_kernel(part, out, recv, s_scatter, s_gather):
    me = lax.axis_index("wt")
    rows = recv.shape[1]
    greet(("wt",))
    first = scatter_start(part, recv, s_scatter, "wt")
    arrived(first)
    out[pl.ds(me * rows, rows)] = summed(part, recv, 0, rows, me * rows)
    second = gather_start(out, rows, s_gather, "wt")
    arrived(second)
    left(first)
    left(second)


def wt_sum(part, n_wt, ident):
    rows, cols = part.shape
    return pl.pallas_call(
        wt_sum_kernel,
        out_shape=jax.ShapeDtypeStruct((rows, cols), F32),
        in_specs=[VMEM],
        out_specs=VMEM,
        scratch_shapes=[
            pltpu.VMEM((n_wt - 1, rows // n_wt, cols), F32),
            pair_sems(n_wt),
            pair_sems(n_wt),
        ],
        compiler_params=pltpu.CompilerParams(
            collective_id=ident, has_side_effects=True, vmem_limit_bytes=VMEM_BYTES
        ),
        cost_estimate=pl.CostEstimate(flops=10**5, bytes_accessed=10**6, transcendentals=0),
    )(part)


def second_norm_kernel(part, tok, gain, out, res, recv, pend, s_scatter, s_gather):
    me = lax.axis_index("wt")
    rows = recv.shape[1]
    greet(("wt",))
    first = line_scatter_start(part, recv, s_scatter)
    first = line_scatter_mid(part, recv, pend, s_scatter, first)
    line_scatter_end(first)
    row0 = me * rows

    def body(at):
        own = tok[pl.ds(pl.multiple_of(row0 + at, 16), 16)].astype(F32)
        r = own + line_summed(part, recv, at, 16, row0)
        res[pl.ds(at, 16)] = r
        inverse = lax.rsqrt(jnp.mean(r * r, axis=-1, keepdims=True) + EPS)
        out[pl.ds(pl.multiple_of(row0 + at, 16), 16)] = (r * inverse * gain[...]).astype(BF16)

    step_rows(rows, 16, body)
    second = line_gather_start(out, rows, s_gather)
    second = line_gather_mid(out, rows, s_gather, second)
    line_gather_end(second)
    left(first)
    left(second)


def second_norm(part, tok_own, gain, n_wt, ident):
    rows, cols = part.shape
    own = rows // n_wt
    return pl.pallas_call(
        second_norm_kernel,
        out_shape=[
            jax.ShapeDtypeStruct((rows, cols), BF16),
            jax.ShapeDtypeStruct((own, cols), F32),
        ],
        in_specs=[VMEM] * 3,
        out_specs=[VMEM] * 2,
        scratch_shapes=[
            pltpu.VMEM((n_wt - 1, own, cols), BF16),
            pltpu.VMEM((own, cols), BF16),
            pair_sems(n_wt),
            pair_sems(n_wt),
        ],
        compiler_params=pltpu.CompilerParams(
            collective_id=ident, has_side_effects=True, vmem_limit_bytes=VMEM_BYTES
        ),
        cost_estimate=pl.CostEstimate(flops=10**6, bytes_accessed=10**8, transcendentals=0),
    )(part, tok_own, gain[None])


def norm_back_rows(grad, vals, gain):
    inverse = lax.rsqrt(jnp.mean(vals * vals, axis=-1, keepdims=True) + EPS)
    normed = vals * inverse
    scaled = grad * gain
    mean = jnp.mean(scaled * normed, axis=-1, keepdims=True)
    return inverse * (scaled - normed * mean), grad * normed


def second_back_kernel(n_spread, part, res, cot, gain, *refs):
    srcs, refs = refs[:n_spread], refs[n_spread:]
    out, d_res, gain_grad = refs[:3]
    dsts, refs = refs[3 : 3 + n_spread], refs[3 + n_spread :]
    recv, pend, s_scatter, s_gather = refs[:4]
    me = lax.axis_index("wt")
    rows = recv.shape[1]
    greet(("wt", "seq") if n_spread else ("wt",))
    first = line_scatter_start(part, recv, s_scatter)
    spreads = [
        spread(srcs[i], dsts[i], refs[4 + 2 * i], refs[5 + 2 * i]) for i in range(n_spread)
    ]
    gain_grad[...] = jnp.zeros_like(gain_grad)
    first = line_scatter_mid(part, recv, pend, s_scatter, first)
    line_scatter_end(first)
    row0 = me * rows

    def body(at):
        grad = line_summed(part, recv, at, 16, row0)
        back, prod = norm_back_rows(grad, res[pl.ds(at, 16)], gain[...])
        gain_grad[...] += prod[:8] + prod[8:]
        d = cot[pl.ds(pl.multiple_of(row0 + at, 16), 16)].astype(F32) + back
        d_res[pl.ds(at, 16)] = d
        out[pl.ds(pl.multiple_of(row0 + at, 16), 16)] = d.astype(BF16)

    step_rows(rows, 16, body)
    second = line_gather_start(out, rows, s_gather)
    second = line_gather_mid(out, rows, s_gather, second)
    line_gather_end(second)
    for sent, kept in spreads:
        kept.wait()
        arrived(sent)
        left(sent)
    left(first)
    left(second)


def second_back(part, res, cot_own, gain, srcs, n_wt, n_seq, ident):
    rows, cols = part.shape
    own = rows // n_wt
    return pl.pallas_call(
        functools.partial(second_back_kernel, len(srcs)),
        out_shape=[
            jax.ShapeDtypeStruct((rows, cols), BF16),
            jax.ShapeDtypeStruct((own, cols), F32),
            jax.ShapeDtypeStruct((8, cols), F32),
        ]
        + [jax.ShapeDtypeStruct((n_seq, rows, cols // n_seq), BF16)] * len(srcs),
        in_specs=[VMEM] * (4 + len(srcs)),
        out_specs=[VMEM] * 3 + [ANY] * len(srcs),
        scratch_shapes=[
            pltpu.VMEM((n_wt - 1, own, cols), BF16),
            pltpu.VMEM((own, cols), BF16),
            pair_sems(n_wt),
            pair_sems(n_wt),
        ]
        + [pair_sems(n_seq), pltpu.SemaphoreType.DMA] * len(srcs),
        compiler_params=pltpu.CompilerParams(
            collective_id=ident, has_side_effects=True, vmem_limit_bytes=VMEM_BYTES
        ),
        cost_estimate=pl.CostEstimate(flops=10**6, bytes_accessed=10**8, transcendentals=0),
    )(part, res, cot_own, gain[None], *srcs)


def last_kernel(cube, part, tok, d_res, gain, gain_grad2, sel, stp, taps, decays, bias3, line, *refs):
    blocks, refs = refs[:cube], refs[cube:]
    if cube:
        cot_t, second_t, branch_t, first_t, acts = refs[:5]
        refs = refs[5:]
    out, block_out, sel_out, stp_out, taps_out, decays_out, *bias_outs = refs[:9]
    gain_outs, refs = refs[9:11], refs[11:]
    if cube:
        grad_outs, late_outs, refs = refs[:4], refs[4 : 4 + cube], refs[4 + cube :]
        tile, s_tile, wholes, refs = refs[0], refs[1], refs[2 : 2 + cube], refs[2 + cube :]
        width = tile.shape[2]
        tiles = acts.shape[1] // width

        def fetch(j, slot):
            columns = acts.at[:, pl.ds(pl.multiple_of(j * width, width), width)]
            return pltpu.make_async_copy(columns, tile.at[slot], s_tile.at[slot])

        def one_tile(j, carry):
            slot = lax.rem(j, 2)

            @pl.when(j + 1 < tiles)
            def _():
                fetch(j + 1, 1 - slot).start()

            fetch(j, slot).wait()
            at = 0
            for left_op, out_ref in zip((cot_t, second_t, second_t, branch_t), grad_outs):
                wide = out_ref.shape[1] // tiles
                out_ref[:, pl.ds(pl.multiple_of(j * wide, wide), wide)] = jnp.dot(
                    left_op[...], tile[slot, :, at : at + wide], preferred_element_type=F32
                )
                at += wide
            return carry

        fetch(0, 0).start()
    recv, pend, recv_sel, recv_stp, recv_chan, pack, chan_out, gain_buf, recv_gz, recv_gs = refs[:10]
    s_scatter, s_gather, s_sel, s_stp, s_chan, s_cg, s_gz, s_gs, s_block = refs[10:19]
    refs = refs[19:]
    me, n_wt = lax.axis_index("wt"), lax.axis_size("wt")
    seq, n_seq = lax.axis_index("seq"), lax.axis_size("seq")
    rows = recv.shape[1]
    block_out[pl.ds(pl.multiple_of(me * rows, 16), rows)] = line[...]
    greet(("wt", "seq"))
    first = line_scatter_start(part, recv, s_scatter)
    cubes = []
    for i in range(cube):
        s_cube, s_own = refs[2 * i : 2 * i + 2]
        cubes.append([cube_first(blocks[i], wholes[i], s_cube), s_cube, wholes[i]])
        cubes[-1].append(keep(blocks[i], wholes[i], s_own))
    share = -(-(KC + NS + 3) // n_seq)
    lines = [(taps, i) for i in range(KC)] + [(decays, i) for i in range(NS)]
    lines += [(bias3, i) for i in range(3)]
    for at, (ref, i) in enumerate(lines):
        pack[at // share, at % share : at % share + 1] = ref[i : i + 1]
    smalls = []
    for src, dst, sems in ((sel, recv_sel, s_sel), (stp, recv_stp, s_stp), (pack, recv_chan, s_chan)):
        for k in range(1, n_seq):
            peer = lax.rem(seq + k, n_seq)
            smalls.append(send(src.at[peer], dst.at[k - 1], sems, k - 1, "seq", peer))
    if cube:
        lax.fori_loop(0, 3, one_tile, 0)
    first = line_scatter_mid(part, recv, pend, s_scatter, first)
    if cube:
        lax.fori_loop(3, tiles - 2, one_tile, 0)
    line_scatter_end(first)
    row0 = me * rows
    gain_buf[...] = jnp.zeros_like(gain_buf)

    def body(at):
        grad = line_summed(part, recv, at, 16, row0)
        own = tok[pl.ds(pl.multiple_of(row0 + at, 16), 16)].astype(F32)
        back, prod = norm_back_rows(grad, own, gain[...])
        gain_buf[...] += prod[:8] + prod[8:]
        out[pl.ds(pl.multiple_of(row0 + at, 16), 16)] = (d_res[pl.ds(at, 16)] + back).astype(BF16)

    step_rows(rows, 16, body)
    second = line_gather_start(out, rows, s_gather)
    third = line_gather_start(block_out, rows, s_block)
    high = recv_gz.shape[1] // 2
    for i, grad in enumerate((gain_buf, gain_grad2)):
        line = jnp.sum(grad[...], axis=0, keepdims=True)
        for t in range(high):
            recv_gz[me, i * high + t : i * high + t + 1] = line[:, t * 128 : (t + 1) * 128]
    mine_z = recv_gz.at[me]
    zs = [send(mine_z, mine_z, s_gz, k - 1, "wt", lax.rem(me + k, n_wt)) for k in range(1, n_wt)]
    cubes2 = [cube_second(whole, sems, one) for one, sems, whole, _ in cubes]
    if cube:
        lax.fori_loop(tiles - 2, tiles, one_tile, 0)
    arrived(smalls)
    for src, recv_one, one_out in ((sel, recv_sel, sel_out), (stp, recv_stp, stp_out)):
        total = src[seq].astype(F32)
        for k in range(n_seq - 1):
            total = total + recv_one[k].astype(F32)
        one_out[...] = total[: one_out.shape[0]]
    total = pack[seq]
    for k in range(n_seq - 1):
        total = total + recv_chan[k]
    chan_out[seq] = total
    mine = chan_out.at[seq]
    chans = [
        send(mine, mine, s_cg, k - 1, "seq", lax.rem(seq + k, n_seq)) for k in range(1, n_seq)
    ]
    second = line_gather_mid(out, rows, s_gather, second)
    third = line_gather_mid(block_out, rows, s_block, third)
    arrived(zs)
    total = recv_gz[0]
    for pos in range(1, n_wt):
        total = total + recv_gz[pos]
    recv_gs[seq] = total
    mine_s = recv_gs.at[seq]
    ss = [
        send(mine_s, mine_s, s_gs, k - 1, "seq", lax.rem(seq + k, n_seq)) for k in range(1, n_seq)
    ]
    cubes3 = [cube_third(whole, sems, two) for (_, sems, whole, _), two in zip(cubes, cubes2)]
    arrived(ss)
    total = recv_gs[0]
    for pos in range(1, n_seq):
        total = total + recv_gs[pos]
    for i, gain_out in enumerate(gain_outs):
        for t in range(high):
            gain_out[:, t * 128 : (t + 1) * 128] = total[i * high + t : i * high + t + 1]
    arrived(chans)
    outs = [(taps_out, i) for i in range(KC)] + [(decays_out, i) for i in range(NS)]
    outs += [(bias_out, 0) for bias_out in bias_outs]
    for at, (ref, i) in enumerate(outs):
        ref[i : i + 1] = chan_out[at // share, at % share : at % share + 1]
    for k, ((one, _, whole, kept), two, three) in enumerate(zip(cubes, cubes2, cubes3)):
        cube_end(one, two, three)
        kept.wait()

        def late_tile(j, carry, whole=whole, late_out=late_outs[k]):
            columns = pl.ds(pl.multiple_of(j * UNITS, UNITS), UNITS)
            act = whole[:, :, columns].reshape(first_t.shape[1], UNITS)
            late_out[:, columns] = jnp.dot(first_t[...], act, preferred_element_type=F32)
            return carry

        lax.fori_loop(0, whole.shape[2] // UNITS, late_tile, 0)
    line_gather_end(second)
    line_gather_end(third)
    for group in (first, second, third, smalls, chans, zs, ss):
        left(group)


def last(
    part, tok_own, d_res, gain, gain_grad2, sel, stp, rows_small, taps, decays, bias3, line,
    blocks, more, n_wt, n_seq, ident,
):
    rows, cols = part.shape
    own = rows // n_wt
    chan = taps.shape[1]
    if more:
        deep, tok_all = more[0].shape
        units = (more[4].shape[1] - chan) // 3
        span = more[4].shape[1] // (units // UNITS)
    return pl.pallas_call(
        functools.partial(last_kernel, len(blocks)),
        out_shape=[
            jax.ShapeDtypeStruct((rows, cols), BF16),
            jax.ShapeDtypeStruct((rows, cols), BF16),
        ]
        + [
            jax.ShapeDtypeStruct((n, chan), F32)
            for n in rows_small + (taps.shape[0], decays.shape[0], 1, 1, 1)
        ]
        + [jax.ShapeDtypeStruct((1, cols), F32)] * 2
        + (
            [jax.ShapeDtypeStruct((deep, w), F32) for w in (units, units, units, chan)]
            + [jax.ShapeDtypeStruct((deep, a.shape[1]), F32) for a in blocks]
            if more
            else []
        ),
        in_specs=[VMEM] * 11 + [ANY] * len(blocks) + ([VMEM] * 4 + [ANY] if more else []),
        out_specs=[VMEM] * (11 + (4 + len(blocks) if more else 0)),
        scratch_shapes=(
            [pltpu.VMEM((2, tok_all, span), BF16), pltpu.SemaphoreType.DMA((2,))]
            + [pltpu.VMEM((n_seq,) + a.shape, BF16) for a in blocks]
            if more
            else []
        )
        + [
            pltpu.VMEM((n_wt - 1, own, cols), BF16),
            pltpu.VMEM((own, cols), BF16),
            pltpu.VMEM((n_seq - 1,) + sel.shape[1:], BF16),
            pltpu.VMEM((n_seq - 1,) + stp.shape[1:], BF16),
            pltpu.VMEM((n_seq - 1, 8, chan), F32),
            pltpu.VMEM((n_seq, 8, chan), F32),
            pltpu.VMEM((n_seq, 8, chan), F32),
            pltpu.VMEM((8, cols), F32),
            pltpu.VMEM((n_wt, 2 * cols // 128, 128), F32),
            pltpu.VMEM((n_seq, 2 * cols // 128, 128), F32),
            pair_sems(n_wt),
            pair_sems(n_wt),
            pair_sems(n_seq),
            pair_sems(n_seq),
            pair_sems(n_seq),
            pair_sems(n_seq),
            pair_sems(n_wt),
            pair_sems(n_seq),
            pair_sems(n_wt),
        ]
        + [cube_sems(), pltpu.SemaphoreType.DMA] * len(blocks),
        compiler_params=pltpu.CompilerParams(
            collective_id=ident, has_side_effects=True, vmem_limit_bytes=VMEM_BYTES
        ),
        cost_estimate=pl.CostEstimate(flops=10**6, bytes_accessed=10**8, transcendentals=0),
    )(part, tok_own, d_res, gain[None], gain_grad2, sel, stp, taps, decays, bias3, line, *blocks, *more)


def hand_out_kernel(n, *refs):
    srcs, dsts, held, sems = refs[:n], refs[n : 2 * n], refs[2 * n : 3 * n], refs[3 * n]
    into = [pltpu.make_async_copy(srcs[i], held[i], sems.at[0, i]) for i in range(n)]
    away = [pltpu.make_async_copy(held[i], dsts[i], sems.at[1, i]) for i in range(n)]
    for copy in into:
        copy.start()
    for first, second in zip(into, away):
        first.wait()
        second.start()
    for copy in away:
        copy.wait()


def hand_out(arrays):
    n = len(arrays)
    size = sum(a.size * a.dtype.itemsize for a in arrays)
    return pl.pallas_call(
        functools.partial(hand_out_kernel, n),
        out_shape=[jax.ShapeDtypeStruct(a.shape, a.dtype) for a in arrays],
        in_specs=[ANY] * n,
        out_specs=[ANY] * n,
        scratch_shapes=[pltpu.VMEM(a.shape, a.dtype) for a in arrays]
        + [pltpu.SemaphoreType.DMA((2, n))],
        compiler_params=pltpu.CompilerParams(vmem_limit_bytes=VMEM_BYTES),
        cost_estimate=pl.CostEstimate(flops=0, bytes_accessed=2 * size, transcendentals=0),
    )(*arrays)


def load(ref):
    return tuple(ref[n] for n in range(NS))


def store(ref, values):
    for n in range(NS):
        ref[n] = values[n]


def fold(mine, box, recv, a2, carried, backward):
    n, me = lax.axis_size("seq"), lax.axis_index("seq")
    carried[...] = jnp.zeros_like(carried)
    for k in range(n - 1, 0, -1):

        @pl.when((me + k < n) if backward else (me >= k))
        def _():
            giver = me + k if backward else me - k
            remote(mine, recv.at[k - 1], box, k - 1, "seq", giver).wait_recv()
            through = recv[k - 1, NS]
            for s in range(NS):
                carried[s] = (
                    jnp.exp2(a2[s] * through) * carried[s] + recv[k - 1, s]
                )


def hand_on(mine, recv, box, backward):
    n, me = lax.axis_size("seq"), lax.axis_index("seq")
    for k in range(1, n):

        @pl.when((me >= k) if backward else (me + k < n))
        def _():
            peer = me - k if backward else me + k
            send(mine, recv.at[k - 1], box, k - 1, "seq", peer)


def handed(mine, recv, box, backward):
    n, me = lax.axis_size("seq"), lax.axis_index("seq")
    for k in range(1, n):

        @pl.when((me >= k) if backward else (me + k < n))
        def _():
            peer = me - k if backward else me + k
            remote(mine, recv.at[k - 1], box, k - 1, "seq", peer).wait_send()


def fwd_kernel(sa, dx, wr, a2, y, h0, mine, recv, box):
    tok = sa.shape[0]
    greet(("seq",))

    def end(t, carry):
        s, d = sa[t], dx[t]
        h, total = carry
        return (
            tuple(jnp.exp2(s * a2[n]) * h[n] + wr[n, t] * d for n in range(NS)),
            total + s,
        )

    zero = jnp.zeros(sa.shape[1:], F32)
    ends, total = lax.fori_loop(0, tok, end, ((zero,) * NS, zero), unroll=4)
    store(mine, ends)
    mine[NS] = total
    hand_on(mine, recv, box, False)
    fold(mine, box, recv, a2, h0, False)

    def body(t, h):
        s, d = sa[t], dx[t]
        new, sums = [], [None] * 4
        for n in range(NS):
            hn = jnp.exp2(s * a2[n]) * h[n] + wr[n, t] * d
            new.append(hn)
            c = wr[NS + n, t] * hn
            sums[n % 4] = c if sums[n % 4] is None else sums[n % 4] + c
        y[t] = (sums[0] + sums[1]) + (sums[2] + sums[3])
        return tuple(new)

    lax.fori_loop(0, tok, body, load(h0), unroll=4)
    handed(mine, recv, box, False)


def fwd_scan(sa, dx, wr, a2, n_seq, ident):
    tok, high = sa.shape[:2]
    return pl.pallas_call(
        fwd_kernel,
        out_shape=[
            jax.ShapeDtypeStruct((tok, high, 128), F32),
            jax.ShapeDtypeStruct((NS, high, 128), F32),
        ],
        in_specs=[VMEM, VMEM, SMEM, VMEM],
        out_specs=[VMEM] * 2,
        scratch_shapes=[
            pltpu.VMEM((NS + 1, high, 128), F32),
            pltpu.VMEM((n_seq - 1, NS + 1, high, 128), F32),
            pair_sems(n_seq),
        ],
        compiler_params=pltpu.CompilerParams(
            collective_id=ident, has_side_effects=True, vmem_limit_bytes=VMEM_BYTES
        ),
        cost_estimate=pl.CostEstimate(
            flops=10**8, bytes_accessed=8 * 10**7, transcendentals=2 * tok * NS * 1024
        ),
    )(sa, dx, wr, a2)


def bwd_kernel(
    cube, sa, dx, wr, do_flat, a2, h0, part, res, *refs
):
    src, refs = refs[:cube], refs[cube:]
    along, ds2, grad_a, sums, out = refs[:5]
    dst, refs = refs[5 : 5 + cube], refs[5 + cube :]
    hs, qw, qr, pw, pr, g0, mine, recv, recv_z, pend, do, al2, d22, box, s_scatter = refs[:15]
    tok = sa.shape[0]
    chunk = qw.shape[0] // (NS * 8)
    high = sa.shape[1]
    for c in range(high):
        do[pl.ds(c, tok, stride=high), :] = do_flat[:, c * 128 : (c + 1) * 128]
    greet(("wt", "seq"))
    first = line_scatter_start(part, recv_z, s_scatter)

    def end(i, carry):
        t = tok - 1 - i
        s, d = sa[t], do[pl.ds(pl.multiple_of(t * high, high), high), :]
        g, total = carry
        return (
            tuple(jnp.exp2(s * a2[n]) * (g[n] + wr[NS + n, t] * d) for n in range(NS)),
            total + s,
        )

    zero = jnp.zeros(sa.shape[1:], F32)
    ends, total = lax.fori_loop(0, tok, end, ((zero,) * NS, zero), unroll=4)
    store(mine, ends)
    mine[NS] = total
    hand_on(mine, recv, box, True)
    if cube:
        s_seq, s_wt, s_own = refs[15:]
        sent, kept = share(src[0], dst[0], s_seq, s_own)
    first = line_scatter_mid(part, recv_z, pend, s_scatter, first)

    def again(t, h):
        s, d = sa[t], dx[t]
        new = []
        for n in range(NS):
            hs[t, n] = h[n]
            new.append(jnp.exp2(s * a2[n]) * h[n] + wr[n, t] * d)
        return tuple(new)

    lax.fori_loop(0, tok, again, load(h0), unroll=2)

    fold(mine, box, recv, a2, g0, True)
    if cube:
        arrived(sent)
        kept.wait()
        passed = pass_pairs(dst[0], s_wt)
    grad_a[...] = jnp.zeros_like(grad_a)

    def one_chunk(j, g):
        base = (tok // chunk - 1 - j) * chunk

        def body(i, g):
            at = chunk - 1 - i
            t = base + at
            s, d, o = sa[t], dx[t], do[pl.ds(pl.multiple_of(t * high, high), high), :]
            al = d2 = None
            new = []
            for n in range(NS):
                hp = hs[t, n]
                f = jnp.exp2(s * a2[n])
                hn = f * hp + wr[n, t] * d
                gn = wr[NS + n, t] * o + g[n]
                adj = f * gn
                new.append(adj)
                th = adj * hp
                grad_a[n] += th * s
                x = wr[n, t] * gn
                al = x if al is None else al + x
                x = a2[n] * th
                d2 = x if d2 is None else d2 + x
                row = pl.multiple_of((at * NS + n) * 8, 8)
                qw[pl.ds(row, 8), :] = gn * d
                qr[pl.ds(row, 8), :] = hn * o
            al2[pl.ds(pl.multiple_of(at * high, high), high), :] = al
            d22[pl.ds(pl.multiple_of(at * high, high), high), :] = d2
            return tuple(new)

        g = lax.fori_loop(0, chunk, body, g)

        def lanes(i, carry):
            for q, p in ((qw, pw), (qr, pr)):
                acc = q[pl.ds(i * NS * 8, NS, stride=8), :]
                for s in range(1, 8):
                    acc = acc + q[pl.ds(i * NS * 8 + s, NS, stride=8), :]
                p[pl.ds(pl.multiple_of(i * NS, NS), NS), :] = acc
            return carry

        lax.fori_loop(0, chunk, lanes, 0, unroll=4)
        lines = pl.ds(pl.multiple_of(base, chunk), chunk)
        for c in range(high):
            columns = slice(c * 128, (c + 1) * 128)
            along[lines, columns] = al2[pl.ds(c, chunk, stride=high), :]
            ds2[lines, columns] = d22[pl.ds(c, chunk, stride=high), :]
        ones = jnp.ones((8, 128), BF16)
        for which, p in enumerate((pw, pr)):
            upper = p[...].astype(BF16)
            lower = (p[...] - upper.astype(F32)).astype(BF16)
            row = which * (tok // chunk) + base // chunk
            sums[pl.ds(row, 1), :] = (nt(ones, upper) + nt(ones, lower))[:1]
        return g

    half = tok // chunk // 2
    g = lax.fori_loop(0, half, one_chunk, load(g0))
    if cube:
        passed = pass_pairs_on(dst[0], s_wt, passed)
    lax.fori_loop(half, tok // chunk, one_chunk, g)
    handed(mine, recv, box, True)
    line_scatter_end(first)
    rows = recv_z.shape[1]
    row0 = lax.axis_index("wt") * rows

    def block_rows(at):
        out[pl.ds(at, 16)] = (res[pl.ds(at, 16)] + line_summed(part, recv_z, at, 16, row0)).astype(BF16)

    step_rows(rows, 16, block_rows)
    left(first)
    if cube:
        arrived(passed[1:])
        left(sent)
        left(passed)


def bwd_scan(sa, dx, wr, do, a2, h0, part, res, src, n_wt, n_seq, ident):
    tok, high = sa.shape[:2]
    rows, cols = part.shape
    chunk = 32
    return pl.pallas_call(
        functools.partial(bwd_kernel, len(src)),
        out_shape=[
            jax.ShapeDtypeStruct((tok, high * 128), F32),
            jax.ShapeDtypeStruct((tok, high * 128), F32),
            jax.ShapeDtypeStruct((NS, high, 128), F32),
            jax.ShapeDtypeStruct((2 * tok // chunk, chunk * NS), F32),
            jax.ShapeDtypeStruct((rows // n_wt, cols), BF16),
        ]
        + [jax.ShapeDtypeStruct((n_seq, n_wt, rows // n_wt, cols // n_seq), BF16)] * len(src),
        in_specs=[VMEM, VMEM, SMEM] + [VMEM] * (5 + len(src)),
        out_specs=[VMEM] * 5 + [ANY] * len(src),
        scratch_shapes=[
            pltpu.VMEM((tok, NS, high, 128), F32),
            pltpu.VMEM((chunk * NS * 8, 128), F32),
            pltpu.VMEM((chunk * NS * 8, 128), F32),
            pltpu.VMEM((chunk * NS, 128), F32),
            pltpu.VMEM((chunk * NS, 128), F32),
            pltpu.VMEM((NS, high, 128), F32),
            pltpu.VMEM((NS + 1, high, 128), F32),
            pltpu.VMEM((n_seq - 1, NS + 1, high, 128), F32),
            pltpu.VMEM((n_wt - 1, rows // n_wt, cols), BF16),
            pltpu.VMEM((rows // n_wt, cols), BF16),
            pltpu.VMEM((tok * high, 128), F32),
            pltpu.VMEM((chunk * high, 128), F32),
            pltpu.VMEM((chunk * high, 128), F32),
            pair_sems(n_seq),
            pair_sems(n_wt),
        ]
        + [pair_sems(n_seq), pair_sems(n_wt), pltpu.SemaphoreType.DMA] * len(src),
        compiler_params=pltpu.CompilerParams(
            collective_id=ident, has_side_effects=True, vmem_limit_bytes=VMEM_BYTES
        ),
        cost_estimate=pl.CostEstimate(
            flops=10**8, bytes_accessed=15 * 10**7, transcendentals=3 * tok * NS * 1024
        ),
    )(sa, dx, wr, do, a2, h0, part, res, *src)


def gather(block):
    return lax.all_gather(block, "seq", axis=0, tiled=True)


def from_behind(block, axis, distance):
    devices = range(lax.axis_size(axis))
    route = [(i - distance, i) for i in devices if i - distance in devices]
    return lax.ppermute(block, axis, route)


def contract(left_op, right_op, pattern):
    return jnp.einsum(pattern, left_op, right_op, preferred_element_type=F32)


def silu_slope(values):
    sigma = jax.nn.sigmoid(values)
    return sigma * (1.0 + values * (1.0 - sigma))


def tiles(rows):
    return rows.reshape(rows.shape[0], rows.shape[1] // 128, 128)


def flat(rows):
    return rows.reshape(rows.shape[0], rows.shape[1] * rows.shape[2])


def local(
    tokens,
    cotangent,
    doc_start,
    premix_gain,
    inner_proj,
    switch_proj,
    conv_taps,
    conv_bias,
    select_proj,
    step_proj,
    step_bias,
    decay_log,
    skip_gain,
    mixer_out,
    preffn_gain,
    ffn_gate,
    ffn_up,
    ffn_down,
):
    tok_count, width = tokens.shape
    chan = inner_proj.shape[1]
    units = ffn_gate.shape[1]
    edge = KC - 1
    n_seq, n_wt = lax.axis_size("seq"), lax.axis_size("wt")
    z = lax.axis_index("wt")
    own = tok_count // n_wt
    cube = n_seq == 8 and n_wt == 4 and n_seq * tok_count <= width

    rows_sel, rows_step = select_proj.shape[0], step_proj.shape[0]
    goes_on = (1 - doc_start).astype(F32)
    before = jnp.concatenate([jnp.ones((edge,), F32), goes_on])
    after = jnp.concatenate([goes_on, jnp.ones((edge,), F32)])

    def same_back(lag):
        same = jnp.ones_like(goes_on)
        for j in range(lag):
            same = same * before[edge - j : edge - j + tok_count]
        return same[:, None]

    def same_ahead(lag):
        same = jnp.ones_like(goes_on)
        for j in range(1, lag + 1):
            same = same * after[j : j + tok_count]
        return same[:, None]

    one = jnp.ones((edge - 1,), F32)
    last_two, head = goes_on[-2:], goes_on[:edge]
    tail_keep = jnp.concatenate([last_two, one[:1]]) * jnp.concatenate([last_two[1:], one])
    head_keep = (
        head
        * jnp.concatenate([one[:1], head[:2]])
        * jnp.concatenate([one, head[:1]])
    )
    if cube:
        (
            w_first, cot_f, first_f, w_small,
            inner_act, prev_rows, switch, conv_out, mixed_in, select,
        ) = first_gather(
            inner_proj, switch_proj,
            step_proj, select_proj,
            cotangent, tokens, premix_gain, conv_taps, conv_bias,
            jnp.broadcast_to(goes_on[:, None], (tok_count, 128)), rows_sel, n_wt, n_seq, 7,
        )
        w_first = w_first.reshape(width, 2 * chan)
        w_mix = gather(mixer_out)
        prev_rows = prev_rows[8 - edge :]
    else:
        token_vals = tokens.astype(F32)
        first_inv = lax.rsqrt(jnp.mean(token_vals * token_vals, axis=-1, keepdims=True) + EPS)
        first_in = (token_vals * first_inv * premix_gain).astype(BF16)
        w_mixer = gather(jnp.concatenate([inner_proj, switch_proj, mixer_out], axis=1))
        w_first, w_mix = w_mixer[:, : 2 * chan], w_mixer[:, 2 * chan :]
        w_small = lax.all_gather(jnp.concatenate([step_proj, select_proj], axis=0), "seq", axis=0)
    w_all = gather(jnp.concatenate([ffn_gate, ffn_up, ffn_down], axis=1))
    w_step = w_small[:, :rows_step].reshape(-1, chan)
    w_select = w_small[:, rows_step : rows_step + rows_sel].reshape(-1, chan)
    if not cube:
        both = contract(first_in, w_first, "td,dc->tc")
        inner_act = both[:, :chan].astype(BF16)
        switch = both[:, chan:]
        prev_rows = from_behind(inner_act[-edge:] * tail_keep[:, None].astype(BF16), "seq", 1)
        extended = jnp.concatenate([prev_rows, inner_act], axis=0).astype(F32)
        conv_out = jnp.zeros((tok_count, chan), F32) + conv_bias[None, :]
        for offset in range(KC):
            conv_out = (
                conv_out
                + conv_taps[offset][None, :]
                * extended[edge - offset : edge - offset + tok_count]
                * same_back(offset)
            )
        mixed_in = jax.nn.silu(conv_out).astype(BF16)
        select = wt_sum(contract(w_select, mixed_in, "jc,tc->jt"), n_wt, 0)
    mixed_f = mixed_in.astype(F32)
    extended = jnp.concatenate([prev_rows.astype(F32), inner_act.astype(F32)], axis=0)
    low_rank = select[:R].astype(BF16)
    write_read = select[R:]
    step_pre = contract(low_rank, w_step, "rt,rc->tc") + step_bias[None, :]
    step_size = jax.nn.softplus(step_pre)
    decay = -jnp.exp(decay_log)
    decay2 = tiles(decay * LOG2E)
    step_a = tiles(jnp.where(doc_start[:, None] > 0, FAR, step_size))
    drive = tiles(step_size * mixed_f)
    scan_out, carried_in = fwd_scan(step_a, drive, write_read, decay2, n_seq, 1)

    scanned = flat(scan_out) + skip_gain[None, :] * mixed_f
    switch_act = jax.nn.silu(switch)
    gated = (scanned * switch_act).astype(BF16)
    mix_part = contract(gated, w_mix, "tc,dc->td").astype(BF16)
    second_in, residual = second_norm(mix_part, tokens, preffn_gain, n_wt, 2)
    if cube:
        line_up = lambda v: v.reshape(n_seq * tok_count, v.shape[-1])
        second_in, head_keep, extended, cot_t, first_t = lax.optimization_barrier(
            (second_in, head_keep, extended, line_up(cot_f).T, line_up(first_f).T)
        )
    acts, down_part, d_second, *second_all = ffn(
        second_in, cotangent, w_all, gated, cube, n_seq, 8
    )
    d_branch, d_residual, grad_preffn = second_back(
        d_second, residual, cotangent, preffn_gain, (), n_wt, n_seq, 3
    )
    d_gated = contract(d_branch, w_mix, "td,dc->tc")
    d_scanned = d_gated * switch_act
    d_switch = (d_gated * scanned * silu_slope(switch)).astype(BF16)
    grad_skip = jnp.sum(d_scanned * mixed_f, axis=0)
    along, through_sum, grad_decay, d_write_read, block_own, *branch_all = bwd_scan(
        step_a, drive, write_read, d_scanned, decay2, carried_in,
        down_part, residual, (d_branch,) if cube else (), n_wt, n_seq, 4,
    )
    d_step = along * mixed_f + through_sum * (1.0 / LOG2E)
    grad_decay_log = flat(grad_decay) * decay
    d_pre = d_step * jax.nn.sigmoid(step_pre)
    grad_step_bias = jnp.sum(d_pre, axis=0)
    d_pre_low = d_pre.astype(BF16)
    pad_rows = lambda v: jnp.pad(
        v.reshape(n_seq, -1, tok_count), ((0, 0), (0, -(v.shape[0] // n_seq) % 16), (0, 0))
    ).reshape(-1, tok_count)
    grad_step = contract(pad_rows(low_rank), d_pre_low, "rt,tc->rc").astype(BF16)
    d_select = wt_sum(
        jnp.concatenate(
            [
                contract(w_step, d_pre_low, "rc,tc->rt"),
                d_write_read.reshape(2, tok_count, NS).swapaxes(1, 2).reshape(2 * NS, tok_count),
            ],
            axis=0,
        ),
        n_wt,
        5,
    )
    d_select = d_select.astype(BF16)
    grad_select = contract(pad_rows(d_select), mixed_in, "jt,tc->jc").astype(BF16)
    d_mixed = (
        along * step_size
        + skip_gain[None, :] * d_scanned
        + contract(d_select, w_select, "jt,jc->tc")
    )
    d_conv = (d_mixed * silu_slope(conv_out)).astype(BF16)
    d_conv_f = d_conv.astype(F32)
    grad_conv_bias = jnp.sum(d_conv_f, axis=0)
    next_rows = from_behind(d_conv[:edge] * head_keep[:, None].astype(BF16), "seq", -1)
    ext_grad = jnp.concatenate([d_conv, next_rows], axis=0).astype(F32)
    d_inner = jnp.zeros_like(d_conv_f)
    taps_rows = []
    for offset in range(KC):
        taps_rows.append(
            jnp.sum(
                d_conv_f
                * extended[edge - offset : edge - offset + tok_count]
                * same_back(offset),
                axis=0,
            )
        )
        d_inner = (
            d_inner
            + conv_taps[offset][None, :]
            * ext_grad[offset : offset + tok_count]
            * same_ahead(offset)
        )
    d_inner_low = d_inner.astype(BF16)
    d_first = contract(
        jnp.concatenate([d_inner_low, d_switch], axis=1), w_first, "tc,dc->td"
    ).astype(BF16)
    more = ()
    if cube:
        more = (cot_t, line_up(second_all[0]).T, line_up(branch_all[0]).T, first_t, gather(acts))
    results = last(
        d_first, tokens, d_residual, premix_gain, grad_preffn,
        grad_select.reshape(n_seq, -1, chan), grad_step.reshape(n_seq, -1, chan), (rows_sel, rows_step),
        jnp.stack(taps_rows, axis=0), grad_decay_log,
        jnp.stack([grad_conv_bias, grad_step_bias, grad_skip]), block_own,
        (d_switch, d_inner_low) if cube else (), more, n_wt, n_seq, 6,
    )
    (
        tokens_grad, block_out, out_select, out_step, g_taps, g_decay, g_conv, g_step, g_skip,
        *others,
    ) = hand_out(results)
    if cube:
        out_down, out_gate, out_up, out_mix, out_switch, out_inner = others[2:]
    else:
        scatter = lambda v: lax.psum_scatter(v, "seq", scatter_dimension=0, tiled=True)
        by_unit = acts.reshape(tok_count, units // UNITS, -1)
        hidden, d_gate, d_up = [
            by_unit[:, :, i * UNITS : (i + 1) * UNITS].reshape(tok_count, units) for i in range(3)
        ]
        out_down = scatter(contract(cotangent, hidden, "td,tf->df"))
        out_gate = scatter(contract(second_in, d_gate, "td,tf->df"))
        out_up = scatter(contract(second_in, d_up, "td,tf->df"))
        out_mix = scatter(contract(d_branch, gated, "td,tc->dc"))
        out_switch = scatter(contract(first_in, d_switch, "td,tc->dc"))
        out_inner = scatter(contract(first_in, d_inner_low, "td,tc->dc"))
    return (
        block_out,
        tokens_grad,
        others[0][0],
        out_inner,
        out_switch,
        g_taps,
        g_conv[0],
        out_select,
        out_step,
        g_step[0],
        g_decay,
        g_skip[0],
        out_mix,
        others[1][0],
        out_gate,
        out_up,
        out_down,
    )


def solution(mesh):
    placed = (
        P("seq", None),
        P("seq", None),
        P("seq"),
        P(),
        P("seq", "wt"),
        P("seq", "wt"),
        P(None, "wt"),
        P("wt"),
        P("seq", "wt"),
        P("seq", "wt"),
        P("wt"),
        P(None, "wt"),
        P("wt"),
        P("seq", "wt"),
        P(),
        P("seq", "wt"),
        P("seq", "wt"),
        P("seq", "wt"),
    )
    return jax.shard_map(
        local,
        mesh=mesh,
        in_specs=placed,
        out_specs=(
            P("seq", None),
            P("seq", None),
            P(),
            P("seq", "wt"),
            P("seq", "wt"),
            P(None, "wt"),
            P("wt"),
            P("seq", "wt"),
            P("seq", "wt"),
            P("wt"),
            P(None, "wt"),
            P("wt"),
            P("seq", "wt"),
            P(),
            P("seq", "wt"),
            P("seq", "wt"),
            P("seq", "wt"),
        ),
        check_vma=False,
    )
```
